128 devices in a mesh: grp: 4 (over x_hi, core), fsdp: 32 (over y, z, x_lo).
Axes of the slice: x: 4 (x_hi: 2, x_lo: 2; x = x_hi * 2 + x_lo), y: 4, z: 4, core: 2. Of those that a mesh axis runs over, the one named last changes fastest.
Arguments:
- caption_states: bfloat16 [32, 128, 4096], P('fsdp'), may hold values from -6 to 6
- caption_lens: int32 [32], replicated, may hold values from 4 to 128
- text_gain: float32 [4096], replicated, may hold values from 0.25 to 1.75
- text_query: bfloat16 [4096, 2048], P(None, 'grp'), may hold values from -0.01171875 to 0.01171875
- text_key: bfloat16 [4096, 2048], P(None, 'grp'), may hold values from -0.09375 to 0.09375
- text_value: bfloat16 [4096, 2048], P(None, 'grp'), may hold values from -0.09375 to 0.09375
- text_bias: float32 [32, 128, 128], P('grp'), may hold values from -4 to 4
- text_out: bfloat16 [2048, 4096], P('grp'), may hold values from -0.125 to 0.125
- final_gain: float32 [4096], replicated, may hold values from 0.25 to 1.75
- cross_key: bfloat16 [4096, 1536], P('fsdp', 'grp'), may hold values from -0.09375 to 0.09375
- cross_value: bfloat16 [4096, 1536], P('fsdp', 'grp'), may hold values from -0.09375 to 0.09375
- video_states: bfloat16 [8192, 3072], P('fsdp'), may hold values from -6 to 6
- video_counts: int32 [32], replicated, may hold values from 128 to 1024, as said below
- sample_caption: int32 [32], replicated, may hold values from 0 to 31, each once
- cross_query: bfloat16 [3072, 1536], P('fsdp', 'grp'), may hold values from -0.109375 to 0.109375
- cross_out: bfloat16 [1536, 3072], P('grp', 'fsdp'), may hold values from -0.15625 to 0.15625
- out_grad: bfloat16 [8192, 3072], P('fsdp'), may hold values from -6 to 6
Outputs:
- updated: bfloat16 [8192, 3072], P('fsdp', 'grp')
- input_grad: bfloat16 [8192, 3072], P('fsdp', 'grp')
- query_grad: float32 [3072, 1536], P('fsdp', 'grp')
- out_weight_grad: float32 [1536, 3072], P('grp', 'fsdp')
- key_grad: bfloat16 [32, 128, 1536], P('fsdp', None, 'grp')
- value_grad: bfloat16 [32, 128, 1536], P('fsdp', None, 'grp')
The draws below stay inside these ranges and needn't reach their ends.
Inputs may be any that keep to these rules, and one draw needn't show every extreme that they name: `video_counts`: counts of the samples in order, summing to 8192. `sample_caption`: each caption belongs to exactly one sample.
All inputs are finite; a program needn't handle non-finite values.
Results may differ from the reference program's by a relative error of at most 0.04.
Values may be sent and summed in bfloat16 or wider, within the bound.
A program may use at most 128 MiB of HBM per device.

```python
import math
import jax
import jax.numpy as jnp
from jax import lax

TEXT_WIDTH = 4096
TEXT_HEADS = 32
TEXT_HEADDIM = 64
MODEL_WIDTH = 3072
CROSS_HEADS = 12
HEAD_SIZE = 128
CAPTION_LEN = 128
VIDEO_DEV = 256
CAPTIONS = 32
VIDEO_TOKENS = 8192
VIDEO_MOST = 1024
N_FSDP = 32


def draw_video_counts(key, part):
    key = jax.random.fold_in(key, 11)
    key_weights, key_order, key_place = jax.random.split(key, 3)
    half = VIDEO_DEV // 2
    others = CAPTIONS - 2
    extra = VIDEO_TOKENS - VIDEO_MOST - half - others * half
    weights = jax.random.randint(key_weights, (others,), 1, 5).astype(jnp.int32)
    total = jnp.sum(weights).astype(jnp.int32)
    share = (extra * weights // total).astype(jnp.int32)
    left = (extra - jnp.sum(share)).astype(jnp.int32)
    order = jax.random.permutation(key_order, others).astype(jnp.int32)
    share = share + (order < left).astype(jnp.int32)
    counts = jnp.concatenate([jnp.full((1,), VIDEO_MOST, jnp.int32), jnp.full((1,), half, jnp.int32), (half + share).astype(jnp.int32)])
    place = jax.random.permutation(key_place, CAPTIONS).astype(jnp.int32)
    return counts[place].astype(jnp.int32)


def touch_ends(values, key, low, largest):
    longest = values.shape.index(max(values.shape))
    spots = []
    for shift in (0, 1):
        where = [jax.random.randint(jax.random.fold_in(key, axis), (), 0, length) for axis, length in enumerate(values.shape)]
        where[longest] = (where[longest] + shift) % values.shape[longest]
        spots.append(tuple(where))
    return values.at[spots[0]].set(low).at[spots[1]].set(largest)


def block_scale(key, dims, shards, low, largest):
    loudness = 1.0
    for dim, shards_of in shards:
        draws = jax.random.uniform(jax.random.fold_in(jax.random.fold_in(key, 6), dim), (shards_of,), jnp.float32, low / len(shards), largest / len(shards))
        loudness = loudness * jnp.repeat(jnp.exp(draws), dims[dim] // shards_of).reshape((-1,) + (1,) * (len(dims) - 1 - dim))
    return loudness


def gaussian(rng, dims, scale, most, cuts=(), held_as=jnp.bfloat16):
    array = jax.random.normal(rng, dims, jnp.float32) * scale
    if len(cuts) > 0:
        array = block_scale(rng, dims, cuts, -0.22, 0.18) * array
    return jnp.clip(array, min=-most, max=most).astype(held_as)


def setup_inputs(seed: int = 0) -> dict:
    streams_of = jax.random.split(jax.random.key(seed), 18)
    return {
        "caption_states": gaussian(streams_of[0], (CAPTIONS, CAPTION_LEN, TEXT_WIDTH), 1.0, 6.0, ((0, 32),)),
        "caption_lens": touch_ends(jax.random.randint(streams_of[1], (CAPTIONS,), 4, CAPTION_LEN + 1), jax.random.fold_in(streams_of[1], 1), 4, CAPTION_LEN).astype(jnp.int32),
        "text_gain": jnp.clip(1.0 + 0.15 * jax.random.normal(streams_of[2], (TEXT_WIDTH,), jnp.float32), 0.25, 1.75),
        "text_query": gaussian(streams_of[3], (TEXT_WIDTH, TEXT_HEADS * TEXT_HEADDIM), (TEXT_WIDTH * TEXT_HEADDIM) ** -0.5, 0.01171875, ((1, 4),)),
        "text_key": gaussian(streams_of[4], (TEXT_WIDTH, TEXT_HEADS * TEXT_HEADDIM), TEXT_WIDTH ** -0.5, 0.09375, ((1, 4),)),
        "text_value": gaussian(streams_of[5], (TEXT_WIDTH, TEXT_HEADS * TEXT_HEADDIM), TEXT_WIDTH ** -0.5, 0.09375, ((1, 4),)),
        "text_bias": gaussian(streams_of[6], (TEXT_HEADS, CAPTION_LEN, CAPTION_LEN), 1.0, 4.0, ((0, 4),), jnp.float32),
        "text_out": gaussian(streams_of[7], (TEXT_HEADS * TEXT_HEADDIM, TEXT_WIDTH), (TEXT_HEADS * TEXT_HEADDIM) ** -0.5, 0.125, ((0, 4),)),
        "final_gain": jnp.clip(1.0 + 0.15 * jax.random.normal(streams_of[8], (TEXT_WIDTH,), jnp.float32), 0.25, 1.75),
        "cross_key": gaussian(streams_of[9], (TEXT_WIDTH, CROSS_HEADS * HEAD_SIZE), TEXT_WIDTH ** -0.5, 0.09375, ((0, 32), (1, 4))),
        "cross_value": gaussian(streams_of[10], (TEXT_WIDTH, CROSS_HEADS * HEAD_SIZE), TEXT_WIDTH ** -0.5, 0.09375, ((0, 32), (1, 4))),
        "video_states": gaussian(streams_of[11], (VIDEO_TOKENS, MODEL_WIDTH), 1.0, 6.0, ((0, 32),)),
        "video_counts": draw_video_counts(jax.random.fold_in(streams_of[17], 71), 0),
        "sample_caption": jax.random.permutation(streams_of[13], CAPTIONS).astype(jnp.int32),
        "cross_query": gaussian(streams_of[14], (MODEL_WIDTH, CROSS_HEADS * HEAD_SIZE), MODEL_WIDTH ** -0.5, 0.109375, ((0, 32), (1, 4))),
        "cross_out": gaussian(streams_of[15], (CROSS_HEADS * HEAD_SIZE, MODEL_WIDTH), (CROSS_HEADS * HEAD_SIZE) ** -0.5, 0.15625, ((0, 4), (1, 32))),
        "out_grad": gaussian(streams_of[16], (VIDEO_TOKENS, MODEL_WIDTH), 1.0, 6.0, ((0, 32),)),
    }


def rms_scale(values, gain):
    mean_square = lax.optimization_barrier(jnp.mean(values * values, axis=-1, keepdims=True))
    return values * lax.rsqrt(mean_square + 1e-06) * gain

def token_captions(video_counts, sample_caption, positions):
    sample_end = jnp.cumsum(video_counts).astype(jnp.int32)
    token_sample = lax.optimization_barrier(jnp.sum((sample_end[None, :] <= positions[:, None]).astype(jnp.int32), axis=1))
    numbers = jnp.arange(sample_caption.shape[0], dtype=jnp.int32)
    picked = token_sample[:, None] == numbers[None, :]
    return lax.optimization_barrier(jnp.sum(jnp.where(picked, sample_caption[None, :], 0), axis=1)).astype(jnp.int32)

def text_encoder(caption_states, caption_lens, text_gain, text_query, text_key, text_value, text_bias, text_out, final_gain):
    flat_states = caption_states.astype(jnp.float32).reshape(CAPTIONS * CAPTION_LEN, TEXT_WIDTH)
    normed = rms_scale(flat_states, text_gain).astype(jnp.bfloat16)

    def heads_of(weight):
        product = jnp.dot(normed, weight, preferred_element_type=jnp.float32).astype(jnp.bfloat16)
        return product.reshape(CAPTIONS, CAPTION_LEN, TEXT_HEADS, TEXT_HEADDIM)
    text_queries = heads_of(text_query)
    text_keys = heads_of(text_key)
    text_values = heads_of(text_value)
    text_scores = jnp.einsum('cihd,cjhd->chij', text_queries.astype(jnp.float32), text_keys.astype(jnp.float32)) + text_bias[None]
    key_valid = jnp.arange(CAPTION_LEN, dtype=jnp.int32)[None, :] < caption_lens[:, None]
    exp_scores = jnp.where(key_valid[:, None, None, :], jnp.exp(text_scores), 0.0)
    text_weights = (exp_scores / lax.optimization_barrier(jnp.sum(exp_scores, axis=-1, keepdims=True))).astype(jnp.bfloat16)
    text_mixed = jnp.einsum('chij,cjhd->cihd', text_weights.astype(jnp.float32), text_values.astype(jnp.float32))
    text_mixed = text_mixed.astype(jnp.bfloat16).reshape(CAPTIONS * CAPTION_LEN, TEXT_HEADS * TEXT_HEADDIM)
    text_sum = flat_states + jnp.dot(text_mixed, text_out, preferred_element_type=jnp.float32)
    return rms_scale(text_sum, final_gain).astype(jnp.bfloat16)

def reference(caption_states, caption_lens, text_gain, text_query, text_key, text_value, text_bias, text_out, final_gain, cross_key, cross_value, video_states, video_counts, sample_caption, cross_query, cross_out, out_grad):
    encoded = text_encoder(caption_states, caption_lens, text_gain, text_query, text_key, text_value, text_bias, text_out, final_gain)
    width = CROSS_HEADS * HEAD_SIZE
    keys_all = jnp.dot(encoded, cross_key, preferred_element_type=jnp.float32).astype(jnp.bfloat16).reshape(CAPTIONS, CAPTION_LEN, width)
    values_all = jnp.dot(encoded, cross_value, preferred_element_type=jnp.float32).astype(jnp.bfloat16).reshape(CAPTIONS, CAPTION_LEN, width)
    positions = jnp.arange(VIDEO_TOKENS, dtype=jnp.int32)
    token_cap = token_captions(video_counts, sample_caption, positions).reshape(N_FSDP, VIDEO_DEV)
    score_scale = 1.0 / math.sqrt(HEAD_SIZE)

    def column_step(carry, inputs):
        key_sum, value_sum, query_sum, outw_sum = carry
        video_col, grad_col, cap_col = inputs
        video = video_col.astype(jnp.float32)
        center = video - lax.optimization_barrier(jnp.mean(video, axis=-1, keepdims=True))
        inverse = lax.rsqrt(lax.optimization_barrier(jnp.mean(center * center, axis=-1, keepdims=True)) + 1e-06)
        video_hat = center * inverse
        video_normed = video_hat.astype(jnp.bfloat16)
        queries = jnp.dot(video_normed, cross_query, preferred_element_type=jnp.float32).astype(jnp.bfloat16)
        queries = queries.reshape(VIDEO_DEV, CROSS_HEADS, HEAD_SIZE)
        chosen_keys = jnp.take(keys_all, cap_col, axis=0).reshape(VIDEO_DEV, CAPTION_LEN, CROSS_HEADS, HEAD_SIZE)
        chosen_values = jnp.take(values_all, cap_col, axis=0).reshape(VIDEO_DEV, CAPTION_LEN, CROSS_HEADS, HEAD_SIZE)
        scores = jnp.einsum('thd,tjhd->thj', queries.astype(jnp.float32), chosen_keys.astype(jnp.float32)) * score_scale
        token_lens = jnp.take(caption_lens, cap_col, axis=0)
        key_valid = (jnp.arange(CAPTION_LEN, dtype=jnp.int32)[None, :] < token_lens[:, None])[:, None, :]
        exp_scores = jnp.where(key_valid, jnp.exp(scores), 0.0)
        weights = exp_scores / lax.optimization_barrier(jnp.sum(exp_scores, axis=-1, keepdims=True))
        probs = weights.astype(jnp.bfloat16)
        attended = jnp.einsum('thj,tjhd->thd', probs.astype(jnp.float32), chosen_values.astype(jnp.float32))
        attended = attended.astype(jnp.bfloat16).reshape(VIDEO_DEV, width)
        updated_col = (video + jnp.dot(attended, cross_out, preferred_element_type=jnp.float32)).astype(jnp.bfloat16)
        d_attended = jnp.dot(grad_col, cross_out.T, preferred_element_type=jnp.float32).astype(jnp.bfloat16)
        d_attended = d_attended.reshape(VIDEO_DEV, CROSS_HEADS, HEAD_SIZE)
        d_probs = jnp.einsum('thd,tjhd->thj', d_attended.astype(jnp.float32), chosen_values.astype(jnp.float32))
        d_scores = (weights * (d_probs - lax.optimization_barrier(jnp.sum(weights * d_probs, axis=-1, keepdims=True))) * score_scale).astype(jnp.bfloat16)
        d_queries = jnp.einsum('thj,tjhd->thd', d_scores.astype(jnp.float32), chosen_keys.astype(jnp.float32))
        d_queries = d_queries.astype(jnp.bfloat16).reshape(VIDEO_DEV, width)
        owners = (cap_col[None, :] == jnp.arange(CAPTIONS, dtype=jnp.int32)[:, None]).astype(jnp.float32)
        key_term = jnp.einsum('ct,thj,thd->cjhd', owners, d_scores.astype(jnp.float32), queries.astype(jnp.float32))
        value_term = jnp.einsum('ct,thj,thd->cjhd', owners, probs.astype(jnp.float32), d_attended.astype(jnp.float32))
        key_term = lax.optimization_barrier(key_term.reshape(CAPTIONS, CAPTION_LEN, width).astype(jnp.bfloat16))
        value_term = lax.optimization_barrier(value_term.reshape(CAPTIONS, CAPTION_LEN, width).astype(jnp.bfloat16))
        d_normed = jnp.dot(d_queries, cross_query.T, preferred_element_type=jnp.float32)
        first_mean = lax.optimization_barrier(jnp.mean(d_normed, axis=-1, keepdims=True))
        second_mean = lax.optimization_barrier(jnp.mean(d_normed * video_hat, axis=-1, keepdims=True))
        input_col = (grad_col.astype(jnp.float32) + inverse * (d_normed - first_mean - video_hat * second_mean)).astype(jnp.bfloat16)
        query_term = lax.optimization_barrier(jnp.dot(video_normed.T, d_queries, preferred_element_type=jnp.float32).astype(jnp.bfloat16))
        outw_term = lax.optimization_barrier(jnp.dot(attended.T, grad_col, preferred_element_type=jnp.float32).astype(jnp.bfloat16))
        carry = (key_sum + key_term.astype(jnp.float32), value_sum + value_term.astype(jnp.float32), query_sum + query_term.astype(jnp.float32), outw_sum + outw_term.astype(jnp.float32))
        return (carry, (updated_col, input_col))
    start_carry = (jnp.zeros((CAPTIONS, CAPTION_LEN, width), jnp.float32), jnp.zeros((CAPTIONS, CAPTION_LEN, width), jnp.float32), jnp.zeros((MODEL_WIDTH, width), jnp.float32), jnp.zeros((width, MODEL_WIDTH), jnp.float32))
    inputs = (video_states.reshape(N_FSDP, VIDEO_DEV, MODEL_WIDTH), out_grad.reshape(N_FSDP, VIDEO_DEV, MODEL_WIDTH), token_cap)
    final_carry, outputs = lax.scan(column_step, start_carry, inputs)
    key_sum, value_sum, query_grad, out_weight_grad = final_carry
    updated = outputs[0].reshape(VIDEO_TOKENS, MODEL_WIDTH)
    input_grad = outputs[1].reshape(VIDEO_TOKENS, MODEL_WIDTH)
    return (updated, input_grad, query_grad, out_weight_grad, key_sum.astype(jnp.bfloat16), value_sum.astype(jnp.bfloat16))
```

```python
import functools, math
import jax, jax.numpy as jnp
from jax import lax
from jax.experimental import pallas as pl
from jax.experimental.pallas import tpu as pltpu
from jax.sharding import PartitionSpec as P
MESH = pl.DeviceIdType.MESH

class Links:
    def __init__(self, sems):
        self.sems, self.keys, self.pending = sems, {}, []
    def sem(self, key):
        return self.sems.at[self.keys.setdefault(key, len(self.keys))]
    def copy(self, src, dst, key, dev):
        c = pltpu.make_async_remote_copy(src_ref=src, dst_ref=dst, send_sem=self.sem(("s", key)), recv_sem=self.sem(("r", key)), device_id=dev, device_id_type=MESH)
        return c
    def send(self, src, dst, key, dev):
        c = self.copy(src, dst, key, dev)
        c.start()
        self.pending.append(c)
    def recv(self, dst, key, dev):
        self.copy(dst, dst, key, dev).wait_recv()
    def drain(self):
        for c in self.pending:
            c.wait_send()
        self.pending = []

def place():
    g, f = lax.axis_index("grp"), lax.axis_index("fsdp")
    return dict(hi=g // 2, core=g % 2, y=f // 8, z=(f // 2) % 4, x=f % 2, g=g, f=f)

def dev(hi, core, y, z, x):
    return {"grp": hi * 2 + core, "fsdp": (y * 4 + z) * 2 + x}

class Gather:
    def __init__(self, L, me, name, G, rows):
        self.L, self.me, self.name, self.G, self.rows = L, me, name, G, rows
    def nb(self, part, first, d):
        m = self.me
        use_z = (m["x"] == 0) if (part == 0) == first else (m["x"] == 1)
        zi = jnp.where(use_z, (m["z"] + d) % 4, m["z"])
        yi = jnp.where(use_z, m["y"], (m["y"] + d) % 4)
        return {"fsdp": (yi * 4 + zi) * 2 + m["x"], "grp": m["g"]}
    def idx(self, part, d1, d2):
        m = self.me
        use_z = (m["x"] == 0) if part == 0 else (m["x"] == 1)
        dz = jnp.where(use_z, d1, d2)
        dy = jnp.where(use_z, d2, d1)
        px = m["x"] if part == 0 else 1 - m["x"]
        return (((m["y"] + dy) % 4) * 4 + (m["z"] + dz) % 4) * 2 + px
    def ref(self, part, d1, d2, half=None):
        b = self.G.at[self.idx(part, d1, d2)]
        if half is None:
            return b
        h = self.rows // 2
        return b.at[pl.ds(half * h, h)]
    def xsend(self, src):
        m = self.me
        self.L.send(src, self.G.at[m["f"]], (self.name, "x"), {"grp": m["g"], "fsdp": m["f"] + 1 - 2 * m["x"]})
    def xrecv(self):
        m = self.me
        self.L.recv(self.ref(1, 0, 0), (self.name, "x"), {"grp": m["g"], "fsdp": m["f"] + 1 - 2 * m["x"]})
    def s1(self, part, first, k, src=None):
        d = (0, 0) if first else (k, 0)
        r = self.ref(part, *d)
        src = r if src is None else src
        for s in (1, 3):
            self.L.send(src, r, (self.name, part, first, k, "s1", s), self.nb(part, first, s))
    def s2(self, part, first, k, s):
        o = 4 - s
        d = (o, 0) if first else (k, o)
        self.L.recv(self.ref(part, *d), (self.name, part, first, k, "s1", s), self.nb(part, first, o))
        half = 0 if s == 1 else 1
        r = self.ref(part, *d, half)
        self.L.send(r, r, (self.name, part, first, k, "s2", s), self.nb(part, first, s))
    def s3(self, part, first, k):
        d = (2, 0) if first else (k, 2)
        for s in (1, 3):
            half = 0 if s == 1 else 1
            self.L.recv(self.ref(part, *d, half), (self.name, part, first, k, "s2", s), self.nb(part, first, 4 - s))
    def run(self, own, xsrc):
        for st in self.stages(own, xsrc):
            st()
    def stages(self, own, xsrc):
        def a():
            self.xsend(xsrc); self.s1(0, True, 0, own)
        def b():
            self.xrecv(); self.s1(1, True, 0)
        def c():
            self.s2(0, True, 0, 1); self.s2(0, True, 0, 3)
            self.s1(0, False, 0, own)
            self.s2(1, True, 0, 1); self.s2(1, True, 0, 3)
            self.s1(1, False, 0)
        def d():
            for k in (1, 3):
                self.s1(0, False, k); self.s1(1, False, k)
        def e():
            self.s3(0, True, 0); self.s1(0, False, 2)
            self.s3(1, True, 0); self.s1(1, False, 2)
        def fw(k):
            def f():
                for part in (0, 1):
                    self.s2(part, False, k, 1); self.s2(part, False, k, 3)
            return f
        def fin(k):
            def f():
                for part in (0, 1):
                    self.s3(part, False, k)
            return f
        return [a, b, c, d, e, fw(0), fw(1), fin(0), fw(3), fin(1), fw(2), fin(3), fin(2)]

def barrier(me, devs):
    b = pltpu.get_barrier_semaphore()
    for d in devs:
        pl.semaphore_signal(b, inc=1, device_id=d, device_id_type=MESH)
    pl.semaphore_wait(b, len(devs))

def neighbours(me):
    m = me
    out = [{"grp": m["g"], "fsdp": m["f"] + 1 - 2 * m["x"]}]
    for d in (1, 3):
        out.append({"grp": m["g"], "fsdp": (m["y"] * 4 + (m["z"] + d) % 4) * 2 + m["x"]})
        out.append({"grp": m["g"], "fsdp": (((m["y"] + d) % 4) * 4 + m["z"]) * 2 + m["x"]})
    return out


class TwoStep:
    def __init__(self, L, me, name, parts, r1, s1, r2):
        self.L, self.me, self.name = L, me, name
        self.parts, self.r1, self.s1, self.r2 = parts, r1, s1, r2
        self.sib = {"grp": me["g"] + 1 - 2 * me["core"], "fsdp": me["f"]}
        self.opp = {"grp": (1 - me["hi"]) * 2 + me["core"], "fsdp": me["f"]}
    def start(self):
        other = 1 - self.me["core"]
        for j in range(2):
            h = 1 - self.me["hi"] if j == 0 else self.me["hi"]
            self.L.send(self.parts.at[2 * h + other], self.r1.at[j], (self.name, "c", j), self.sib)
    def mid(self):
        m = self.me
        self.L.recv(self.r1.at[0], (self.name, "c", 0), self.sib)
        self.s1[...] = (self.parts[2 * (1 - m["hi"]) + m["core"]].astype(jnp.float32) + self.r1[0].astype(jnp.float32)).astype(jnp.bfloat16)
        self.L.send(self.s1, self.r2, (self.name, "o"), self.opp)
    def end(self):
        m = self.me
        self.L.recv(self.r1.at[1], (self.name, "c", 1), self.sib)
        self.L.recv(self.r2, (self.name, "o"), self.opp)
        return self.parts[2 * m["hi"] + m["core"]].astype(jnp.float32) + self.r1[1].astype(jnp.float32) + self.r2[...].astype(jnp.float32)


def along_x(me, d):
    X = (me["hi"] * 2 + me["x"] + d) % 4
    return X // 2, X % 2


def same_core(me, d):
    hi, x = along_x(me, d)
    return dev(hi, me["core"], me["y"], me["z"], x)


class Eight:
    def __init__(self, L, me, name, E, rows):
        self.L, self.me, self.name, self.E, self.rows = L, me, name, E, rows
        self.sib = {"grp": me["g"] + 1 - 2 * me["core"], "fsdp": me["f"]}
    def ref(self, d, core, half=None):
        hi, x = along_x(self.me, d)
        r = self.E.at[x, hi * 2 + core]
        if half is None:
            return r
        h = self.rows // 2
        return r.at[pl.ds(half * h, h)]
    def start(self):
        r = self.ref(0, self.me["core"])
        for s in (1, 3):
            self.L.send(r, r, (self.name, "s1", s), same_core(self.me, s))
        self.L.send(r, r, (self.name, "sib", 0), self.sib)
    def mid(self):
        c = self.me["core"]
        for s in (1, 3):
            r = self.ref(4 - s, c)
            self.L.recv(r, (self.name, "s1", s), same_core(self.me, s))
            half = 0 if s == 1 else 1
            rh = self.ref(4 - s, c, half)
            self.L.send(rh, rh, (self.name, "s2", s), same_core(self.me, s))
            self.L.send(r, r, (self.name, "sib", 4 - s), self.sib)
    def mid2(self):
        c = self.me["core"]
        for s in (1, 3):
            half = 0 if s == 1 else 1
            rh = self.ref(2, c, half)
            self.L.recv(rh, (self.name, "s2", s), same_core(self.me, s))
            self.L.send(rh, rh, (self.name, "sib2", s), self.sib)
    def end(self):
        oc = 1 - self.me["core"]
        for d in (0, 1, 3):
            self.L.recv(self.ref(d, oc), (self.name, "sib", d), self.sib)
        for s in (1, 3):
            self.L.recv(self.ref(2, oc, 0 if s == 1 else 1), (self.name, "sib2", s), self.sib)


def eight_others(me):
    out = []
    for d in range(4):
        hi, x = along_x(me, d)
        for c in (0, 1):
            if d == 0 and c == 0:
                continue
            core = 1 - me["core"] if c == 1 else me["core"]
            out.append(((d, c), dev(hi, core, me["y"], me["z"], x), (x, hi * 2 + core)))
    return out


class Scatter:
    def __init__(self, L, me, name, D, ra, rb, rx):
        self.L, self.me, self.name, self.D, self.ra, self.rb, self.rx = L, me, name, D, ra, rb, rx
        self.rows = D.shape[1]
    def axis(self, part, stage):
        m = self.me
        own = m["x"] == 0 if part == 0 else m["x"] == 1
        return own if stage == 1 else jnp.logical_not(own)
    def nb(self, part, stage, d):
        m = self.me
        use_z = self.axis(part, stage)
        zi = jnp.where(use_z, (m["z"] + d) % 4, m["z"])
        yi = jnp.where(use_z, m["y"], (m["y"] + d) % 4)
        return {"fsdp": (yi * 4 + zi) * 2 + m["x"], "grp": m["g"]}
    def ref(self, part, stage, k, d, half=None):
        m = self.me
        use_z = self.axis(part, stage)
        dz = jnp.where(use_z, d, k)
        dy = jnp.where(use_z, k, d)
        px = m["x"] if part == 0 else 1 - m["x"]
        b = self.D.at[(((m["y"] + dy) % 4) * 4 + (m["z"] + dz) % 4) * 2 + px]
        if half is None:
            return b
        h = self.rows // 2
        return b.at[pl.ds(half * h, h)]
    def slot(self, stage, k):
        return k if stage == 0 else 4
    def far(self, part, stage, k):
        h = self.rows // 2
        for s in (1, 3):
            half = 0 if s == 1 else 1
            self.L.send(self.ref(part, stage, k, 2, half), self.ra.at[part, self.slot(stage, k), pl.ds(half * h, h)], (self.name, part, stage, k, "far", s), self.nb(part, stage, s))
    def near(self, part, stage, k):
        h = self.rows // 2
        for s in (1, 3):
            half = 0 if s == 1 else 1
            buf = self.ra.at[part, self.slot(stage, k), pl.ds(half * h, h)]
            self.L.recv(buf, (self.name, part, stage, k, "far", s), self.nb(part, stage, 4 - s))
            r = self.ref(part, stage, k, s, half)
            r[...] = (r[...].astype(jnp.float32) + buf[...].astype(jnp.float32)).astype(jnp.bfloat16)
            self.L.send(self.ref(part, stage, k, s), self.rb.at[part, self.slot(stage, k), half], (self.name, part, stage, k, "near", s), self.nb(part, stage, s))
    def total(self, part, stage, k):
        for s in (1, 3):
            half = 0 if s == 1 else 1
            self.L.recv(self.rb.at[part, self.slot(stage, k), half], (self.name, part, stage, k, "near", s), self.nb(part, stage, 4 - s))
        b = self.rb.at[part, self.slot(stage, k)]
        return self.ref(part, stage, k, 0)[...].astype(jnp.float32) + b[0].astype(jnp.float32) + b[1].astype(jnp.float32)
    def fold(self, part, stage, k):
        t = self.total(part, stage, k)
        self.ref(part, stage, k, 0)[...] = t.astype(jnp.bfloat16)
    def partner(self):
        m = self.me
        return {"grp": m["g"], "fsdp": m["f"] + 1 - 2 * m["x"]}
    def xsend(self):
        self.fold(1, 1, 0)
        self.L.send(self.ref(1, 1, 0, 0), self.rx, (self.name, "x"), self.partner())
    def result(self):
        t = self.total(0, 1, 0)
        self.L.recv(self.rx, (self.name, "x"), self.partner())
        return t + self.rx[...].astype(jnp.float32)
    def stages(self):
        def a():
            for k in (2, 1, 3, 0):
                for part in (1, 0):
                    self.far(part, 0, k)
        def b(k):
            def f():
                for part in (1, 0):
                    self.near(part, 0, k)
            return f
        def c(k):
            def f():
                for part in (1, 0):
                    self.fold(part, 0, k)
                    if k == 2:
                        self.far(part, 1, 0)
            return f
        def d():
            for part in (1, 0):
                self.near(part, 1, 0)
        return [a, b(2), b(1), c(2), b(3), c(1), b(0), c(3), d, c(0), self.xsend]


class Spread:
    def __init__(self, L, me, name, src, dst, send_sem, recv_sem):
        self.me, self.src, self.dst, self.ss, self.rs = me, src, dst, send_sem, recv_sem
    def copy(self, j):
        m = self.me
        to = (m["f"] + j) % 32
        return pltpu.make_async_remote_copy(src_ref=self.src(to), dst_ref=self.dst(m["f"]), send_sem=self.ss, recv_sem=self.rs, device_id={"grp": m["g"], "fsdp": to}, device_id_type=MESH)
    def start(self):
        @pl.loop(1, 32)
        def _(j):
            self.copy(j).start()


def wait_bytes(like, send_sem, recv_sem, devid, recv=True, send=True):
    c = pltpu.make_async_remote_copy(src_ref=like, dst_ref=like, send_sem=send_sem, recv_sem=recv_sem, device_id=devid, device_id_type=MESH)
    if recv:
        c.wait_recv()
    if send:
        c.wait_send()


def V():
    return pl.BlockSpec(memory_space=pltpu.VMEM)


def S():
    return pl.BlockSpec(memory_space=pltpu.SMEM)


def call(kernel, name, cid, n_in, outs, scratch, smem=()):
    return pl.pallas_call(
        kernel,
        out_shape=tuple(jax.ShapeDtypeStruct(s, d) for s, d in outs),
        in_specs=[S() if i in smem else V() for i in range(n_in)],
        out_specs=tuple(V() for _ in outs),
        scratch_shapes=scratch,
        compiler_params=pltpu.CompilerParams(collective_id=cid, has_side_effects=True, vmem_limit_bytes=60 << 20),
        name=name,
    )


BF, F32 = jnp.bfloat16, jnp.float32
DMA = pltpu.SemaphoreType.DMA


def k1(kv, qo, parts, cs, fgain, gw, gq, E, SS, r1, s1, r2, sems):
    me = place()
    L = Links(sems)
    others = eight_others(me)
    barrier(me, [d for _, d, _ in others] + neighbours(me)[1:])
    A, B = Gather(L, me, "w", gw, 128), Gather(L, me, "q", gq, 192)
    sa, sb = A.stages(kv.at[me["x"]], kv.at[1 - me["x"]]), B.stages(qo, qo)
    T = TwoStep(L, me, "t", parts, r1, s1, r2)
    X = Eight(L, me, "e", E, 128)
    T.start()
    sa[0]()
    gw[me["f"]] = kv[me["x"]]
    gq[me["f"]] = qo[...]
    sa[1]()
    T.mid()
    sa[2]()
    sa[3]()
    total = T.end()
    ts = total + cs[...].astype(F32)
    E[me["x"], me["g"]] = (ts * fgain[...]).astype(BF)
    ss = jnp.sum(ts * ts, axis=1, keepdims=True)
    SS[me["x"], me["g"]] = jnp.broadcast_to(ss, (128, 128)).T[:8]
    X.start()
    r = SS.at[me["x"], me["g"]]
    for key, d, _ in others:
        L.send(r, r, ("ss", (4 - key[0]) % 4, key[1]), d)
    sa[4]()
    X.mid()
    sa[5]()
    X.mid2()
    rest = []
    for i in range(8):
        if 6 + i < len(sa):
            sa[6 + i]()
        sb[i]()
    X.end()
    for key, d, slot in others:
        L.recv(SS.at[slot[0], slot[1]], ("ss", key[0], key[1]), d)
    for b in sb[8:]:
        b()
    L.drain()


def k2(kvp, cap, R, C, sb, s1, r1, s2, r2):
    me = place()
    partner = {"grp": me["g"], "fsdp": (me["f"] + 1) % 32}
    barrier(me, [{"grp": me["g"], "fsdp": (me["f"] + j) % 32} for j in range(1, 32)])
    yz = me["f"] // 2

    def p1(j):
        to = (yz + j) % 16
        return pltpu.make_async_remote_copy(src_ref=kvp.at[to], dst_ref=C.at[pl.ds(2 * yz, 2)], send_sem=s1, recv_sem=r1, device_id={"grp": me["g"], "fsdp": to * 2 + me["x"]}, device_id_type=MESH)

    @pl.loop(1, 16)
    def _(j):
        p1(j).start()
    C[pl.ds(2 * yz, 2)] = kvp[yz]
    wait_bytes(C.at[pl.ds(0, 30)], s1, r1, partner)

    def p2(j):
        to = (me["f"] + j) % 32
        return to, pltpu.make_async_remote_copy(src_ref=sb.at[to], dst_ref=R.at[me["f"]], send_sem=s2, recv_sem=r2, device_id={"grp": me["g"], "fsdp": to}, device_id_type=MESH)

    @pl.loop(1, 32)
    def _(j):
        to, c = p2(j)
        for s in range(3):
            sb[to, s] = C[cap[to * 3 + s]]
        c.start()
    for s in range(3):
        R[me["f"], s] = C[cap[me["f"] * 3 + s]]
    wait_bytes(R.at[pl.ds(0, 31)], s2, r2, partner)


def k3(d_in, op, dn, vhat, T, idx, G, out_sum, d_sum, stat, KV, D, ra, rb, rx, o1, o2, o3, n1, n2, n3, R, C, s1, r1, s2, r2, sems):
    me = place()
    L = Links(sems)
    partner = {"grp": me["g"], "fsdp": (me["f"] + 1) % 32}
    grp = [{"grp": (me["g"] + j) % 4, "fsdp": me["f"]} for j in range(1, 4)]
    barrier(me, [{"grp": me["g"], "fsdp": (me["f"] + j) % 32} for j in range(1, 32)] + grp)
    D[...] = d_in[...]
    sc = Scatter(L, me, "d", D, ra, rb, rx)
    stages = sc.stages()
    Tn = TwoStep(L, me, "n", dn, n1, n2, n3)
    To = TwoStep(L, me, "o", op, o1, o2, o3)

    @pl.loop(1, 32)
    def _(j):
        to = (me["f"] + j) % 32
        pltpu.make_async_remote_copy(src_ref=T.at[to], dst_ref=R.at[pl.ds(3 * me["f"], 3)], send_sem=s1, recv_sem=r1, device_id={"grp": me["g"], "fsdp": to}, device_id_type=MESH).start()
    stages[0]()
    Tn.start()
    To.start()
    R[pl.ds(96, 3)] = jnp.zeros((3, 8, 384), BF)
    R[pl.ds(3 * me["f"], 3)] = T[me["f"]]
    Tn.mid()
    To.mid()
    stages[1]()
    stages[2]()
    wait_bytes(R.at[pl.ds(0, 93)], s1, r1, partner)

    @pl.loop(0, 32)
    def _(c):
        acc = R[idx[c * 5]].astype(F32)
        for m in range(1, 5):
            acc = acc + R[idx[c * 5 + m]].astype(F32)
        C[c] = acc.astype(BF)

    @pl.loop(1, 32)
    def _(j):
        to = (me["f"] + j) % 32
        pltpu.make_async_remote_copy(src_ref=C.at[to], dst_ref=KV.at[me["f"]], send_sem=s2, recv_sem=r2, device_id={"grp": me["g"], "fsdp": to}, device_id_type=MESH).start()
    KV[me["f"]] = C[me["f"]]
    for s in stages[3:5]:
        s()
    t = Tn.end()
    d_sum[...] = t
    a = jnp.sum(t, axis=1, keepdims=True)
    b = jnp.sum(t * vhat[...], axis=1, keepdims=True)
    stat[me["g"], 0] = jnp.broadcast_to(a, (256, 128)).T[:8]
    stat[me["g"], 1] = jnp.broadcast_to(b, (256, 128)).T[:8]
    mine = stat.at[me["g"]]
    for j in range(1, 4):
        L.send(mine, mine, ("st", j), grp[j - 1])
    for s in stages[5:]:
        s()
    out_sum[...] = To.end()
    G[...] = sc.result()
    for j in range(1, 4):
        L.recv(stat.at[(me["g"] + 4 - j) % 4], ("st", j), grp[3 - j])
    wait_bytes(KV.at[pl.ds(0, 31)], s2, r2, partner)
    L.drain()


HEAD_SIZE = 128


def rms_scale(values, gain):
    mean_square = jnp.mean(values * values, axis=-1, keepdims=True)
    return values * lax.rsqrt(mean_square + 1e-06) * gain


def dot(a, b, ca, cb):
    return lax.dot_general(a, b, (((ca,), (cb,)), ((), ())), preferred_element_type=F32)


def tables(video_counts, sample_caption):
    numbers = jnp.arange(32, dtype=jnp.int32)
    end = jnp.sum(jnp.where(numbers[None, :] <= numbers[:, None], video_counts[None, :], 0), axis=1)
    first = jnp.sum((end[None, :] <= (256 * numbers)[:, None]).astype(jnp.int32), axis=1)
    slot = first[:, None] + jnp.arange(3, dtype=jnp.int32)
    clipped = jnp.minimum(slot, 31)
    cap = jnp.sum(jnp.where(clipped[:, :, None] == numbers, sample_caption, 0), axis=2)
    hit = sample_caption[None, :] == numbers[:, None]
    sample = jnp.sum(jnp.where(hit, numbers[None, :], 0), axis=1)
    stop = jnp.sum(jnp.where(hit, end[None, :], 0), axis=1)
    start = stop - jnp.sum(jnp.where(hit, video_counts[None, :], 0), axis=1)
    d = (start // 256)[:, None] + jnp.arange(5, dtype=jnp.int32)
    first_d = jnp.sum(jnp.where(jnp.minimum(d, 31)[:, :, None] == numbers, first, 0), axis=2)
    idx = jnp.where((d < 32) & (d * 256 < stop[:, None]), 3 * d + sample[:, None] - first_d, 96)
    return end, first, slot, cap, idx.reshape(160)


def local(caption_states, caption_lens, text_gain, text_query, text_key, text_value, text_bias, text_out, final_gain, cross_key, cross_value, video_states, video_counts, sample_caption, cross_query, cross_out, out_grad):
    f, g = lax.axis_index("fsdp"), lax.axis_index("grp")
    flat = caption_states.reshape(128, 4096).astype(F32)
    normed = rms_scale(flat, text_gain).astype(BF)
    heads = lambda w: jnp.dot(normed, w, preferred_element_type=F32).astype(BF).reshape(128, 8, 64)
    tq, tk, tv = heads(text_query), heads(text_key), heads(text_value)
    ts = jnp.einsum("ihd,jhd->hij", tq, tk, preferred_element_type=F32) + text_bias
    mylen = lax.dynamic_slice_in_dim(caption_lens, f, 1)[0]
    e = jnp.where(jnp.arange(128)[None, None, :] < mylen, jnp.exp(ts), 0.0)
    tw = (e / jnp.sum(e, axis=-1, keepdims=True)).astype(BF)
    tm = jnp.einsum("hij,jhd->ihd", tw, tv, preferred_element_type=F32).astype(BF).reshape(128, 512)
    parts = jnp.dot(tm, text_out, preferred_element_type=F32).astype(BF).reshape(128, 4, 1024).transpose(1, 0, 2)
    cs = lax.dynamic_slice_in_dim(caption_states[0], g * 1024, 1024, 1)
    fg = lax.dynamic_slice_in_dim(final_gain, g * 1024, 1024, 0)[None]
    kv = jnp.stack([cross_key, cross_value])
    qo = jnp.concatenate([cross_query, cross_out.T])
    gw, gq, E, SS = call(
        k1, "gather_text", 0, 5,
        [((32, 128, 384), BF), ((32, 192, 384), BF), ((2, 4, 128, 1024), BF), ((2, 4, 8, 128), F32)],
        [pltpu.VMEM((2, 128, 1024), BF), pltpu.VMEM((128, 1024), BF), pltpu.VMEM((128, 1024), BF), DMA((256,))],
    )(kv, qo, parts, cs, fg)
    rstd = lax.rsqrt(jnp.sum(SS[:, :, 0, :], axis=1) / 4096 + 1e-6).reshape(256, 1)
    X = E.transpose(0, 2, 1, 3).reshape(256, 4096)
    kvp = (jnp.dot(X, gw.reshape(4096, 384), preferred_element_type=F32) * rstd).astype(BF)
    kvp = kvp.reshape(2, 16, 8, 384).transpose(1, 0, 2, 3)
    end, first, slot, cap, idx = tables(video_counts, sample_caption)
    (R,) = call(
        k2, "spread_kv", 1, 2, [((32, 3, 8, 384), BF)],
        [pltpu.VMEM((32, 8, 384), BF), pltpu.VMEM((32, 3, 8, 384), BF), DMA, DMA, DMA, DMA],
        smem=(1,),
    )(kvp, cap.reshape(96))
    R = R.reshape(16, 2, 3, 8, 384).transpose(1, 2, 0, 3, 4).reshape(2, 3, 128, 384)
    ks, vs = R[0].reshape(3, 128, 3, 128), R[1].reshape(3, 128, 3, 128)
    positions = f * 256 + jnp.arange(256, dtype=jnp.int32)
    token_sample = jnp.sum((end[None, :] <= positions[:, None]).astype(jnp.int32), axis=1)
    my_slot = lax.dynamic_slice_in_dim(slot, f, 1)[0]
    my_cap = lax.dynamic_slice_in_dim(cap, f, 1)[0]
    lens = jnp.sum(jnp.where(my_cap[:, None] == jnp.arange(32), caption_lens[None, :], 0), axis=1)
    member = token_sample[None, :] == my_slot[:, None]
    token_lens = jnp.sum(jnp.where(member, lens[:, None], 0), axis=0)
    mh = member.astype(BF)
    video = video_states.astype(F32)
    center = video - jnp.mean(video, axis=-1, keepdims=True)
    inverse = lax.rsqrt(jnp.mean(center * center, axis=-1, keepdims=True) + 1e-06)
    vhat = center * inverse
    vn = vhat.astype(BF)
    Wq, WoT = gq[:, :96].reshape(3072, 384), gq[:, 96:].reshape(3072, 384)
    scale = 1.0 / math.sqrt(HEAD_SIZE)
    q = jnp.dot(vn, Wq, preferred_element_type=F32).astype(BF).reshape(256, 3, 128)
    pick = lambda a: jnp.where(member[0][:, None, None], a[0], jnp.where(member[1][:, None, None], a[1], a[2]))
    sc = pick(jnp.einsum("thd,kjhd->kthj", q, ks, preferred_element_type=F32)) * scale
    valid = (jnp.arange(128)[None, :] < token_lens[:, None])[:, None, :]
    ex = jnp.where(valid, jnp.exp(sc), 0.0)
    w = ex / jnp.sum(ex, axis=-1, keepdims=True)
    p = w.astype(BF)
    mp = mh[:, :, None, None] * p[None]
    att = jnp.einsum("kthj,kjhd->thd", mp, vs, preferred_element_type=F32).astype(BF).reshape(256, 384)
    op = dot(att, WoT, 1, 1).astype(BF).reshape(256, 4, 768).transpose(1, 0, 2)
    da = dot(out_grad, WoT, 1, 0).astype(BF).reshape(256, 3, 128)
    dp = pick(jnp.einsum("thd,kjhd->kthj", da, vs, preferred_element_type=F32))
    ds = (w * (dp - jnp.sum(w * dp, axis=-1, keepdims=True)) * scale).astype(BF)
    ms = mh[:, :, None, None] * ds[None]
    dq = jnp.einsum("kthj,kjhd->thd", ms, ks, preferred_element_type=F32).astype(BF).reshape(256, 384)
    kt = jnp.einsum("kthj,thd->kjhd", ms, q, preferred_element_type=F32).astype(BF).reshape(3, 16, 8, 384)
    vt = jnp.einsum("kthj,thd->kjhd", mp, da, preferred_element_type=F32).astype(BF).reshape(3, 16, 8, 384)
    T = jnp.stack([kt, vt]).transpose(2, 0, 1, 3, 4).reshape(32, 3, 8, 384)
    D = jnp.concatenate([dot(vn, dq, 0, 0).astype(BF).reshape(32, 96, 384), dot(out_grad, att, 0, 0).astype(BF).reshape(32, 96, 384)], axis=1)
    dn = dot(dq, Wq, 1, 1).astype(BF).reshape(256, 4, 768).transpose(1, 0, 2)
    cut = lambda a: lax.dynamic_slice_in_dim(a, g * 768, 768, 1)
    vh = cut(vhat)
    half = [pltpu.VMEM((2, 256, 768), BF), pltpu.VMEM((256, 768), BF), pltpu.VMEM((256, 768), BF)]
    G, out_sum, d_sum, stat, KV = call(
        k3, "reduce_grads", 2, 6,
        [((192, 384), F32), ((256, 768), F32), ((256, 768), F32), ((4, 2, 8, 256), F32), ((32, 8, 384), BF)],
        [pltpu.VMEM((32, 192, 384), BF), pltpu.VMEM((2, 5, 192, 384), BF), pltpu.VMEM((2, 5, 2, 192, 384), BF), pltpu.VMEM((192, 384), BF)]
        + half + half + [pltpu.VMEM((99, 8, 384), BF), pltpu.VMEM((32, 8, 384), BF), DMA, DMA, DMA, DMA, DMA((256,))],
        smem=(5,),
    )(D, op, dn, vh, T, idx)
    updated = (cut(video_states).astype(F32) + out_sum).astype(BF)
    mean = jnp.sum(stat[:, :, 0], axis=0) / 3072
    ig = (cut(out_grad).astype(F32) + inverse * (d_sum - mean[0][:, None] - vh * mean[1][:, None])).astype(BF)
    KV = KV.reshape(16, 2, 8, 384)
    return updated, ig, G[:96], G[96:].T, KV[:, 0].reshape(1, 128, 384), KV[:, 1].reshape(1, 128, 384)


def solution(mesh):
    in_specs = (P("fsdp"), P(), P(), P(None, "grp"), P(None, "grp"), P(None, "grp"), P("grp"), P("grp"), P(), P("fsdp", "grp"), P("fsdp", "grp"), P("fsdp"), P(), P(), P("fsdp", "grp"), P("grp", "fsdp"), P("fsdp"))
    out_specs = (P("fsdp", "grp"), P("fsdp", "grp"), P("fsdp", "grp"), P("grp", "fsdp"), P("fsdp", None, "grp"), P("fsdp", None, "grp"))
    return jax.shard_map(local, mesh=mesh, in_specs=in_specs, out_specs=out_specs, check_vma=False)
```

```python
import math

import jax
import jax.numpy as jnp
from jax import lax
from jax.experimental import pallas as pl
from jax.experimental.pallas import tpu as pltpu
from jax.sharding import PartitionSpec as P
MESH = pl.DeviceIdType.MESH
BF, F32 = jnp.bfloat16, jnp.float32
DMA = pltpu.SemaphoreType.DMA
HEAD_SIZE = 128

class Links:
    def __init__(self, sems):
        self.sems, self.keys, self.pending = sems, {}, []
    def sem(self, key):
        return self.sems.at[self.keys.setdefault(key, len(self.keys))]
    def copy(self, src, dst, key, dev, group=None):
        send = self.sem(("s", group if group else key))
        return pltpu.make_async_remote_copy(src_ref=src, dst_ref=dst, send_sem=send, recv_sem=self.sem(("r", key)), device_id=dev, device_id_type=MESH)
    def send(self, src, dst, key, dev, group=None):
        c = self.copy(src, dst, key, dev, group)
        c.start()
        if group is None:
            self.pending.append(c)
    def recv(self, dst, key, dev, group=None):
        self.copy(dst, dst, key, dev, group).wait_recv()
    def sent(self, blocks, group, key, dev):
        self.copy(blocks, blocks, key, dev, group).wait_send()
    def drain(self):
        for c in self.pending:
            c.wait_send()
        self.pending = []

def place():
    g, f = lax.axis_index("grp"), lax.axis_index("fsdp")
    return dict(hi=g // 2, core=g % 2, y=f // 8, z=(f // 2) % 4, x=f % 2, g=g, f=f)

def dev(hi, core, y, z, x):
    return {"grp": hi * 2 + core, "fsdp": (y * 4 + z) * 2 + x}

class Gather:
    def __init__(self, L, me, name, G, rows):
        self.L, self.me, self.name, self.G, self.rows = L, me, name, G, rows
    def nb(self, part, first, d):
        m = self.me
        use_z = (m["x"] == 0) if (part == 0) == first else (m["x"] == 1)
        zi = jnp.where(use_z, (m["z"] + d) % 4, m["z"])
        yi = jnp.where(use_z, m["y"], (m["y"] + d) % 4)
        return {"fsdp": (yi * 4 + zi) * 2 + m["x"], "grp": m["g"]}
    def idx(self, part, d1, d2):
        m = self.me
        use_z = (m["x"] == 0) if part == 0 else (m["x"] == 1)
        dz = jnp.where(use_z, d1, d2)
        dy = jnp.where(use_z, d2, d1)
        px = m["x"] if part == 0 else 1 - m["x"]
        return (((m["y"] + dy) % 4) * 4 + (m["z"] + dz) % 4) * 2 + px
    def ref(self, part, d1, d2, half=None):
        b = self.G.at[self.idx(part, d1, d2)]
        if half is None:
            return b
        h = self.rows // 2
        return b.at[pl.ds(half * h, h)]
    def xsend(self, src):
        m = self.me
        self.L.send(src, self.G.at[m["f"]], (self.name, "x"), {"grp": m["g"], "fsdp": m["f"] + 1 - 2 * m["x"]}, self.name)
    def xrecv(self):
        m = self.me
        self.L.recv(self.ref(1, 0, 0), (self.name, "x"), {"grp": m["g"], "fsdp": m["f"] + 1 - 2 * m["x"]}, self.name)
    def s1(self, part, first, k, src=None):
        d = (0, 0) if first else (k, 0)
        r = self.ref(part, *d)
        src = r if src is None else src
        for s in (1, 3):
            self.L.send(src, r, (self.name, part, first, k, "s1", s), self.nb(part, first, s), self.name)
    def s2(self, part, first, k, s):
        o = 4 - s
        d = (o, 0) if first else (k, o)
        self.L.recv(self.ref(part, *d), (self.name, part, first, k, "s1", s), self.nb(part, first, o), self.name)
        half = 0 if s == 1 else 1
        r = self.ref(part, *d, half)
        self.L.send(r, r, (self.name, part, first, k, "s2", s), self.nb(part, first, s), self.name)
    def s3(self, part, first, k):
        d = (2, 0) if first else (k, 2)
        for s in (1, 3):
            half = 0 if s == 1 else 1
            self.L.recv(self.ref(part, *d, half), (self.name, part, first, k, "s2", s), self.nb(part, first, 4 - s), self.name)
    def run(self, own, xsrc):
        for st in self.stages(own, xsrc):
            st()
    def stages(self, own, xsrc):
        def a():
            self.s1(0, True, 0, own)
        def b():
            self.xrecv(); self.s1(1, True, 0)
        def c():
            self.s2(0, True, 0, 1); self.s2(0, True, 0, 3)
            self.s1(0, False, 0, own)
            self.s2(1, True, 0, 1); self.s2(1, True, 0, 3)
            self.s1(1, False, 0)
        def d():
            for k in (1, 3):
                self.s1(0, False, k); self.s1(1, False, k)
        def e():
            self.s3(0, True, 0); self.s1(0, False, 2)
            self.s3(1, True, 0); self.s1(1, False, 2)
        def fw(k):
            def f():
                for part in (0, 1):
                    self.s2(part, False, k, 1); self.s2(part, False, k, 3)
            return f
        def fin(k):
            def f():
                for part in (0, 1):
                    self.s3(part, False, k)
            return f
        return [a, b, c, d, e, fw(0), fw(1), fin(0), fw(3), fin(1), fw(2), fin(3), fin(2)]
    def sent(self):
        m = self.me
        self.L.sent(self.G.at[pl.ds(0, 31)], self.name, (self.name, "x"), {"grp": m["g"], "fsdp": m["f"] + 1 - 2 * m["x"]})

def barrier(me, devs):
    b = pltpu.get_barrier_semaphore()
    for d in devs:
        pl.semaphore_signal(b, inc=1, device_id=d, device_id_type=MESH)
    pl.semaphore_wait(b, len(devs))

def neighbours(me):
    m = me
    out = [{"grp": m["g"], "fsdp": m["f"] + 1 - 2 * m["x"]}]
    for d in (1, 3):
        out.append({"grp": m["g"], "fsdp": (m["y"] * 4 + (m["z"] + d) % 4) * 2 + m["x"]})
        out.append({"grp": m["g"], "fsdp": (((m["y"] + d) % 4) * 4 + m["z"]) * 2 + m["x"]})
    return out


class TwoStep:
    def __init__(self, L, me, name, parts, r0, r1, s1, r2):
        self.L, self.me, self.name = L, me, name
        self.parts, self.r, self.s1, self.r2 = parts, (r0, r1), s1, r2
        self.sib = {"grp": me["g"] + 1 - 2 * me["core"], "fsdp": me["f"]}
        self.opp = {"grp": (1 - me["hi"]) * 2 + me["core"], "fsdp": me["f"]}
    def order(self):
        hi, core = self.me["hi"], self.me["core"]
        return [2 * (1 - hi) + 1 - core, 2 * hi + 1 - core, 2 * (1 - hi) + core, 2 * hi + core]
    def start(self, j):
        self.L.send(self.parts.at[self.order()[j]], self.r[j], (self.name, "c", j), self.sib)
    def mid(self):
        m = self.me
        self.L.recv(self.r[0], (self.name, "c", 0), self.sib)
        for i in range(self.s1.shape[0] // 32):
            rows = pl.ds(i * 32, 32)
            self.s1[rows] = (self.parts[2 * (1 - m["hi"]) + m["core"], rows].astype(F32) + self.r[0][rows].astype(F32)).astype(BF)
        self.L.send(self.s1, self.r2, (self.name, "o"), self.opp)
    def end(self):
        self.L.recv(self.r[1], (self.name, "c", 1), self.sib)
        self.L.recv(self.r2, (self.name, "o"), self.opp)
    def total(self, rows):
        m = self.me
        return self.parts[2 * m["hi"] + m["core"], rows].astype(F32) + self.r[1][rows].astype(F32) + self.r2[rows].astype(F32)


def along_x(me, d):
    X = (me["hi"] * 2 + me["x"] + d) % 4
    return X // 2, X % 2


def same_core(me, d):
    hi, x = along_x(me, d)
    return dev(hi, me["core"], me["y"], me["z"], x)


class Eight:
    def __init__(self, L, me, name, E, rows):
        self.L, self.me, self.name, self.E, self.rows = L, me, name, E, rows
        self.sib = {"grp": me["g"] + 1 - 2 * me["core"], "fsdp": me["f"]}
    def ref(self, d, core, half=None):
        hi, x = along_x(self.me, d)
        r = self.E.at[x, hi * 2 + core]
        if half is None:
            return r
        h = self.rows // 2
        return r.at[pl.ds(half * h, h)]
    def start(self):
        r = self.ref(0, self.me["core"])
        for s in (1, 3):
            self.L.send(r, r, (self.name, "s1", s), same_core(self.me, s))
        self.L.send(r, r, (self.name, "sib", 0), self.sib)
    def mid(self):
        c = self.me["core"]
        for s in (1, 3):
            r = self.ref(4 - s, c)
            self.L.recv(r, (self.name, "s1", s), same_core(self.me, s))
            half = 0 if s == 1 else 1
            rh = self.ref(4 - s, c, half)
            self.L.send(rh, rh, (self.name, "s2", s), same_core(self.me, s))
            self.L.send(r, r, (self.name, "sib", 4 - s), self.sib)
    def mid2(self):
        c = self.me["core"]
        for s in (1, 3):
            half = 0 if s == 1 else 1
            rh = self.ref(2, c, half)
            self.L.recv(rh, (self.name, "s2", s), same_core(self.me, s))
            self.L.send(rh, rh, (self.name, "sib2", s), self.sib)
    def end(self):
        oc = 1 - self.me["core"]
        for d in (0, 1, 3):
            self.L.recv(self.ref(d, oc), (self.name, "sib", d), self.sib)
        for s in (1, 3):
            self.L.recv(self.ref(2, oc, 0 if s == 1 else 1), (self.name, "sib2", s), self.sib)


def eight_others(me):
    out = []
    for d in range(4):
        hi, x = along_x(me, d)
        for c in (0, 1):
            if d == 0 and c == 0:
                continue
            core = 1 - me["core"] if c == 1 else me["core"]
            out.append(((d, c), dev(hi, core, me["y"], me["z"], x), (x, hi * 2 + core)))
    return out


class Scatter:
    def __init__(self, L, me, name, D, ra, rb, rx):
        self.L, self.me, self.name, self.D, self.ra, self.rb, self.rx = L, me, name, D, ra, rb, rx
        self.rows = D.shape[1]
    def axis(self, part, stage):
        m = self.me
        own = m["x"] == 0 if part == 0 else m["x"] == 1
        return own if stage == 1 else jnp.logical_not(own)
    def nb(self, part, stage, d):
        m = self.me
        use_z = self.axis(part, stage)
        zi = jnp.where(use_z, (m["z"] + d) % 4, m["z"])
        yi = jnp.where(use_z, m["y"], (m["y"] + d) % 4)
        return {"fsdp": (yi * 4 + zi) * 2 + m["x"], "grp": m["g"]}
    def ref(self, part, stage, k, d, half=None):
        m = self.me
        use_z = self.axis(part, stage)
        dz = jnp.where(use_z, d, k)
        dy = jnp.where(use_z, k, d)
        px = m["x"] if part == 0 else 1 - m["x"]
        b = self.D.at[(((m["y"] + dy) % 4) * 4 + (m["z"] + dz) % 4) * 2 + px]
        if half is None:
            return b
        h = self.rows // 2
        return b.at[pl.ds(half * h, h)]
    def slot(self, stage, k):
        return k if stage == 0 else 4
    def far(self, part, stage, k):
        h = self.rows // 2
        for s in (1, 3):
            half = 0 if s == 1 else 1
            self.L.send(self.ref(part, stage, k, 2, half), self.ra.at[part, self.slot(stage, k), half], (self.name, part, stage, k, "far", s), self.nb(part, stage, s), self.name)
    def near(self, part, stage, k):
        h = self.rows // 2
        for s in (1, 3):
            half = 0 if s == 1 else 1
            buf = self.ra.at[part, self.slot(stage, k), half]
            self.L.recv(buf, (self.name, part, stage, k, "far", s), self.nb(part, stage, 4 - s), self.name)
            r = self.ref(part, stage, k, s, half)
            r[...] = (r[...].astype(F32) + buf[...].astype(F32)).astype(BF)
            self.L.send(self.ref(part, stage, k, s), self.rb.at[part, self.slot(stage, k), half], (self.name, part, stage, k, "near", s), self.nb(part, stage, s), self.name)
    def total(self, part, stage, k):
        for s in (1, 3):
            half = 0 if s == 1 else 1
            self.L.recv(self.rb.at[part, self.slot(stage, k), half], (self.name, part, stage, k, "near", s), self.nb(part, stage, 4 - s), self.name)
        b = self.rb.at[part, self.slot(stage, k)]
        return self.ref(part, stage, k, 0)[...].astype(F32) + b[0].astype(F32) + b[1].astype(F32)
    def fold(self, part, stage, k):
        t = self.total(part, stage, k)
        self.ref(part, stage, k, 0)[...] = t.astype(BF)
    def partner(self):
        m = self.me
        return {"grp": m["g"], "fsdp": m["f"] + 1 - 2 * m["x"]}
    def xsend(self):
        self.fold(1, 1, 0)
        self.L.send(self.ref(1, 1, 0, 0), self.rx, (self.name, "x"), self.partner(), self.name)
    def result(self):
        t = self.total(0, 1, 0)
        self.L.recv(self.rx, (self.name, "x"), self.partner(), self.name)
        return t + self.rx[...].astype(F32)
    def stages(self):
        def a():
            for k in (2, 1, 3, 0):
                for part in (1, 0):
                    self.far(part, 0, k)
        def b(k):
            def f():
                for part in (1, 0):
                    self.near(part, 0, k)
            return f
        def c(k):
            def f():
                for part in (1, 0):
                    self.fold(part, 0, k)
                    if k == 2:
                        self.far(part, 1, 0)
            return f
        def d():
            for part in (1, 0):
                self.near(part, 1, 0)
        return [a, b(2), b(1), c(2), b(3), c(1), b(0), c(3), d, c(0), self.xsend]
    def sent(self):
        self.L.sent(self.D.at[pl.ds(0, 31)], self.name, (self.name, "x"), self.partner())


def wait_bytes(like, send_sem, recv_sem, devid, recv=True, send=True):
    c = pltpu.make_async_remote_copy(src_ref=like, dst_ref=like, send_sem=send_sem, recv_sem=recv_sem, device_id=devid, device_id_type=MESH)
    if recv:
        c.wait_recv()
    if send:
        c.wait_send()


def dot(a, b, ca, cb):
    return lax.dot_general(a, b, (((ca,), (cb,)), ((), ())), preferred_element_type=F32)


class Refs:
    pass


P_IN = ["lens", "counts", "scap", "kv", "qo", "tgain", "fgain", "cs_h", "tq_h", "tk_h", "tv_h", "bias_h", "tout_h", "vid_h", "grad_h"]
P_OUT = {
    "qb": ((256, 384), BF),
    "da": ((256, 384), BF),
    "ks": ((2, 384, 384), BF),
    "gq": ((32, 192, 384), BF),
    "vnT": ((3072, 256), BF),
    "gradT": ((3072, 256), BF),
    "mu": ((256, 1), F32),
    "inv": ((256, 1), F32),
}
P_SCRATCH = {
    "cs": ((128, 4096), BF),
    "normed": ((128, 4096), BF),
    "wt": ((2, 4096, 512), BF),
    "bias": ((8, 128, 128), F32),
    "tqkv": ((3, 128, 512), BF),
    "tm": ((128, 512), BF),
    "vid": ((256, 3072), BF),
    "grad": ((256, 3072), BF),
    "vn": ((256, 3072), BF),
    "gw": ((32, 128, 384), BF),
    "parts": ((4, 128, 1024), BF),
    "t0": ((128, 1024), BF),
    "t1": ((128, 1024), BF),
    "t2": ((128, 1024), BF),
    "t3": ((128, 1024), BF),
    "E": ((2, 4, 128, 1024), BF),
    "sscol": ((128, 1), F32),
    "SS": ((2, 4, 8, 128), F32),
    "kvp": ((16, 2, 8, 384), BF),
    "C": ((32, 8, 384), BF),
    "sb": ((32, 3, 8, 384), BF),
    "R": ((32, 3, 8, 384), BF),
}
P_TABLES = {"end": 32, "first": 32, "cap": 96, "samp": 32}
Q_IN = ["edge", "sidx", "qb", "da", "ks", "mu", "inv", "gq_h", "vnT_h", "gradT_h", "vid_h", "grad_h"]
Q_OUT = {
    "updated": ((256, 768), BF),
    "igrad": ((256, 768), BF),
    "qgrad": ((96, 384), F32),
    "ograd": ((96, 384), F32),
    "kgrad": ((128, 384), BF),
    "vgrad": ((128, 384), BF),
}
Q_SCRATCH = {
    "gq": ((32, 192, 384), BF),
    "vnT": ((3072, 256), BF),
    "gradT": ((3072, 256), BF),
    "vid": ((256, 3072), BF),
    "grad": ((256, 3072), BF),
    "att": ((256, 384), BF),
    "dq": ((256, 384), BF),
    "w": ((3, 256, 128), F32),
    "mp": ((3, 256, 384), BF),
    "T": ((32, 3, 8, 384), BF),
    "Dw": ((32, 96, 384), BF),
    "Dq": ((32, 96, 384), BF),
    "ra1": ((2, 5, 2, 48, 384), BF),
    "rb1": ((2, 5, 2, 96, 384), BF),
    "rx1": ((96, 384), BF),
    "ra2": ((2, 5, 2, 48, 384), BF),
    "rb2": ((2, 5, 2, 96, 384), BF),
    "rx2": ((96, 384), BF),
    "op": ((4, 256, 768), BF),
    "o0": ((256, 768), BF),
    "o1": ((256, 768), BF),
    "o2": ((256, 768), BF),
    "o3": ((256, 768), BF),
    "dn": ((4, 256, 768), BF),
    "n0": ((256, 768), BF),
    "n1": ((256, 768), BF),
    "n2": ((256, 768), BF),
    "n3": ((256, 768), BF),
    "scol": ((2, 256, 1), F32),
    "stat": ((4, 2, 8, 256), F32),
    "RG": ((99, 8, 384), BF),
    "CG": ((32, 8, 384), BF),
    "KV": ((32, 8, 384), BF),
}


def fill_tables(r):
    def total(s, acc):
        acc = acc + r.counts[s]
        r.end[s] = acc
        return acc
    lax.fori_loop(0, 32, total, jnp.int32(0))

    @pl.loop(0, 32)
    def _(d):
        count = jnp.int32(0)
        for s in range(32):
            count = count + (r.end[s] <= 256 * d).astype(jnp.int32)
        r.first[d] = count
        for t in range(3):
            r.cap[d * 3 + t] = r.scap[jnp.minimum(count + t, 31)]

    @pl.loop(0, 32)
    def _(c):
        s = jnp.int32(0)
        for t in range(32):
            s = s + jnp.where(r.scap[t] == c, t, 0)
        s = jnp.minimum(s, 31)
        stop = r.end[s]
        d0 = (stop - r.counts[s]) // 256
        for m in range(5):
            d = d0 + m
            valid = (d < 32) & (d * 256 < stop)
            r.sidx[c * 5 + m] = jnp.clip(jnp.where(valid, 3 * d + s - r.first[jnp.minimum(d, 31)], 96), 0, 96)


def named(refs, names):
    r = Refs()
    for n, ref in zip(names, refs):
        setattr(r, n, ref)
    return r


def encode(*refs):
    r = named(refs, P_IN + list(P_OUT) + ["edge", "sidx"] + list(P_SCRATCH) + list(P_TABLES) + ["sems", "lsem", "asem"])
    me = place()
    f, g, core, hi = me["f"], me["g"], me["core"], me["hi"]
    L = Links(r.sems)
    loads = {}

    def load(name, src, dst):
        c = pltpu.make_async_copy(src, dst, r.lsem.at[len(loads)])
        c.start()
        loads[name] = c
    load("cs", r.cs_h, r.cs)

    def load_text(a, wh):
        for k in range(2):
            rows = pl.ds(k * 2048, 2048)
            load(("wt", a, k), wh.at[rows], r.wt.at[a % 2, rows])
    load_text(0, r.tq_h)
    load_text(1, r.tk_h)
    load("bias", r.bias_h, r.bias)
    load("vid", r.vid_h, r.vid)
    load("grad", r.grad_h, r.grad)

    others = eight_others(me)
    fs = [{"grp": g, "fsdp": (f + j) % 32} for j in range(1, 32)]
    barrier(me, fs + [{"grp": (g + j) % 4, "fsdp": f // 2 * 2 + x} for j in range(1, 4) for x in range(2)])

    A, B = Gather(L, me, "w", r.gw, 128), Gather(L, me, "q", r.gq, 192)
    sa, sb = A.stages(r.kv.at[me["x"]], None), B.stages(r.qo, None)
    A.xsend(r.kv.at[1 - me["x"]])
    B.xsend(r.qo)
    sa[0]()
    r.gw[f] = r.kv[me["x"]]
    r.gq[f] = r.qo[...]

    loads["cs"].wait()

    @pl.loop(0, 8)
    def _(i):
        rows = pl.ds(i * 16, 16)
        x = r.cs[rows].astype(F32)
        mean_square = jnp.mean(x * x, axis=-1, keepdims=True)
        r.normed[rows] = (x * lax.rsqrt(mean_square + 1e-06) * r.tgain[...]).astype(BF)

    def project(a):
        acc = jnp.zeros((128, 512), F32)
        for k in range(2):
            loads["wt", a, k].wait()
            acc = acc + jnp.dot(r.normed[:, pl.ds(k * 2048, 2048)], r.wt[a % 2, pl.ds(k * 2048, 2048)], preferred_element_type=F32)
        r.tqkv[a] = acc.astype(BF)
    sa[1]()
    project(0)
    load_text(2, r.tv_h)
    sa[2]()
    sa[3]()
    project(1)
    for k in range(8):
        load(("wo", k), r.tout_h.at[:, pl.ds(k * 512, 512)], r.wt.at[1, pl.ds(k * 512, 512)])
    sa[4]()
    sb[0]()
    project(2)
    sa[5]()
    sb[1]()
    loads["bias"].wait()
    lane = lax.broadcasted_iota(jnp.int32, (128, 128), 1)
    valid = lane < r.lens[f]

    def text_pair(p):
        cols = pl.ds(p * 128, 128)
        q, k, v = r.tqkv[0, :, cols], r.tqkv[1, :, cols], r.tqkv[2, :, cols]
        out = []
        for i in range(2):
            qh = jnp.where((lane < 64) == (i == 0), q.astype(F32), 0.0).astype(BF)
            ex = jnp.where(valid, jnp.exp(dot(qh, k, 1, 1) + r.bias[2 * p + i]), 0.0)
            wts = (ex / jnp.sum(ex, axis=-1, keepdims=True)).astype(BF)
            out.append(dot(wts, v, 1, 0))
        r.tm[:, cols] = jnp.where(lane < 64, out[0], out[1]).astype(BF)
    text_pair(0)
    text_pair(1)
    sa[6]()
    sb[2]()
    sb[3]()
    text_pair(2)
    text_pair(3)
    sa[7]()
    for k in range(8):
        loads["wo", k].wait()
    T = TwoStep(L, me, "t", r.parts, r.t0, r.t1, r.t2, r.t3)
    for j, s in enumerate(T.order()):
        for n in range(2):
            cols = pl.ds(n * 512, 512)
            r.parts[s, :, cols] = jnp.dot(r.tm[...], r.wt[1, pl.ds((2 * s + n) * 512, 512)], preferred_element_type=F32).astype(BF)
        if j < 2:
            T.start(j)
    sa[8]()
    sb[4]()
    T.mid()
    fill_tables(r)
    sa[9]()
    sa[10]()
    sb[5]()
    T.end()

    @pl.loop(0, 8)
    def _(i):
        rows, cols = pl.ds(i * 16, 16), pl.ds(pl.multiple_of(g * 1024, 1024), 1024)
        ts = T.total(rows) + r.cs[rows, cols].astype(F32)
        r.E[me["x"], g, rows] = (ts * r.fgain[:, cols]).astype(BF)
        r.sscol[rows] = jnp.sum(ts * ts, axis=1, keepdims=True)
    X = Eight(L, me, "e", r.E, 128)
    X.start()
    r.SS[me["x"], g] = jnp.broadcast_to(r.sscol[...], (128, 128)).T[:8]
    mine = r.SS.at[me["x"], g]
    for key, d, _ in others:
        L.send(mine, mine, ("ss", (4 - key[0]) % 4, key[1]), d)
    sb[6]()

    loads["vid"].wait()

    @pl.loop(0, 16)
    def _(i):
        rows = pl.ds(i * 16, 16)
        v = r.vid[rows].astype(F32)
        mean = jnp.mean(v, axis=-1, keepdims=True)
        center = v - mean
        inverse = lax.rsqrt(jnp.mean(center * center, axis=-1, keepdims=True) + 1e-06)
        r.mu[rows], r.inv[rows] = mean, inverse
        r.vn[rows] = (center * inverse).astype(BF)
    X.mid()
    sb[7]()
    loads["grad"].wait()

    @pl.loop(0, 24)
    def _(i):
        lanes = pl.ds(pl.multiple_of(i * 128, 128), 128)
        r.vnT[lanes] = r.vn[:, lanes].T
        r.gradT[lanes] = r.grad[:, lanes].T
    X.mid2()
    sa[11]()
    sa[12]()
    sb[8]()
    X.end()
    for key, d, slot in others:
        L.recv(r.SS.at[slot[0], slot[1]], ("ss", key[0], key[1]), d)

    acc = jnp.zeros((256, 384), F32)
    for k in range(4):
        acc = acc + jnp.dot(r.E[:, k].reshape(256, 1024), r.gw[k * 8 : k * 8 + 8].reshape(1024, 384), preferred_element_type=F32)
    for c in range(2):
        ss = r.SS[c, 0, :1] + r.SS[c, 1, :1] + r.SS[c, 2, :1] + r.SS[c, 3, :1]
        col = jnp.broadcast_to(ss, (128, 128)).T[:, :1]
        r.kvp[:, c] = (acc[c * 128 : c * 128 + 128] * lax.rsqrt(col / 4096 + 1e-06)).reshape(16, 8, 384).astype(BF)

    partner = {"grp": g, "fsdp": (f + 1) % 32}
    yz = f // 2

    @pl.loop(1, 16)
    def _(j):
        to = (yz + j) % 16
        pltpu.make_async_remote_copy(src_ref=r.kvp.at[to], dst_ref=r.C.at[pl.ds(2 * yz, 2)], send_sem=r.asem.at[0], recv_sem=r.asem.at[1], device_id={"grp": g, "fsdp": to * 2 + me["x"]}, device_id_type=MESH).start()
    r.C[pl.ds(2 * yz, 2)] = r.kvp[yz]
    sb[9]()
    wait_bytes(r.C.at[pl.ds(0, 30)], r.asem.at[0], r.asem.at[1], partner)

    @pl.loop(1, 32)
    def _(j):
        to = (f + j) % 32
        for s in range(3):
            r.sb[to, s] = r.C[r.cap[to * 3 + s]]
        pltpu.make_async_remote_copy(src_ref=r.sb.at[to], dst_ref=r.R.at[f], send_sem=r.asem.at[2], recv_sem=r.asem.at[3], device_id={"grp": g, "fsdp": to}, device_id_type=MESH).start()
    for s in range(3):
        r.R[f, s] = r.C[r.cap[f * 3 + s]]
    for s in sb[10:]:
        s()

    acc = jnp.zeros((256, 384), F32)
    acc2 = jnp.zeros((256, 384), F32)
    for k in range(4):
        cols = pl.ds(k * 768, 768)
        acc = acc + jnp.dot(r.vn[:, cols], r.gq[k * 8 : k * 8 + 8, 0:96].reshape(768, 384), preferred_element_type=F32)
    r.qb[...] = acc.astype(BF)
    for k in range(4):
        cols = pl.ds(k * 768, 768)
        acc2 = acc2 + jnp.dot(r.grad[:, cols], r.gq[k * 8 : k * 8 + 8, 96:192].reshape(768, 384), preferred_element_type=F32)
    r.da[...] = acc2.astype(BF)

    first = r.first[f]
    r.edge[0], r.edge[1] = r.end[jnp.minimum(first, 31)], r.end[jnp.minimum(first + 1, 31)]
    for s in range(3):
        r.edge[2 + s] = r.lens[r.cap[f * 3 + s]]
    wait_bytes(r.R.at[pl.ds(0, 31)], r.asem.at[2], r.asem.at[3], partner)
    for kv in range(2):
        for s in range(3):
            r.ks[kv, pl.ds(s * 128, 128)] = r.R[:, s].reshape(16, 2, 8, 384)[:, kv].astype(F32).reshape(128, 384).astype(BF)
    A.sent()
    B.sent()
    L.drain()


def attend(*refs):
    r = named(refs, Q_IN + list(Q_OUT) + list(Q_SCRATCH) + ["sems", "lsem", "asem"])
    me = place()
    f, g, core, hi = me["f"], me["g"], me["core"], me["hi"]
    L = Links(r.sems)
    partner = {"grp": g, "fsdp": (f + 1) % 32}
    loads = {}
    for i, n in enumerate(("gradT", "gq", "vnT", "vid", "grad")):
        loads[n] = pltpu.make_async_copy(getattr(r, n + "_h"), getattr(r, n), r.lsem.at[i])
        loads[n].start()
    barrier(me, [{"grp": g, "fsdp": (f + j) % 32} for j in range(1, 32)] + [{"grp": (g + j) % 4, "fsdp": f} for j in range(1, 4)])
    position = lax.broadcasted_iota(jnp.int32, (256, 128), 0) + f * 256
    slot = (position >= r.edge[0]).astype(jnp.int32) + (position >= r.edge[1]).astype(jnp.int32)
    token_len = jnp.where(slot == 0, r.edge[2], jnp.where(slot == 1, r.edge[3], r.edge[4]))
    token_valid = lax.broadcasted_iota(jnp.int32, (256, 128), 1) < token_len
    scale = 1.0 / math.sqrt(HEAD_SIZE)

    def pick(a):
        return jnp.where(slot == 0, a[:, 0:128], jnp.where(slot == 1, a[:, 128:256], a[:, 256:384]))

    def placed(a):
        return jnp.concatenate([jnp.where(slot == s, a, 0.0).astype(BF) for s in range(3)], axis=1)

    for h in range(3):
        cols = pl.ds(h * 128, 128)
        scores = pick(dot(r.qb[:, cols], r.ks[0, :, cols], 1, 1)) * scale
        ex = jnp.where(token_valid, jnp.exp(scores), 0.0)
        w = ex / jnp.sum(ex, axis=-1, keepdims=True)
        r.w[h] = w
        mp = placed(w)
        r.mp[h] = mp
        r.att[:, cols] = dot(mp, r.ks[1, :, cols], 1, 0).astype(BF)

    def weight_grad(D, left, right):
        @pl.loop(0, 8)
        def _(i):
            rows = pl.ds(i * 384, 384)
            D[pl.ds(i * 4, 4)] = dot(left[rows], right[...], 1, 0).reshape(4, 96, 384).astype(BF)
    loads["gradT"].wait()
    weight_grad(r.Dw, r.gradT, r.att)
    S1 = Scatter(L, me, "d1", r.Dw, r.ra1, r.rb1, r.rx1)
    S2 = Scatter(L, me, "d2", r.Dq, r.ra2, r.rb2, r.rx2)
    s1, s2 = S1.stages(), S2.stages()
    s1[0]()
    loads["gq"].wait()
    O = TwoStep(L, me, "o", r.op, r.o0, r.o1, r.o2, r.o3)
    N = TwoStep(L, me, "n", r.dn, r.n0, r.n1, r.n2, r.n3)
    for j, s in enumerate(O.order()):
        r.op[s] = dot(r.att[...], r.gq[pl.ds(s * 8, 8), 96:192].reshape(768, 384), 1, 1).astype(BF)
        if j < 2:
            O.start(j)
    s1[1]()

    for h in range(3):
        cols = pl.ds(h * 128, 128)
        d_probs = pick(dot(r.da[:, cols], r.ks[1, :, cols], 1, 1))
        w = r.w[h]
        ds = w * (d_probs - jnp.sum(w * d_probs, axis=-1, keepdims=True)) * scale
        ms = placed(ds)
        r.dq[:, cols] = dot(ms, r.ks[0, :, cols], 1, 0).astype(BF)
        kt = dot(ms, r.qb[:, cols], 0, 0)
        vt = dot(r.mp[h], r.da[:, cols], 0, 0)
        for s in range(3):
            rows = slice(s * 128, s * 128 + 128)
            both = jnp.stack([kt[rows].reshape(16, 8, 128), vt[rows].reshape(16, 8, 128)], axis=1)
            r.T[:, s, :, cols] = both.reshape(32, 8, 128).astype(BF)
    O.mid()

    @pl.loop(1, 32)
    def _(j):
        to = (f + j) % 32
        pltpu.make_async_remote_copy(src_ref=r.T.at[to], dst_ref=r.RG.at[pl.ds(3 * f, 3)], send_sem=r.asem.at[4], recv_sem=r.asem.at[5], device_id={"grp": g, "fsdp": to}, device_id_type=MESH).start()
    s1[2]()
    s1[3]()
    loads["vnT"].wait()
    weight_grad(r.Dq, r.vnT, r.dq)
    s2[0]()
    s1[4]()
    s1[5]()
    for j, s in enumerate(N.order()):
        r.dn[s] = dot(r.dq[...], r.gq[pl.ds(s * 8, 8), 0:96].reshape(768, 384), 1, 1).astype(BF)
        if j < 2:
            N.start(j)
    s1[6]()
    s1[7]()
    N.mid()
    s1[8]()
    s2[1]()
    s2[2]()
    r.RG[pl.ds(96, 3)] = jnp.zeros((3, 8, 384), BF)
    r.RG[pl.ds(3 * f, 3)] = r.T[f]
    wait_bytes(r.RG.at[pl.ds(0, 93)], r.asem.at[4], r.asem.at[5], partner)

    @pl.loop(0, 32)
    def _(c):
        acc = r.RG[r.sidx[c * 5]].astype(F32)
        for m in range(1, 5):
            acc = acc + r.RG[r.sidx[c * 5 + m]].astype(F32)
        r.CG[c] = acc.astype(BF)

    @pl.loop(1, 32)
    def _(j):
        to = (f + j) % 32
        pltpu.make_async_remote_copy(src_ref=r.CG.at[to], dst_ref=r.KV.at[f], send_sem=r.asem.at[6], recv_sem=r.asem.at[7], device_id={"grp": g, "fsdp": to}, device_id_type=MESH).start()
    r.KV[f] = r.CG[f]
    for i in (9, 10):
        s1[i]()
    for i in (3, 4, 5):
        s2[i]()
    O.end()
    loads["vid"].wait()
    loads["grad"].wait()
    cols = pl.ds(pl.multiple_of(g * 768, 768), 768)

    @pl.loop(0, 16)
    def _(i):
        rows = pl.ds(i * 16, 16)
        r.updated[rows] = (r.vid[rows, cols].astype(F32) + O.total(rows)).astype(BF)
    s2[6]()
    s2[7]()
    N.end()

    def video_hat(rows):
        return (r.vid[rows, cols].astype(F32) - r.mu[rows]) * r.inv[rows]

    @pl.loop(0, 16)
    def _(i):
        rows = pl.ds(i * 16, 16)
        t = N.total(rows)
        r.scol[0, rows] = jnp.sum(t, axis=1, keepdims=True)
        r.scol[1, rows] = jnp.sum(t * video_hat(rows), axis=1, keepdims=True)
    for k in range(2):
        r.stat[g, k] = jnp.broadcast_to(r.scol[k], (256, 128)).T[:8]
    grp = [{"grp": (g + j) % 4, "fsdp": f} for j in range(1, 4)]
    for j in range(1, 4):
        L.send(r.stat.at[g], r.stat.at[g], ("st", j), grp[j - 1])
    for i in (8, 9, 10):
        s2[i]()
    r.ograd[...] = S1.result()
    for j in range(1, 4):
        L.recv(r.stat.at[(g + 4 - j) % 4], ("st", j), grp[3 - j])
    for k in range(2):
        s = r.stat[0, k, :1] + r.stat[1, k, :1] + r.stat[2, k, :1] + r.stat[3, k, :1]
        r.scol[k] = jnp.broadcast_to(s / 3072, (128, 256)).T[:, :1]

    @pl.loop(0, 16)
    def _(i):
        rows = pl.ds(i * 16, 16)
        d = N.total(rows) - r.scol[0, rows] - video_hat(rows) * r.scol[1, rows]
        r.igrad[rows] = (r.grad[rows, cols].astype(F32) + r.inv[rows] * d).astype(BF)
    wait_bytes(r.KV.at[pl.ds(0, 31)], r.asem.at[6], r.asem.at[7], partner)
    r.kgrad[...] = r.KV[...].reshape(16, 2, 8, 384)[:, 0].astype(F32).reshape(128, 384).astype(BF)
    r.vgrad[...] = r.KV[...].reshape(16, 2, 8, 384)[:, 1].astype(F32).reshape(128, 384).astype(BF)
    r.qgrad[...] = S2.result()
    S1.sent()
    S2.sent()
    L.drain()


def local(caption_states, caption_lens, text_gain, text_query, text_key, text_value, text_bias, text_out, final_gain, cross_key, cross_value, video_states, video_counts, sample_caption, cross_query, cross_out, out_grad):
    kv = jnp.stack([cross_key, cross_value])
    qo = jnp.concatenate([cross_query, cross_out.T])
    V, M, A = pltpu.VMEM, pltpu.SMEM, pl.ANY

    def call(kernel, name, cid, args, spaces, outs, tables, scratch, smem):
        return pl.pallas_call(
            kernel,
            out_shape=tuple(jax.ShapeDtypeStruct(s, d) for s, d in outs.values()) + tuple(jax.ShapeDtypeStruct((n,), jnp.int32) for n in tables),
            in_specs=[pl.BlockSpec(memory_space=s) for s in spaces],
            out_specs=tuple(pl.BlockSpec(memory_space=V) for _ in outs) + tuple(pl.BlockSpec(memory_space=M) for _ in tables),
            scratch_shapes=[V(s, d) for s, d in scratch.values()] + [M((n,), jnp.int32) for n in smem] + [DMA((128,)), DMA((24,)), DMA((8,))],
            compiler_params=pltpu.CompilerParams(collective_id=cid, has_side_effects=True, vmem_limit_bytes=58 << 20),
            name=name,
        )(*args)
    args = [caption_lens, video_counts, sample_caption, kv, qo, text_gain[None], final_gain[None], caption_states.reshape(128, 4096), text_query, text_key, text_value, text_bias, text_out, video_states, out_grad]
    qb, da, ks, gq, vnT, gradT, mu, inv, edge, sidx = call(encode, "encode", 0, args, [M] * 3 + [V] * 4 + [A] * 8, P_OUT, (8, 160), P_SCRATCH, P_TABLES.values())
    args = [edge, sidx, qb, da, ks, mu, inv, gq, vnT, gradT, video_states, out_grad]
    updated, igrad, qgrad, ograd, kgrad, vgrad = call(attend, "attend", 1, args, [M] * 2 + [V] * 5 + [A] * 5, Q_OUT, (), Q_SCRATCH, ())
    return updated, igrad, qgrad, ograd.T, kgrad[None], vgrad[None]


def solution(mesh):
    in_specs = (P("fsdp"), P(), P(), P(None, "grp"), P(None, "grp"), P(None, "grp"), P("grp"), P("grp"), P(), P("fsdp", "grp"), P("fsdp", "grp"), P("fsdp"), P(), P(), P("fsdp", "grp"), P("grp", "fsdp"), P("fsdp"))
    out_specs = (P("fsdp", "grp"), P("fsdp", "grp"), P("fsdp", "grp"), P("grp", "fsdp"), P("fsdp", None, "grp"), P("fsdp", None, "grp"))
    return jax.shard_map(local, mesh=mesh, in_specs=in_specs, out_specs=out_specs, check_vma=False)
```

```python
import math

import jax
import jax.numpy as jnp
from jax import lax
from jax.experimental import pallas as pl
from jax.experimental.pallas import tpu as pltpu
from jax.sharding import PartitionSpec as P
MESH = pl.DeviceIdType.MESH
BF, F32 = jnp.bfloat16, jnp.float32
DMA = pltpu.SemaphoreType.DMA
HEAD_SIZE = 128

class Links:
    def __init__(self, sems):
        self.sems, self.keys, self.pending = sems, {}, []
    def sem(self, key):
        return self.sems.at[self.keys.setdefault(key, len(self.keys))]
    def copy(self, src, dst, key, dev, group=None):
        send = self.sem(("s", group if group else key))
        return pltpu.make_async_remote_copy(src_ref=src, dst_ref=dst, send_sem=send, recv_sem=self.sem(("r", key)), device_id=dev, device_id_type=MESH)
    def send(self, src, dst, key, dev, group=None):
        c = self.copy(src, dst, key, dev, group)
        c.start()
        if group is None:
            self.pending.append(c)
    def recv(self, dst, key, dev, group=None):
        self.copy(dst, dst, key, dev, group).wait_recv()
    def sent(self, blocks, group, key, dev):
        self.copy(blocks, blocks, key, dev, group).wait_send()
    def drain(self):
        for c in self.pending:
            c.wait_send()
        self.pending = []

def place():
    g, f = lax.axis_index("grp"), lax.axis_index("fsdp")
    return dict(hi=g // 2, core=g % 2, y=f // 8, z=(f // 2) % 4, x=f % 2, g=g, f=f)

def dev(hi, core, y, z, x):
    return {"grp": hi * 2 + core, "fsdp": (y * 4 + z) * 2 + x}

class Gather:
    def __init__(self, L, me, name, G, rows):
        self.L, self.me, self.name, self.G, self.rows = L, me, name, G, rows
    def nb(self, part, first, d):
        m = self.me
        use_z = (m["x"] == 0) if (part == 0) == first else (m["x"] == 1)
        zi = jnp.where(use_z, (m["z"] + d) % 4, m["z"])
        yi = jnp.where(use_z, m["y"], (m["y"] + d) % 4)
        return {"fsdp": (yi * 4 + zi) * 2 + m["x"], "grp": m["g"]}
    def idx(self, part, d1, d2):
        m = self.me
        use_z = (m["x"] == 0) if part == 0 else (m["x"] == 1)
        dz = jnp.where(use_z, d1, d2)
        dy = jnp.where(use_z, d2, d1)
        px = m["x"] if part == 0 else 1 - m["x"]
        return (((m["y"] + dy) % 4) * 4 + (m["z"] + dz) % 4) * 2 + px
    def ref(self, part, d1, d2, half=None):
        b = self.G.at[self.idx(part, d1, d2)]
        if half is None:
            return b
        h = self.rows // 2
        return b.at[pl.ds(half * h, h)]
    def xsend(self, src):
        m = self.me
        self.L.send(src, self.G.at[m["f"]], (self.name, "x"), {"grp": m["g"], "fsdp": m["f"] + 1 - 2 * m["x"]}, self.name)
    def xrecv(self):
        m = self.me
        self.L.recv(self.ref(1, 0, 0), (self.name, "x"), {"grp": m["g"], "fsdp": m["f"] + 1 - 2 * m["x"]}, self.name)
    def s1(self, part, first, k, src=None):
        d = (0, 0) if first else (k, 0)
        r = self.ref(part, *d)
        src = r if src is None else src
        for s in (1, 3):
            self.L.send(src, r, (self.name, part, first, k, "s1", s), self.nb(part, first, s), self.name)
    def s2(self, part, first, k, s):
        o = 4 - s
        d = (o, 0) if first else (k, o)
        self.L.recv(self.ref(part, *d), (self.name, part, first, k, "s1", s), self.nb(part, first, o), self.name)
        half = 0 if s == 1 else 1
        r = self.ref(part, *d, half)
        self.L.send(r, r, (self.name, part, first, k, "s2", s), self.nb(part, first, s), self.name)
    def s3(self, part, first, k):
        d = (2, 0) if first else (k, 2)
        for s in (1, 3):
            half = 0 if s == 1 else 1
            self.L.recv(self.ref(part, *d, half), (self.name, part, first, k, "s2", s), self.nb(part, first, 4 - s), self.name)
    def stages(self, own):
        def a():
            self.s1(0, True, 0, own)
            self.s1(0, False, 0, own)
        def b():
            self.xrecv()
            self.s1(1, True, 0)
            self.s1(1, False, 0)
        def c():
            for part in (0, 1):
                self.s2(part, True, 0, 1)
                self.s2(part, True, 0, 3)
        def d():
            for k in (1, 3):
                self.s1(0, False, k); self.s1(1, False, k)
        def e():
            self.s3(0, True, 0); self.s1(0, False, 2)
            self.s3(1, True, 0); self.s1(1, False, 2)
        def fw(k):
            def f():
                for part in (0, 1):
                    self.s2(part, False, k, 1); self.s2(part, False, k, 3)
            return f
        def fin(k):
            def f():
                for part in (0, 1):
                    self.s3(part, False, k)
            return f
        return [a, b, c, d, e, fw(0), fw(1), fin(0), fw(3), fin(1), fw(2), fin(3), fin(2)]
    def sent(self):
        m = self.me
        self.L.sent(self.G.at[pl.ds(0, 31)], self.name, (self.name, "x"), {"grp": m["g"], "fsdp": m["f"] + 1 - 2 * m["x"]})

def barrier(me, devs):
    b = pltpu.get_barrier_semaphore()
    for d in devs:
        pl.semaphore_signal(b, inc=1, device_id=d, device_id_type=MESH)
    pl.semaphore_wait(b, len(devs))

def neighbours(me):
    m = me
    out = [{"grp": m["g"], "fsdp": m["f"] + 1 - 2 * m["x"]}]
    for d in (1, 3):
        out.append({"grp": m["g"], "fsdp": (m["y"] * 4 + (m["z"] + d) % 4) * 2 + m["x"]})
        out.append({"grp": m["g"], "fsdp": (((m["y"] + d) % 4) * 4 + m["z"]) * 2 + m["x"]})
    return out


class TwoStep:
    def __init__(self, L, me, name, parts, r0, r1, s1, r2):
        self.L, self.me, self.name = L, me, name
        self.parts, self.r, self.s1, self.r2 = parts, (r0, r1), s1, r2
        self.sib = {"grp": me["g"] + 1 - 2 * me["core"], "fsdp": me["f"]}
        self.opp = {"grp": (1 - me["hi"]) * 2 + me["core"], "fsdp": me["f"]}
    def order(self):
        hi, core = self.me["hi"], self.me["core"]
        return [2 * (1 - hi) + 1 - core, 2 * hi + 1 - core, 2 * (1 - hi) + core, 2 * hi + core]
    def start(self, j):
        self.L.send(self.parts.at[self.order()[j]], self.r[j], (self.name, "c", j), self.sib)
    def mid(self):
        m = self.me
        self.L.recv(self.r[0], (self.name, "c", 0), self.sib)
        for i in range(self.s1.shape[0] // 32):
            rows = pl.ds(i * 32, 32)
            self.s1[rows] = (self.parts[2 * (1 - m["hi"]) + m["core"], rows].astype(F32) + self.r[0][rows].astype(F32)).astype(BF)
        self.L.send(self.s1, self.r2, (self.name, "o"), self.opp)
    def end(self):
        self.L.recv(self.r[1], (self.name, "c", 1), self.sib)
        self.L.recv(self.r2, (self.name, "o"), self.opp)
    def total(self, rows):
        m = self.me
        return self.parts[2 * m["hi"] + m["core"], rows].astype(F32) + self.r[1][rows].astype(F32) + self.r2[rows].astype(F32)


def along_x(me, d):
    X = (me["hi"] * 2 + me["x"] + d) % 4
    return X // 2, X % 2


def same_core(me, d):
    hi, x = along_x(me, d)
    return dev(hi, me["core"], me["y"], me["z"], x)


class Eight:
    def __init__(self, L, me, name, E, rows):
        self.L, self.me, self.name, self.E, self.rows = L, me, name, E, rows
        self.sib = {"grp": me["g"] + 1 - 2 * me["core"], "fsdp": me["f"]}
    def ref(self, d, core, half=None):
        hi, x = along_x(self.me, d)
        r = self.E.at[x, hi * 2 + core]
        if half is None:
            return r
        h = self.rows // 2
        return r.at[pl.ds(half * h, h)]
    def start(self):
        r = self.ref(0, self.me["core"])
        for s in (1, 3):
            self.L.send(r, r, (self.name, "s1", s), same_core(self.me, s))
        self.L.send(r, r, (self.name, "sib", 0), self.sib)
    def mid(self):
        c = self.me["core"]
        for s in (1, 3):
            r = self.ref(4 - s, c)
            self.L.recv(r, (self.name, "s1", s), same_core(self.me, s))
            half = 0 if s == 1 else 1
            rh = self.ref(4 - s, c, half)
            self.L.send(rh, rh, (self.name, "s2", s), same_core(self.me, s))
            self.L.send(r, r, (self.name, "sib", 4 - s), self.sib)
    def mid2(self):
        c = self.me["core"]
        for s in (1, 3):
            half = 0 if s == 1 else 1
            rh = self.ref(2, c, half)
            self.L.recv(rh, (self.name, "s2", s), same_core(self.me, s))
            self.L.send(rh, rh, (self.name, "sib2", s), self.sib)
    def end(self):
        oc = 1 - self.me["core"]
        for d in (0, 1, 3):
            self.L.recv(self.ref(d, oc), (self.name, "sib", d), self.sib)
        for s in (1, 3):
            self.L.recv(self.ref(2, oc, 0 if s == 1 else 1), (self.name, "sib2", s), self.sib)


def eight_others(me):
    out = []
    for d in range(4):
        hi, x = along_x(me, d)
        for c in (0, 1):
            if d == 0 and c == 0:
                continue
            core = 1 - me["core"] if c == 1 else me["core"]
            out.append(((d, c), dev(hi, core, me["y"], me["z"], x), (x, hi * 2 + core)))
    return out


class Scatter:
    def __init__(self, L, me, name, D, ra, rb, rx):
        self.L, self.me, self.name, self.D, self.ra, self.rb, self.rx = L, me, name, D, ra, rb, rx
        self.rows = D.shape[1]
    def axis(self, part, stage):
        m = self.me
        own = m["x"] == 0 if part == 0 else m["x"] == 1
        return own if stage == 1 else jnp.logical_not(own)
    def nb(self, part, stage, d):
        m = self.me
        use_z = self.axis(part, stage)
        zi = jnp.where(use_z, (m["z"] + d) % 4, m["z"])
        yi = jnp.where(use_z, m["y"], (m["y"] + d) % 4)
        return {"fsdp": (yi * 4 + zi) * 2 + m["x"], "grp": m["g"]}
    def ref(self, part, stage, k, d, half=None):
        m = self.me
        use_z = self.axis(part, stage)
        dz = jnp.where(use_z, d, k)
        dy = jnp.where(use_z, k, d)
        px = m["x"] if part == 0 else 1 - m["x"]
        b = self.D.at[(((m["y"] + dy) % 4) * 4 + (m["z"] + dz) % 4) * 2 + px]
        if half is None:
            return b
        h = self.rows // 2
        return b.at[pl.ds(half * h, h)]
    def slot(self, stage, k):
        return k if stage == 0 else 4
    def far(self, part, stage, k):
        h = self.rows // 2
        for s in (1, 3):
            half = 0 if s == 1 else 1
            self.L.send(self.ref(part, stage, k, 2, half), self.ra.at[part, self.slot(stage, k), half], (self.name, part, stage, k, "far", s), self.nb(part, stage, s), self.name)
    def near(self, part, stage, k):
        h = self.rows // 2
        for s in (1, 3):
            half = 0 if s == 1 else 1
            buf = self.ra.at[part, self.slot(stage, k), half]
            self.L.recv(buf, (self.name, part, stage, k, "far", s), self.nb(part, stage, 4 - s), self.name)
            r = self.ref(part, stage, k, s, half)
            r[...] = (r[...].astype(F32) + buf[...].astype(F32)).astype(BF)
            self.L.send(self.ref(part, stage, k, s), self.rb.at[part, self.slot(stage, k), half], (self.name, part, stage, k, "near", s), self.nb(part, stage, s), self.name)
    def total(self, part, stage, k):
        for s in (1, 3):
            half = 0 if s == 1 else 1
            self.L.recv(self.rb.at[part, self.slot(stage, k), half], (self.name, part, stage, k, "near", s), self.nb(part, stage, 4 - s), self.name)
        b = self.rb.at[part, self.slot(stage, k)]
        return self.ref(part, stage, k, 0)[...].astype(F32) + b[0].astype(F32) + b[1].astype(F32)
    def fold(self, part, stage, k):
        t = self.total(part, stage, k)
        self.ref(part, stage, k, 0)[...] = t.astype(BF)
    def partner(self):
        m = self.me
        return {"grp": m["g"], "fsdp": m["f"] + 1 - 2 * m["x"]}
    def xsend(self):
        self.fold(1, 1, 0)
        self.L.send(self.ref(1, 1, 0, 0), self.rx, (self.name, "x"), self.partner(), self.name)
    def result(self):
        t = self.total(0, 1, 0)
        self.L.recv(self.rx, (self.name, "x"), self.partner(), self.name)
        return t + self.rx[...].astype(F32)
    def stages(self):
        def a():
            for k in (2, 1, 3, 0):
                for part in (1, 0):
                    self.far(part, 0, k)
        def b(k):
            def f():
                for part in (1, 0):
                    self.near(part, 0, k)
            return f
        def c(k):
            def f():
                for part in (1, 0):
                    self.fold(part, 0, k)
                    if k == 2:
                        self.far(part, 1, 0)
            return f
        def d():
            for part in (1, 0):
                self.near(part, 1, 0)
        return [a, b(2), b(1), c(2), b(3), c(1), b(0), c(3), d, c(0), self.xsend]
    def sent(self):
        self.L.sent(self.D.at[pl.ds(0, 31)], self.name, (self.name, "x"), self.partner())


def wait_bytes(like, send_sem, recv_sem, devid, recv=True, send=True):
    c = pltpu.make_async_remote_copy(src_ref=like, dst_ref=like, send_sem=send_sem, recv_sem=recv_sem, device_id=devid, device_id_type=MESH)
    if recv:
        c.wait_recv()
    if send:
        c.wait_send()


def dot(a, b, ca, cb):
    return lax.dot_general(a, b, (((ca,), (cb,)), ((), ())), preferred_element_type=F32)


class Refs:
    pass


P_IN = ["lens", "counts", "scap", "tgain", "fgain", "cs_h", "tq_h", "tk_h", "tv_h", "bias_h", "tout_h", "vid_h", "grad_h", "ck_h", "cv_h", "cq_h", "co_h"]
P_OUT = {
    "qb": ((256, 384), BF),
    "da": ((256, 384), BF),
    "ks": ((2, 384, 384), BF),
    "gq": ((32, 192, 384), BF),
    "vnT": ((3072, 256), BF),
    "gradT": ((3072, 256), BF),
    "mu": ((256, 1), F32),
    "inv": ((256, 1), F32),
}
P_SCRATCH = {
    "kv": ((2, 128, 384), BF),
    "qo": ((192, 384), BF),
    "cs": ((128, 4096), BF),
    "normed": ((128, 4096), BF),
    "wt": ((2, 4096, 512), BF),
    "bias": ((8, 128, 128), F32),
    "tqkv": ((3, 128, 512), BF),
    "tm": ((128, 512), BF),
    "vid": ((256, 3072), BF),
    "grad": ((256, 3072), BF),
    "vn": ((256, 3072), BF),
    "gw": ((32, 128, 384), BF),
    "parts": ((4, 128, 1024), BF),
    "t0": ((128, 1024), BF),
    "t1": ((128, 1024), BF),
    "t2": ((128, 1024), BF),
    "t3": ((128, 1024), BF),
    "E": ((2, 4, 128, 1024), BF),
    "sscol": ((128, 1), F32),
    "SS": ((2, 4, 8, 128), F32),
    "kvp": ((16, 2, 8, 384), BF),
    "C": ((32, 8, 384), BF),
    "sb": ((32, 3, 8, 384), BF),
    "R": ((32, 3, 8, 384), BF),
}
P_TABLES = {"end": 32, "first": 32, "cap": 96, "samp": 32}
Q_IN = ["edge", "sidx", "qb", "da", "ks", "mu", "inv", "gq_h", "vnT_h", "gradT_h", "vid_h", "grad_h"]
Q_OUT = {
    "updated": ((256, 768), BF),
    "igrad": ((256, 768), BF),
    "qgrad": ((96, 384), F32),
    "ograd": ((96, 384), F32),
    "kgrad": ((128, 384), BF),
    "vgrad": ((128, 384), BF),
}
Q_SCRATCH = {
    "gq": ((32, 192, 384), BF),
    "vnT": ((3072, 256), BF),
    "gradT": ((3072, 256), BF),
    "vid": ((256, 3072), BF),
    "grad": ((256, 3072), BF),
    "att": ((256, 384), BF),
    "dq": ((256, 384), BF),
    "w": ((3, 256, 128), F32),
    "mp": ((3, 256, 384), BF),
    "T": ((32, 3, 8, 384), BF),
    "Dw": ((32, 96, 384), BF),
    "Dq": ((32, 96, 384), BF),
    "ra1": ((2, 5, 2, 48, 384), BF),
    "rb1": ((2, 5, 2, 96, 384), BF),
    "rx1": ((96, 384), BF),
    "ra2": ((2, 5, 2, 48, 384), BF),
    "rb2": ((2, 5, 2, 96, 384), BF),
    "rx2": ((96, 384), BF),
    "op": ((4, 256, 768), BF),
    "o0": ((256, 768), BF),
    "o1": ((256, 768), BF),
    "o2": ((256, 768), BF),
    "o3": ((256, 768), BF),
    "dn": ((4, 256, 768), BF),
    "n0": ((256, 768), BF),
    "n1": ((256, 768), BF),
    "n2": ((256, 768), BF),
    "n3": ((256, 768), BF),
    "scol": ((2, 256, 1), F32),
    "stat": ((4, 2, 8, 256), F32),
    "RG": ((99, 8, 384), BF),
    "CG": ((32, 8, 384), BF),
    "KV": ((32, 8, 384), BF),
}


def fill_tables(r):
    def total(s, acc):
        acc = acc + r.counts[s]
        r.end[s] = acc
        return acc
    lax.fori_loop(0, 32, total, jnp.int32(0))

    @pl.loop(0, 32)
    def _(d):
        count = jnp.int32(0)
        for s in range(32):
            count = count + (r.end[s] <= 256 * d).astype(jnp.int32)
        r.first[d] = count
        for t in range(3):
            r.cap[d * 3 + t] = r.scap[jnp.minimum(count + t, 31)]

    @pl.loop(0, 32)
    def _(c):
        s = jnp.int32(0)
        for t in range(32):
            s = s + jnp.where(r.scap[t] == c, t, 0)
        s = jnp.minimum(s, 31)
        stop = r.end[s]
        d0 = (stop - r.counts[s]) // 256
        for m in range(5):
            d = d0 + m
            valid = (d < 32) & (d * 256 < stop)
            r.sidx[c * 5 + m] = jnp.clip(jnp.where(valid, 3 * d + s - r.first[jnp.minimum(d, 31)], 96), 0, 96)


def named(refs, names):
    r = Refs()
    for n, ref in zip(names, refs):
        setattr(r, n, ref)
    return r


def encode(*refs):
    r = named(refs, P_IN + list(P_OUT) + ["edge", "sidx"] + list(P_SCRATCH) + list(P_TABLES) + ["sems", "lsem", "asem"])
    me = place()
    f, g, core, hi = me["f"], me["g"], me["core"], me["hi"]
    L = Links(r.sems)
    loads = {}

    def load(name, src, dst):
        c = pltpu.make_async_copy(src, dst, r.lsem.at[len(loads)])
        c.start()
        loads[name] = c
    load("ck", r.ck_h, r.kv.at[0])
    load("cv", r.cv_h, r.kv.at[1])
    load("cq", r.cq_h, r.qo.at[pl.ds(0, 96)])
    load("co", r.co_h, r.qo.at[pl.ds(96, 96)])
    load("cs", r.cs_h, r.cs)

    def load_text(a, wh):
        for k in range(2):
            rows = pl.ds(k * 2048, 2048)
            load(("wt", a, k), wh.at[rows], r.wt.at[a % 2, rows])
    load_text(0, r.tq_h)
    load_text(1, r.tk_h)
    load("bias", r.bias_h, r.bias)
    load("vid", r.vid_h, r.vid)
    load("grad", r.grad_h, r.grad)

    others = eight_others(me)
    fs = [{"grp": g, "fsdp": (f + j) % 32} for j in range(1, 32)]
    barrier(me, fs + [{"grp": (g + j) % 4, "fsdp": f // 2 * 2 + x} for j in range(1, 4) for x in range(2)])

    A, B = Gather(L, me, "w", r.gw, 128), Gather(L, me, "q", r.gq, 192)
    sa, sb = A.stages(r.kv.at[me["x"]]), B.stages(r.qo)
    for n in ("ck", "cv", "cq", "co"):
        loads[n].wait()
    A.xsend(r.kv.at[1 - me["x"]])
    sa[0]()
    B.xsend(r.qo)
    sb[0]()
    r.gw[f] = r.kv[me["x"]]
    r.gq[f] = r.qo[...]

    loads["cs"].wait()

    @pl.loop(0, 8)
    def _(i):
        rows = pl.ds(i * 16, 16)
        x = r.cs[rows].astype(F32)
        mean_square = jnp.mean(x * x, axis=-1, keepdims=True)
        r.normed[rows] = (x * lax.rsqrt(mean_square + 1e-06) * r.tgain[...]).astype(BF)

    def project(a):
        acc = jnp.zeros((128, 512), F32)
        for k in range(2):
            loads["wt", a, k].wait()
            acc = acc + jnp.dot(r.normed[:, pl.ds(k * 2048, 2048)], r.wt[a % 2, pl.ds(k * 2048, 2048)], preferred_element_type=F32)
        r.tqkv[a] = acc.astype(BF)
    project(0)
    load_text(2, r.tv_h)
    sa[1]()
    project(1)
    for k in range(8):
        load(("wo", k), r.tout_h.at[:, pl.ds(k * 512, 512)], r.wt.at[1, pl.ds(k * 512, 512)])
    sb[1]()
    project(2)
    sa[2]()
    sa[3]()
    loads["bias"].wait()
    lane = lax.broadcasted_iota(jnp.int32, (128, 128), 1)
    valid = lane < r.lens[f]

    def text_pair(p):
        cols = pl.ds(p * 128, 128)
        q, k, v = r.tqkv[0, :, cols], r.tqkv[1, :, cols], r.tqkv[2, :, cols]
        out = []
        for i in range(2):
            qh = jnp.where((lane < 64) == (i == 0), q.astype(F32), 0.0).astype(BF)
            ex = jnp.where(valid, jnp.exp(dot(qh, k, 1, 1) + r.bias[2 * p + i]), 0.0)
            wts = (ex / jnp.sum(ex, axis=-1, keepdims=True)).astype(BF)
            out.append(dot(wts, v, 1, 0))
        r.tm[:, cols] = jnp.where(lane < 64, out[0], out[1]).astype(BF)
    text_pair(0)
    text_pair(1)
    sb[2]()
    sb[3]()
    text_pair(2)
    text_pair(3)
    sa[4]()
    sa[5]()
    for k in range(8):
        loads["wo", k].wait()
    T = TwoStep(L, me, "t", r.parts, r.t0, r.t1, r.t2, r.t3)
    for j, s in enumerate(T.order()):
        for n in range(2):
            cols = pl.ds(n * 512, 512)
            r.parts[s, :, cols] = jnp.dot(r.tm[...], r.wt[1, pl.ds((2 * s + n) * 512, 512)], preferred_element_type=F32).astype(BF)
        if j < 2:
            T.start(j)
    sb[4]()
    sb[5]()
    T.mid()
    fill_tables(r)
    sa[6]()
    sb[6]()
    T.end()

    @pl.loop(0, 8)
    def _(i):
        rows, cols = pl.ds(i * 16, 16), pl.ds(pl.multiple_of(g * 1024, 1024), 1024)
        ts = T.total(rows) + r.cs[rows, cols].astype(F32)
        r.E[me["x"], g, rows] = (ts * r.fgain[:, cols]).astype(BF)
        r.sscol[rows] = jnp.sum(ts * ts, axis=1, keepdims=True)
    X = Eight(L, me, "e", r.E, 128)
    X.start()
    r.SS[me["x"], g] = jnp.broadcast_to(r.sscol[...], (128, 128)).T[:8]
    mine = r.SS.at[me["x"], g]
    for key, d, _ in others:
        L.send(mine, mine, ("ss", (4 - key[0]) % 4, key[1]), d)
    sa[7]()
    sa[8]()

    loads["vid"].wait()

    @pl.loop(0, 16)
    def _(i):
        rows = pl.ds(i * 16, 16)
        v = r.vid[rows].astype(F32)
        mean = jnp.mean(v, axis=-1, keepdims=True)
        center = v - mean
        inverse = lax.rsqrt(jnp.mean(center * center, axis=-1, keepdims=True) + 1e-06)
        r.mu[rows], r.inv[rows] = mean, inverse
        r.vn[rows] = (center * inverse).astype(BF)
    X.mid()
    sb[7]()
    sb[8]()
    loads["grad"].wait()

    @pl.loop(0, 24)
    def _(i):
        lanes = pl.ds(pl.multiple_of(i * 128, 128), 128)
        r.vnT[lanes] = r.vn[:, lanes].T
        r.gradT[lanes] = r.grad[:, lanes].T
    X.mid2()
    for i in range(9, 13):
        sa[i]()
    sb[9]()
    sb[10]()
    X.end()
    for key, d, slot in others:
        L.recv(r.SS.at[slot[0], slot[1]], ("ss", key[0], key[1]), d)

    acc = jnp.zeros((256, 384), F32)
    for k in range(4):
        acc = acc + jnp.dot(r.E[:, k].reshape(256, 1024), r.gw[k * 8 : k * 8 + 8].reshape(1024, 384), preferred_element_type=F32)
    for c in range(2):
        ss = r.SS[c, 0, :1] + r.SS[c, 1, :1] + r.SS[c, 2, :1] + r.SS[c, 3, :1]
        col = jnp.broadcast_to(ss, (128, 128)).T[:, :1]
        r.kvp[:, c] = (acc[c * 128 : c * 128 + 128] * lax.rsqrt(col / 4096 + 1e-06)).reshape(16, 8, 384).astype(BF)

    partner = {"grp": g, "fsdp": (f + 1) % 32}
    yz = f // 2

    @pl.loop(1, 16)
    def _(j):
        to = (yz + j) % 16
        pltpu.make_async_remote_copy(src_ref=r.kvp.at[to], dst_ref=r.C.at[pl.ds(2 * yz, 2)], send_sem=r.asem.at[0], recv_sem=r.asem.at[1], device_id={"grp": g, "fsdp": to * 2 + me["x"]}, device_id_type=MESH).start()
    r.C[pl.ds(2 * yz, 2)] = r.kvp[yz]
    wait_bytes(r.C.at[pl.ds(0, 30)], r.asem.at[0], r.asem.at[1], partner)

    @pl.loop(1, 32)
    def _(j):
        to = (f + j) % 32
        for s in range(3):
            r.sb[to, s] = r.C[r.cap[to * 3 + s]]
        pltpu.make_async_remote_copy(src_ref=r.sb.at[to], dst_ref=r.R.at[f], send_sem=r.asem.at[2], recv_sem=r.asem.at[3], device_id={"grp": g, "fsdp": to}, device_id_type=MESH).start()
    for s in range(3):
        r.R[f, s] = r.C[r.cap[f * 3 + s]]
    for s in sb[11:]:
        s()

    acc = jnp.zeros((256, 384), F32)
    acc2 = jnp.zeros((256, 384), F32)
    for k in range(4):
        cols = pl.ds(k * 768, 768)
        acc = acc + jnp.dot(r.vn[:, cols], r.gq[k * 8 : k * 8 + 8, 0:96].reshape(768, 384), preferred_element_type=F32)
    r.qb[...] = acc.astype(BF)
    for k in range(4):
        cols = pl.ds(k * 768, 768)
        acc2 = acc2 + jnp.dot(r.grad[:, cols], r.gq[k * 8 : k * 8 + 8, 96:192].reshape(768, 384), preferred_element_type=F32)
    r.da[...] = acc2.astype(BF)

    first = r.first[f]
    r.edge[0], r.edge[1] = r.end[jnp.minimum(first, 31)], r.end[jnp.minimum(first + 1, 31)]
    for s in range(3):
        r.edge[2 + s] = r.lens[r.cap[f * 3 + s]]
    wait_bytes(r.R.at[pl.ds(0, 31)], r.asem.at[2], r.asem.at[3], partner)
    for kv in range(2):
        for s in range(3):
            r.ks[kv, pl.ds(s * 128, 128)] = r.R[:, s].reshape(16, 2, 8, 384)[:, kv].astype(F32).reshape(128, 384).astype(BF)
    A.sent()
    B.sent()
    L.drain()


def attend(*refs):
    r = named(refs, Q_IN + list(Q_OUT) + list(Q_SCRATCH) + ["sems", "lsem", "asem"])
    me = place()
    f, g, core, hi = me["f"], me["g"], me["core"], me["hi"]
    L = Links(r.sems)
    partner = {"grp": g, "fsdp": (f + 1) % 32}
    loads = {}
    for i, n in enumerate(("gradT", "gq", "vnT", "vid", "grad")):
        loads[n] = pltpu.make_async_copy(getattr(r, n + "_h"), getattr(r, n), r.lsem.at[i])
        loads[n].start()
    barrier(me, [{"grp": g, "fsdp": (f + j) % 32} for j in range(1, 32)] + [{"grp": (g + j) % 4, "fsdp": f} for j in range(1, 4)])
    position = lax.broadcasted_iota(jnp.int32, (256, 128), 0) + f * 256
    slot = (position >= r.edge[0]).astype(jnp.int32) + (position >= r.edge[1]).astype(jnp.int32)
    token_len = jnp.where(slot == 0, r.edge[2], jnp.where(slot == 1, r.edge[3], r.edge[4]))
    token_valid = lax.broadcasted_iota(jnp.int32, (256, 128), 1) < token_len
    scale = 1.0 / math.sqrt(HEAD_SIZE)

    def pick(a):
        return jnp.where(slot == 0, a[:, 0:128], jnp.where(slot == 1, a[:, 128:256], a[:, 256:384]))

    def placed(a):
        return jnp.concatenate([jnp.where(slot == s, a, 0.0).astype(BF) for s in range(3)], axis=1)

    for h in range(3):
        cols = pl.ds(h * 128, 128)
        scores = pick(dot(r.qb[:, cols], r.ks[0, :, cols], 1, 1)) * scale
        ex = jnp.where(token_valid, jnp.exp(scores), 0.0)
        w = ex / jnp.sum(ex, axis=-1, keepdims=True)
        r.w[h] = w
        mp = placed(w)
        r.mp[h] = mp
        r.att[:, cols] = dot(mp, r.ks[1, :, cols], 1, 0).astype(BF)

    def weight_grad(D, left, right):
        @pl.loop(0, 8)
        def _(i):
            rows = pl.ds(i * 384, 384)
            D[pl.ds(i * 4, 4)] = dot(left[rows], right[...], 1, 0).reshape(4, 96, 384).astype(BF)
    loads["gradT"].wait()
    weight_grad(r.Dw, r.gradT, r.att)
    S1 = Scatter(L, me, "d1", r.Dw, r.ra1, r.rb1, r.rx1)
    S2 = Scatter(L, me, "d2", r.Dq, r.ra2, r.rb2, r.rx2)
    s1, s2 = S1.stages(), S2.stages()
    s1[0]()
    loads["gq"].wait()
    O = TwoStep(L, me, "o", r.op, r.o0, r.o1, r.o2, r.o3)
    N = TwoStep(L, me, "n", r.dn, r.n0, r.n1, r.n2, r.n3)
    for j, s in enumerate(O.order()):
        r.op[s] = dot(r.att[...], r.gq[pl.ds(s * 8, 8), 96:192].reshape(768, 384), 1, 1).astype(BF)
        if j < 2:
            O.start(j)
    s1[1]()

    for h in range(3):
        cols = pl.ds(h * 128, 128)
        d_probs = pick(dot(r.da[:, cols], r.ks[1, :, cols], 1, 1))
        w = r.w[h]
        ds = w * (d_probs - jnp.sum(w * d_probs, axis=-1, keepdims=True)) * scale
        ms = placed(ds)
        r.dq[:, cols] = dot(ms, r.ks[0, :, cols], 1, 0).astype(BF)
        kt = dot(ms, r.qb[:, cols], 0, 0)
        vt = dot(r.mp[h], r.da[:, cols], 0, 0)
        for s in range(3):
            rows = slice(s * 128, s * 128 + 128)
            both = jnp.stack([kt[rows].reshape(16, 8, 128), vt[rows].reshape(16, 8, 128)], axis=1)
            r.T[:, s, :, cols] = both.reshape(32, 8, 128).astype(BF)
    O.mid()

    @pl.loop(1, 32)
    def _(j):
        to = (f + j) % 32
        pltpu.make_async_remote_copy(src_ref=r.T.at[to], dst_ref=r.RG.at[pl.ds(3 * f, 3)], send_sem=r.asem.at[4], recv_sem=r.asem.at[5], device_id={"grp": g, "fsdp": to}, device_id_type=MESH).start()
    s1[2]()
    s1[3]()
    loads["vnT"].wait()
    weight_grad(r.Dq, r.vnT, r.dq)
    s2[0]()
    s1[4]()
    s1[5]()
    for j, s in enumerate(N.order()):
        r.dn[s] = dot(r.dq[...], r.gq[pl.ds(s * 8, 8), 0:96].reshape(768, 384), 1, 1).astype(BF)
        if j < 2:
            N.start(j)
    s1[6]()
    s1[7]()
    N.mid()
    s1[8]()
    s2[1]()
    s2[2]()
    r.RG[pl.ds(96, 3)] = jnp.zeros((3, 8, 384), BF)
    r.RG[pl.ds(3 * f, 3)] = r.T[f]
    wait_bytes(r.RG.at[pl.ds(0, 93)], r.asem.at[4], r.asem.at[5], partner)

    @pl.loop(0, 32)
    def _(c):
        acc = r.RG[r.sidx[c * 5]].astype(F32)
        for m in range(1, 5):
            acc = acc + r.RG[r.sidx[c * 5 + m]].astype(F32)
        r.CG[c] = acc.astype(BF)

    @pl.loop(1, 32)
    def _(j):
        to = (f + j) % 32
        pltpu.make_async_remote_copy(src_ref=r.CG.at[to], dst_ref=r.KV.at[f], send_sem=r.asem.at[6], recv_sem=r.asem.at[7], device_id={"grp": g, "fsdp": to}, device_id_type=MESH).start()
    r.KV[f] = r.CG[f]
    for i in (9, 10):
        s1[i]()
    for i in (3, 4, 5):
        s2[i]()
    O.end()
    loads["vid"].wait()
    loads["grad"].wait()
    cols = pl.ds(pl.multiple_of(g * 768, 768), 768)

    @pl.loop(0, 16)
    def _(i):
        rows = pl.ds(i * 16, 16)
        r.updated[rows] = (r.vid[rows, cols].astype(F32) + O.total(rows)).astype(BF)
    s2[6]()
    s2[7]()
    N.end()

    def video_hat(rows):
        return (r.vid[rows, cols].astype(F32) - r.mu[rows]) * r.inv[rows]

    @pl.loop(0, 16)
    def _(i):
        rows = pl.ds(i * 16, 16)
        t = N.total(rows)
        r.scol[0, rows] = jnp.sum(t, axis=1, keepdims=True)
        r.scol[1, rows] = jnp.sum(t * video_hat(rows), axis=1, keepdims=True)
    for k in range(2):
        r.stat[g, k] = jnp.broadcast_to(r.scol[k], (256, 128)).T[:8]
    grp = [{"grp": (g + j) % 4, "fsdp": f} for j in range(1, 4)]
    for j in range(1, 4):
        L.send(r.stat.at[g], r.stat.at[g], ("st", j), grp[j - 1])
    for i in (8, 9, 10):
        s2[i]()
    r.ograd[...] = S1.result()
    for j in range(1, 4):
        L.recv(r.stat.at[(g + 4 - j) % 4], ("st", j), grp[3 - j])
    for k in range(2):
        s = r.stat[0, k, :1] + r.stat[1, k, :1] + r.stat[2, k, :1] + r.stat[3, k, :1]
        r.scol[k] = jnp.broadcast_to(s / 3072, (128, 256)).T[:, :1]

    @pl.loop(0, 16)
    def _(i):
        rows = pl.ds(i * 16, 16)
        d = N.total(rows) - r.scol[0, rows] - video_hat(rows) * r.scol[1, rows]
        r.igrad[rows] = (r.grad[rows, cols].astype(F32) + r.inv[rows] * d).astype(BF)
    wait_bytes(r.KV.at[pl.ds(0, 31)], r.asem.at[6], r.asem.at[7], partner)
    r.kgrad[...] = r.KV[...].reshape(16, 2, 8, 384)[:, 0].astype(F32).reshape(128, 384).astype(BF)
    r.vgrad[...] = r.KV[...].reshape(16, 2, 8, 384)[:, 1].astype(F32).reshape(128, 384).astype(BF)
    r.qgrad[...] = S2.result()
    S1.sent()
    S2.sent()
    L.drain()


def hand_over(*refs):
    copies = [pltpu.make_async_copy(refs[i], refs[6 + i], refs[12].at[i]) for i in range(6)]
    for c in copies:
        c.start()
    for c in copies:
        c.wait()


def local(caption_states, caption_lens, text_gain, text_query, text_key, text_value, text_bias, text_out, final_gain, cross_key, cross_value, video_states, video_counts, sample_caption, cross_query, cross_out, out_grad):
    V, M, A = pltpu.VMEM, pltpu.SMEM, pl.ANY

    def call(kernel, name, cid, args, spaces, outs, tables, scratch, smem):
        return pl.pallas_call(
            kernel,
            out_shape=tuple(jax.ShapeDtypeStruct(s, d) for s, d in outs.values()) + tuple(jax.ShapeDtypeStruct((n,), jnp.int32) for n in tables),
            in_specs=[pl.BlockSpec(memory_space=s) for s in spaces],
            out_specs=tuple(pl.BlockSpec(memory_space=V) for _ in outs) + tuple(pl.BlockSpec(memory_space=M) for _ in tables),
            scratch_shapes=[V(s, d) for s, d in scratch.values()] + [M((n,), jnp.int32) for n in smem] + [DMA((128,)), DMA((24,)), DMA((8,))],
            compiler_params=pltpu.CompilerParams(collective_id=cid, has_side_effects=True, vmem_limit_bytes=58 << 20),
            name=name,
        )(*args)
    args = [caption_lens, video_counts, sample_caption, text_gain[None], final_gain[None], caption_states.reshape(128, 4096), text_query, text_key, text_value, text_bias, text_out, video_states, out_grad, cross_key, cross_value, cross_query, cross_out.T]
    qb, da, ks, gq, vnT, gradT, mu, inv, edge, sidx = call(encode, "encode", 0, args, [M] * 3 + [V] * 2 + [A] * 12, P_OUT, (8, 160), P_SCRATCH, P_TABLES.values())
    args = [edge, sidx, qb, da, ks, mu, inv, gq, vnT, gradT, video_states, out_grad]
    outs = call(attend, "attend", 1, args, [M] * 2 + [V] * 5 + [A] * 5, Q_OUT, (), Q_SCRATCH, ())
    updated, igrad, qgrad, ograd, kgrad, vgrad = pl.pallas_call(
        hand_over,
        out_shape=tuple(jax.ShapeDtypeStruct(s, d) for s, d in Q_OUT.values()),
        in_specs=[pl.BlockSpec(memory_space=A)] * 6,
        out_specs=(pl.BlockSpec(memory_space=A),) * 6,
        scratch_shapes=[DMA((6,))],
        name="hand_over",
    )(*outs)
    return updated, igrad, qgrad, ograd.T, kgrad[None], vgrad[None]


def solution(mesh):
    in_specs = (P("fsdp"), P(), P(), P(None, "grp"), P(None, "grp"), P(None, "grp"), P("grp"), P("grp"), P(), P("fsdp", "grp"), P("fsdp", "grp"), P("fsdp"), P(), P(), P("fsdp", "grp"), P("grp", "fsdp"), P("fsdp"))
    out_specs = (P("fsdp", "grp"), P("fsdp", "grp"), P("fsdp", "grp"), P("grp", "fsdp"), P("fsdp", None, "grp"), P("fsdp", None, "grp"))
    return jax.shard_map(local, mesh=mesh, in_specs=in_specs, out_specs=out_specs, check_vma=False)
```

```python
import math

import jax
import jax.numpy as jnp
from jax import lax
from jax.experimental import pallas as pl
from jax.experimental.pallas import tpu as pltpu
from jax.sharding import PartitionSpec as P
MESH = pl.DeviceIdType.MESH
BF, F32 = jnp.bfloat16, jnp.float32
DMA = pltpu.SemaphoreType.DMA
HEAD_SIZE = 128

class Links:
    def __init__(self, sems):
        self.sems, self.keys, self.pending = sems, {}, []
    def sem(self, key):
        return self.sems.at[self.keys.setdefault(key, len(self.keys))]
    def copy(self, src, dst, key, dev, group=None):
        send = self.sem(("s", group if group else key))
        return pltpu.make_async_remote_copy(src_ref=src, dst_ref=dst, send_sem=send, recv_sem=self.sem(("r", key)), device_id=dev, device_id_type=MESH)
    def send(self, src, dst, key, dev, group=None):
        c = self.copy(src, dst, key, dev, group)
        c.start()
        if group is None:
            self.pending.append(c)
    def recv(self, dst, key, dev, group=None):
        self.copy(dst, dst, key, dev, group).wait_recv()
    def sent(self, blocks, group, key, dev):
        self.copy(blocks, blocks, key, dev, group).wait_send()
    def drain(self):
        for c in self.pending:
            c.wait_send()
        self.pending = []

def place():
    g, f = lax.axis_index("grp"), lax.axis_index("fsdp")
    return dict(hi=g // 2, core=g % 2, y=f // 8, z=(f // 2) % 4, x=f % 2, g=g, f=f)

def dev(hi, core, y, z, x):
    return {"grp": hi * 2 + core, "fsdp": (y * 4 + z) * 2 + x}

class Gather:
    def __init__(self, L, me, name, G, rows):
        self.L, self.me, self.name, self.G, self.rows = L, me, name, G, rows
    def nb(self, part, first, d):
        m = self.me
        use_z = (m["x"] == 0) if (part == 0) == first else (m["x"] == 1)
        zi = jnp.where(use_z, (m["z"] + d) % 4, m["z"])
        yi = jnp.where(use_z, m["y"], (m["y"] + d) % 4)
        return {"fsdp": (yi * 4 + zi) * 2 + m["x"], "grp": m["g"]}
    def idx(self, part, d1, d2):
        m = self.me
        use_z = (m["x"] == 0) if part == 0 else (m["x"] == 1)
        dz = jnp.where(use_z, d1, d2)
        dy = jnp.where(use_z, d2, d1)
        px = m["x"] if part == 0 else 1 - m["x"]
        return (((m["y"] + dy) % 4) * 4 + (m["z"] + dz) % 4) * 2 + px
    def ref(self, part, d1, d2, half=None):
        b = self.G.at[self.idx(part, d1, d2)]
        if half is None:
            return b
        h = self.rows // 2
        return b.at[pl.ds(half * h, h)]
    def xsend(self, src):
        m = self.me
        self.L.send(src, self.G.at[m["f"]], (self.name, "x"), {"grp": m["g"], "fsdp": m["f"] + 1 - 2 * m["x"]}, self.name)
    def xrecv(self):
        m = self.me
        self.L.recv(self.ref(1, 0, 0), (self.name, "x"), {"grp": m["g"], "fsdp": m["f"] + 1 - 2 * m["x"]}, self.name)
    def s1(self, part, first, k, src=None):
        d = (0, 0) if first else (k, 0)
        r = self.ref(part, *d)
        src = r if src is None else src
        for s in (1, 3):
            self.L.send(src, r, (self.name, part, first, k, "s1", s), self.nb(part, first, s), self.name)
    def s2(self, part, first, k, s):
        o = 4 - s
        d = (o, 0) if first else (k, o)
        self.L.recv(self.ref(part, *d), (self.name, part, first, k, "s1", s), self.nb(part, first, o), self.name)
        half = 0 if s == 1 else 1
        r = self.ref(part, *d, half)
        self.L.send(r, r, (self.name, part, first, k, "s2", s), self.nb(part, first, s), self.name)
    def s3(self, part, first, k):
        d = (2, 0) if first else (k, 2)
        for s in (1, 3):
            half = 0 if s == 1 else 1
            self.L.recv(self.ref(part, *d, half), (self.name, part, first, k, "s2", s), self.nb(part, first, 4 - s), self.name)
    def stages(self, own):
        def a():
            self.s1(0, True, 0, own)
            self.s1(0, False, 0, own)
        def b():
            self.xrecv()
            self.s1(1, True, 0)
            self.s1(1, False, 0)
        def c():
            for part in (0, 1):
                self.s2(part, True, 0, 1)
                self.s2(part, True, 0, 3)
        def d():
            for k in (1, 3):
                self.s1(0, False, k); self.s1(1, False, k)
        def e():
            self.s3(0, True, 0); self.s1(0, False, 2)
            self.s3(1, True, 0); self.s1(1, False, 2)
        def fw(k):
            def f():
                for part in (0, 1):
                    self.s2(part, False, k, 1); self.s2(part, False, k, 3)
            return f
        def fin(k):
            def f():
                for part in (0, 1):
                    self.s3(part, False, k)
            return f
        return [a, b, c, d, e, fw(0), fw(1), fin(0), fw(3), fin(1), fw(2), fin(3), fin(2)]
    def sent(self):
        m = self.me
        self.L.sent(self.G.at[pl.ds(0, 31)], self.name, (self.name, "x"), {"grp": m["g"], "fsdp": m["f"] + 1 - 2 * m["x"]})

def barrier(me, devs):
    b = pltpu.get_barrier_semaphore()
    for d in devs:
        pl.semaphore_signal(b, inc=1, device_id=d, device_id_type=MESH)
    pl.semaphore_wait(b, len(devs))

def neighbours(me):
    m = me
    out = [{"grp": m["g"], "fsdp": m["f"] + 1 - 2 * m["x"]}]
    for d in (1, 3):
        out.append({"grp": m["g"], "fsdp": (m["y"] * 4 + (m["z"] + d) % 4) * 2 + m["x"]})
        out.append({"grp": m["g"], "fsdp": (((m["y"] + d) % 4) * 4 + m["z"]) * 2 + m["x"]})
    return out


class TwoStep:
    def __init__(self, L, me, name, parts, r0, r1, s1, r2):
        self.L, self.me, self.name = L, me, name
        self.parts, self.r, self.s1, self.r2 = parts, (r0, r1), s1, r2
        self.sib = {"grp": me["g"] + 1 - 2 * me["core"], "fsdp": me["f"]}
        self.opp = {"grp": (1 - me["hi"]) * 2 + me["core"], "fsdp": me["f"]}
    def order(self):
        hi, core = self.me["hi"], self.me["core"]
        return [2 * (1 - hi) + 1 - core, 2 * hi + 1 - core, 2 * (1 - hi) + core, 2 * hi + core]
    def start(self, j):
        self.L.send(self.parts.at[self.order()[j]], self.r[j], (self.name, "c", j), self.sib)
    def mid(self):
        m = self.me
        self.L.recv(self.r[0], (self.name, "c", 0), self.sib)
        for i in range(self.s1.shape[0] // 32):
            rows = pl.ds(i * 32, 32)
            self.s1[rows] = (self.parts[2 * (1 - m["hi"]) + m["core"], rows].astype(F32) + self.r[0][rows].astype(F32)).astype(BF)
        self.L.send(self.s1, self.r2, (self.name, "o"), self.opp)
    def end(self):
        self.L.recv(self.r[1], (self.name, "c", 1), self.sib)
        self.L.recv(self.r2, (self.name, "o"), self.opp)
    def total(self, rows):
        m = self.me
        return self.parts[2 * m["hi"] + m["core"], rows].astype(F32) + self.r[1][rows].astype(F32) + self.r2[rows].astype(F32)


def along_x(me, d):
    X = (me["hi"] * 2 + me["x"] + d) % 4
    return X // 2, X % 2


def same_core(me, d):
    hi, x = along_x(me, d)
    return dev(hi, me["core"], me["y"], me["z"], x)


class Eight:
    def __init__(self, L, me, name, E, rows):
        self.L, self.me, self.name, self.E, self.rows = L, me, name, E, rows
        self.sib = {"grp": me["g"] + 1 - 2 * me["core"], "fsdp": me["f"]}
    def ref(self, d, core, half=None):
        hi, x = along_x(self.me, d)
        r = self.E.at[x, hi * 2 + core]
        if half is None:
            return r
        h = self.rows // 2
        return r.at[pl.ds(half * h, h)]
    def start(self):
        r = self.ref(0, self.me["core"])
        for s in (1, 3):
            self.L.send(r, r, (self.name, "s1", s), same_core(self.me, s))
        self.L.send(r, r, (self.name, "sib", 0), self.sib)
    def mid(self):
        c = self.me["core"]
        for s in (1, 3):
            r = self.ref(4 - s, c)
            self.L.recv(r, (self.name, "s1", s), same_core(self.me, s))
            half = 0 if s == 1 else 1
            rh = self.ref(4 - s, c, half)
            self.L.send(rh, rh, (self.name, "s2", s), same_core(self.me, s))
            self.L.send(r, r, (self.name, "sib", 4 - s), self.sib)
    def mid2(self):
        c = self.me["core"]
        for s in (1, 3):
            half = 0 if s == 1 else 1
            rh = self.ref(2, c, half)
            self.L.recv(rh, (self.name, "s2", s), same_core(self.me, s))
            self.L.send(rh, rh, (self.name, "sib2", s), self.sib)
    def end(self):
        oc = 1 - self.me["core"]
        for d in (0, 1, 3):
            self.L.recv(self.ref(d, oc), (self.name, "sib", d), self.sib)
        for s in (1, 3):
            self.L.recv(self.ref(2, oc, 0 if s == 1 else 1), (self.name, "sib2", s), self.sib)


def eight_others(me):
    out = []
    for d in range(4):
        hi, x = along_x(me, d)
        for c in (0, 1):
            if d == 0 and c == 0:
                continue
            core = 1 - me["core"] if c == 1 else me["core"]
            out.append(((d, c), dev(hi, core, me["y"], me["z"], x), (x, hi * 2 + core)))
    return out


class Scatter:
    def __init__(self, L, me, name, D, ra, rb, rx):
        self.L, self.me, self.name, self.D, self.ra, self.rb, self.rx = L, me, name, D, ra, rb, rx
        self.rows = D.shape[1]
    def axis(self, part, stage):
        m = self.me
        own = m["x"] == 0 if part == 0 else m["x"] == 1
        return own if stage == 1 else jnp.logical_not(own)
    def nb(self, part, stage, d):
        m = self.me
        use_z = self.axis(part, stage)
        zi = jnp.where(use_z, (m["z"] + d) % 4, m["z"])
        yi = jnp.where(use_z, m["y"], (m["y"] + d) % 4)
        return {"fsdp": (yi * 4 + zi) * 2 + m["x"], "grp": m["g"]}
    def ref(self, part, stage, k, d, half=None):
        m = self.me
        use_z = self.axis(part, stage)
        dz = jnp.where(use_z, d, k)
        dy = jnp.where(use_z, k, d)
        px = m["x"] if part == 0 else 1 - m["x"]
        b = self.D.at[(((m["y"] + dy) % 4) * 4 + (m["z"] + dz) % 4) * 2 + px]
        if half is None:
            return b
        h = self.rows // 2
        return b.at[pl.ds(half * h, h)]
    def slot(self, stage, k):
        return k if stage == 0 else 4
    def far(self, part, stage, k):
        h = self.rows // 2
        for s in (1, 3):
            half = 0 if s == 1 else 1
            self.L.send(self.ref(part, stage, k, 2, half), self.ra.at[part, self.slot(stage, k), half], (self.name, part, stage, k, "far", s), self.nb(part, stage, s), self.name)
    def near(self, part, stage, k):
        h = self.rows // 2
        for s in (1, 3):
            half = 0 if s == 1 else 1
            buf = self.ra.at[part, self.slot(stage, k), half]
            self.L.recv(buf, (self.name, part, stage, k, "far", s), self.nb(part, stage, 4 - s), self.name)
            r = self.ref(part, stage, k, s, half)
            r[...] = (r[...].astype(F32) + buf[...].astype(F32)).astype(BF)
            self.L.send(self.ref(part, stage, k, s), self.rb.at[part, self.slot(stage, k), half], (self.name, part, stage, k, "near", s), self.nb(part, stage, s), self.name)
    def total(self, part, stage, k):
        for s in (1, 3):
            half = 0 if s == 1 else 1
            self.L.recv(self.rb.at[part, self.slot(stage, k), half], (self.name, part, stage, k, "near", s), self.nb(part, stage, 4 - s), self.name)
        b = self.rb.at[part, self.slot(stage, k)]
        return self.ref(part, stage, k, 0)[...].astype(F32) + b[0].astype(F32) + b[1].astype(F32)
    def fold(self, part, stage, k):
        t = self.total(part, stage, k)
        self.ref(part, stage, k, 0)[...] = t.astype(BF)
    def partner(self):
        m = self.me
        return {"grp": m["g"], "fsdp": m["f"] + 1 - 2 * m["x"]}
    def xsend(self):
        self.fold(1, 1, 0)
        self.L.send(self.ref(1, 1, 0, 0), self.rx, (self.name, "x"), self.partner(), self.name)
    def result(self):
        t = self.total(0, 1, 0)
        self.L.recv(self.rx, (self.name, "x"), self.partner(), self.name)
        return t + self.rx[...].astype(F32)
    def stages(self):
        def a():
            for k in (2, 1, 3, 0):
                for part in (1, 0):
                    self.far(part, 0, k)
        def b(k):
            def f():
                for part in (1, 0):
                    self.near(part, 0, k)
            return f
        def c(k):
            def f():
                for part in (1, 0):
                    self.fold(part, 0, k)
                    if k == 2:
                        self.far(part, 1, 0)
            return f
        def d():
            for part in (1, 0):
                self.near(part, 1, 0)
        return [a, b(2), b(1), c(2), b(3), c(1), b(0), c(3), d, c(0), self.xsend]
    def sent(self):
        self.L.sent(self.D.at[pl.ds(0, 31)], self.name, (self.name, "x"), self.partner())


def wait_bytes(like, send_sem, recv_sem, devid, recv=True, send=True):
    c = pltpu.make_async_remote_copy(src_ref=like, dst_ref=like, send_sem=send_sem, recv_sem=recv_sem, device_id=devid, device_id_type=MESH)
    if recv:
        c.wait_recv()
    if send:
        c.wait_send()


def dot(a, b, ca, cb):
    return lax.dot_general(a, b, (((ca,), (cb,)), ((), ())), preferred_element_type=F32)


class Refs:
    pass


P_IN = ["lens", "counts", "scap", "tgain", "fgain", "cs_h", "tq_h", "tk_h", "tv_h", "bias_h", "tout_h", "vid_h", "grad_h", "ck_h", "cv_h", "cq_h", "co_h"]
P_OUT = {
    "qb": ((256, 384), BF),
    "da": ((256, 384), BF),
    "ks": ((2, 384, 384), BF),
    "mu": ((256, 1), F32),
    "inv": ((256, 1), F32),
}
P_FAR = {
    "gq": ((32, 192, 384), BF),
    "vnT": ((3072, 256), BF),
    "gradT": ((3072, 256), BF),
}
P_SCRATCH = {
    "kv": ((2, 128, 384), BF),
    "qo": ((192, 384), BF),
    "cs": ((128, 4096), BF),
    "normed": ((128, 4096), BF),
    "wt": ((2, 4096, 512), BF),
    "bias": ((8, 128, 128), F32),
    "tqkv": ((3, 128, 512), BF),
    "tm": ((128, 512), BF),
    "vid": ((256, 3072), BF),
    "grad": ((256, 3072), BF),
    "vn": ((256, 3072), BF),
    "gw": ((32, 128, 384), BF),
    "parts": ((4, 128, 1024), BF),
    "t0": ((128, 1024), BF),
    "t1": ((128, 1024), BF),
    "t2": ((128, 1024), BF),
    "t3": ((128, 1024), BF),
    "E": ((2, 4, 128, 1024), BF),
    "sscol": ((128, 1), F32),
    "SS": ((2, 4, 8, 128), F32),
    "kvp": ((16, 2, 8, 384), BF),
    "C": ((32, 8, 384), BF),
    "sb": ((32, 3, 8, 384), BF),
    "R": ((32, 3, 8, 384), BF),
}
P_TABLES = {"end": 32, "first": 32, "cap": 96, "samp": 32}
Q_IN = ["edge", "sidx", "qb", "da", "ks", "mu", "inv", "gq_h", "vnT_h", "gradT_h", "vid_h", "grad_h"]
Q_OUT = {
    "updated": ((256, 768), BF),
    "igrad": ((256, 768), BF),
    "qgrad": ((96, 384), F32),
    "ograd": ((96, 384), F32),
    "kgrad": ((128, 384), BF),
    "vgrad": ((128, 384), BF),
}
Q_SCRATCH = {
    "gq": ((32, 192, 384), BF),
    "vnT": ((3072, 256), BF),
    "gradT": ((3072, 256), BF),
    "vid": ((256, 3072), BF),
    "grad": ((256, 3072), BF),
    "att": ((256, 384), BF),
    "dq": ((256, 384), BF),
    "w": ((3, 256, 128), F32),
    "mp": ((3, 256, 384), BF),
    "ms": ((3, 256, 384), BF),
    "T": ((32, 3, 8, 384), BF),
    "Dw": ((32, 96, 384), BF),
    "Dq": ((32, 96, 384), BF),
    "ra1": ((2, 5, 2, 48, 384), BF),
    "rb1": ((2, 5, 2, 96, 384), BF),
    "rx1": ((96, 384), BF),
    "ra2": ((2, 5, 2, 48, 384), BF),
    "rb2": ((2, 5, 2, 96, 384), BF),
    "rx2": ((96, 384), BF),
    "op": ((4, 256, 768), BF),
    "o0": ((256, 768), BF),
    "o1": ((256, 768), BF),
    "o2": ((256, 768), BF),
    "o3": ((256, 768), BF),
    "dn": ((4, 256, 768), BF),
    "n0": ((256, 768), BF),
    "n1": ((256, 768), BF),
    "n2": ((256, 768), BF),
    "n3": ((256, 768), BF),
    "scol": ((2, 256, 1), F32),
    "stat": ((4, 2, 8, 256), F32),
    "RG": ((99, 8, 384), BF),
    "CG": ((32, 8, 384), BF),
    "KV": ((32, 8, 384), BF),
}


def fill_tables(r):
    def total(s, acc):
        acc = acc + r.counts[s]
        r.end[s] = acc
        return acc
    lax.fori_loop(0, 32, total, jnp.int32(0))

    @pl.loop(0, 32)
    def _(d):
        count = jnp.int32(0)
        for s in range(32):
            count = count + (r.end[s] <= 256 * d).astype(jnp.int32)
        r.first[d] = count
        for t in range(3):
            r.cap[d * 3 + t] = r.scap[jnp.minimum(count + t, 31)]

    @pl.loop(0, 32)
    def _(c):
        s = jnp.int32(0)
        for t in range(32):
            s = s + jnp.where(r.scap[t] == c, t, 0)
        s = jnp.minimum(s, 31)
        stop = r.end[s]
        d0 = (stop - r.counts[s]) // 256
        for m in range(5):
            d = d0 + m
            valid = (d < 32) & (d * 256 < stop)
            r.sidx[c * 5 + m] = jnp.clip(jnp.where(valid, 3 * d + s - r.first[jnp.minimum(d, 31)], 96), 0, 96)


def named(refs, names):
    r = Refs()
    for n, ref in zip(names, refs):
        setattr(r, n, ref)
    return r


def encode(*refs):
    r = named(refs, P_IN + list(P_OUT) + [n + "_o" for n in P_FAR] + ["edge", "sidx"] + list(P_FAR) + list(P_SCRATCH) + list(P_TABLES) + ["sems", "lsem", "asem"])
    me = place()
    f, g, core, hi = me["f"], me["g"], me["core"], me["hi"]
    L = Links(r.sems)
    loads = {}

    def load(name, src, dst):
        c = pltpu.make_async_copy(src, dst, r.lsem.at[len(loads)])
        c.start()
        loads[name] = c
    load("ck", r.ck_h, r.kv.at[0])
    load("cv", r.cv_h, r.kv.at[1])
    load("cq", r.cq_h, r.qo.at[pl.ds(0, 96)])
    load("co", r.co_h, r.qo.at[pl.ds(96, 96)])
    load("cs", r.cs_h, r.cs)

    def load_text(a, wh):
        for k in range(2):
            rows = pl.ds(k * 2048, 2048)
            load(("wt", a, k), wh.at[rows], r.wt.at[a % 2, rows])
    load_text(0, r.tq_h)
    load_text(1, r.tk_h)
    load("bias", r.bias_h, r.bias)
    load("vid", r.vid_h, r.vid)
    load("grad", r.grad_h, r.grad)

    others = eight_others(me)
    fs = [{"grp": g, "fsdp": (f + j) % 32} for j in range(1, 32)]
    barrier(me, fs + [{"grp": (g + j) % 4, "fsdp": f // 2 * 2 + x} for j in range(1, 4) for x in range(2)])

    A, B = Gather(L, me, "w", r.gw, 128), Gather(L, me, "q", r.gq, 192)
    sa, sb = A.stages(r.kv.at[me["x"]]), B.stages(r.qo)
    for n in ("ck", "cv", "cq", "co"):
        loads[n].wait()
    A.xsend(r.kv.at[1 - me["x"]])
    sa[0]()
    B.xsend(r.qo)
    sb[0]()
    r.gw[f] = r.kv[me["x"]]
    r.gq[f] = r.qo[...]

    loads["cs"].wait()

    @pl.loop(0, 8)
    def _(i):
        rows = pl.ds(i * 16, 16)
        x = r.cs[rows].astype(F32)
        mean_square = jnp.mean(x * x, axis=-1, keepdims=True)
        r.normed[rows] = (x * lax.rsqrt(mean_square + 1e-06) * r.tgain[...]).astype(BF)

    def project(a):
        acc = jnp.zeros((128, 512), F32)
        for k in range(2):
            loads["wt", a, k].wait()
            acc = acc + jnp.dot(r.normed[:, pl.ds(k * 2048, 2048)], r.wt[a % 2, pl.ds(k * 2048, 2048)], preferred_element_type=F32)
        r.tqkv[a] = acc.astype(BF)
    project(0)
    load_text(2, r.tv_h)
    sa[1]()
    project(1)
    for k in range(8):
        load(("wo", k), r.tout_h.at[:, pl.ds(k * 512, 512)], r.wt.at[1, pl.ds(k * 512, 512)])
    sb[1]()
    project(2)
    sa[2]()
    sa[3]()
    loads["bias"].wait()
    lane = lax.broadcasted_iota(jnp.int32, (128, 128), 1)
    valid = lane < r.lens[f]

    def text_pair(p):
        cols = pl.ds(p * 128, 128)
        q, k, v = r.tqkv[0, :, cols], r.tqkv[1, :, cols], r.tqkv[2, :, cols]
        out = []
        for i in range(2):
            qh = jnp.where((lane < 64) == (i == 0), q.astype(F32), 0.0).astype(BF)
            ex = jnp.where(valid, jnp.exp(dot(qh, k, 1, 1) + r.bias[2 * p + i]), 0.0)
            wts = (ex / jnp.sum(ex, axis=-1, keepdims=True)).astype(BF)
            out.append(dot(wts, v, 1, 0))
        r.tm[:, cols] = jnp.where(lane < 64, out[0], out[1]).astype(BF)
    text_pair(0)
    text_pair(1)
    sb[2]()
    sb[3]()
    text_pair(2)
    text_pair(3)
    sa[4]()
    sa[5]()
    for k in range(8):
        loads["wo", k].wait()
    T = TwoStep(L, me, "t", r.parts, r.t0, r.t1, r.t2, r.t3)
    for j, s in enumerate(T.order()):
        for n in range(2):
            cols = pl.ds(n * 512, 512)
            r.parts[s, :, cols] = jnp.dot(r.tm[...], r.wt[1, pl.ds((2 * s + n) * 512, 512)], preferred_element_type=F32).astype(BF)
        if j < 2:
            T.start(j)
    sb[4]()
    sb[5]()
    T.mid()
    fill_tables(r)
    sa[6]()
    sb[6]()
    T.end()

    @pl.loop(0, 8)
    def _(i):
        rows, cols = pl.ds(i * 16, 16), pl.ds(pl.multiple_of(g * 1024, 1024), 1024)
        ts = T.total(rows) + r.cs[rows, cols].astype(F32)
        r.E[me["x"], g, rows] = (ts * r.fgain[:, cols]).astype(BF)
        r.sscol[rows] = jnp.sum(ts * ts, axis=1, keepdims=True)
    X = Eight(L, me, "e", r.E, 128)
    X.start()
    r.SS[me["x"], g] = jnp.broadcast_to(r.sscol[...], (128, 128)).T[:8]
    mine = r.SS.at[me["x"], g]
    for key, d, _ in others:
        L.send(mine, mine, ("ss", (4 - key[0]) % 4, key[1]), d)
    sa[7]()
    sa[8]()

    loads["vid"].wait()

    @pl.loop(0, 16)
    def _(i):
        rows = pl.ds(i * 16, 16)
        v = r.vid[rows].astype(F32)
        mean = jnp.mean(v, axis=-1, keepdims=True)
        center = v - mean
        inverse = lax.rsqrt(jnp.mean(center * center, axis=-1, keepdims=True) + 1e-06)
        r.mu[rows], r.inv[rows] = mean, inverse
        r.vn[rows] = (center * inverse).astype(BF)
    X.mid()
    sb[7]()
    sb[8]()
    loads["grad"].wait()

    @pl.loop(0, 24)
    def _(i):
        lanes = pl.ds(pl.multiple_of(i * 128, 128), 128)
        r.vnT[lanes] = r.vn[:, lanes].T
        r.gradT[lanes] = r.grad[:, lanes].T
    load("vnT_o", r.vnT, r.vnT_o)
    load("gradT_o", r.gradT, r.gradT_o)
    X.mid2()
    for i in range(9, 13):
        sa[i]()
    sb[9]()
    sb[10]()
    X.end()
    for key, d, slot in others:
        L.recv(r.SS.at[slot[0], slot[1]], ("ss", key[0], key[1]), d)

    acc = jnp.zeros((256, 384), F32)
    for k in range(4):
        acc = acc + jnp.dot(r.E[:, k].reshape(256, 1024), r.gw[k * 8 : k * 8 + 8].reshape(1024, 384), preferred_element_type=F32)
    for c in range(2):
        ss = r.SS[c, 0, :1] + r.SS[c, 1, :1] + r.SS[c, 2, :1] + r.SS[c, 3, :1]
        col = jnp.broadcast_to(ss, (128, 128)).T[:, :1]
        r.kvp[:, c] = (acc[c * 128 : c * 128 + 128] * lax.rsqrt(col / 4096 + 1e-06)).reshape(16, 8, 384).astype(BF)

    partner = {"grp": g, "fsdp": (f + 1) % 32}
    yz = f // 2

    @pl.loop(1, 16)
    def _(j):
        to = (yz + j) % 16
        pltpu.make_async_remote_copy(src_ref=r.kvp.at[to], dst_ref=r.C.at[pl.ds(2 * yz, 2)], send_sem=r.asem.at[0], recv_sem=r.asem.at[1], device_id={"grp": g, "fsdp": to * 2 + me["x"]}, device_id_type=MESH).start()
    r.C[pl.ds(2 * yz, 2)] = r.kvp[yz]
    wait_bytes(r.C.at[pl.ds(0, 30)], r.asem.at[0], r.asem.at[1], partner)

    @pl.loop(1, 32)
    def _(j):
        to = (f + j) % 32
        for s in range(3):
            r.sb[to, s] = r.C[r.cap[to * 3 + s]]
        pltpu.make_async_remote_copy(src_ref=r.sb.at[to], dst_ref=r.R.at[f], send_sem=r.asem.at[2], recv_sem=r.asem.at[3], device_id={"grp": g, "fsdp": to}, device_id_type=MESH).start()
    for s in range(3):
        r.R[f, s] = r.C[r.cap[f * 3 + s]]
    for s in sb[11:]:
        s()
    load("gq_o", r.gq, r.gq_o)

    acc = jnp.zeros((256, 384), F32)
    acc2 = jnp.zeros((256, 384), F32)
    for k in range(4):
        cols = pl.ds(k * 768, 768)
        acc = acc + jnp.dot(r.vn[:, cols], r.gq[k * 8 : k * 8 + 8, 0:96].reshape(768, 384), preferred_element_type=F32)
    r.qb[...] = acc.astype(BF)
    for k in range(4):
        cols = pl.ds(k * 768, 768)
        acc2 = acc2 + jnp.dot(r.grad[:, cols], r.gq[k * 8 : k * 8 + 8, 96:192].reshape(768, 384), preferred_element_type=F32)
    r.da[...] = acc2.astype(BF)

    first = r.first[f]
    r.edge[0], r.edge[1] = r.end[jnp.minimum(first, 31)], r.end[jnp.minimum(first + 1, 31)]
    for s in range(3):
        r.edge[2 + s] = r.lens[r.cap[f * 3 + s]]
    wait_bytes(r.R.at[pl.ds(0, 31)], r.asem.at[2], r.asem.at[3], partner)
    for kv in range(2):
        for s in range(3):
            r.ks[kv, pl.ds(s * 128, 128)] = r.R[:, s].reshape(16, 2, 8, 384)[:, kv].astype(F32).reshape(128, 384).astype(BF)
    A.sent()
    B.sent()
    L.drain()
    for n in P_FAR:
        loads[n + "_o"].wait()


def attend(*refs):
    r = named(refs, Q_IN + list(Q_OUT) + list(Q_SCRATCH) + ["sems", "lsem", "asem"])
    me = place()
    f, g, core, hi = me["f"], me["g"], me["core"], me["hi"]
    L = Links(r.sems)
    partner = {"grp": g, "fsdp": (f + 1) % 32}
    loads = {}
    for i, n in enumerate(("gradT", "gq", "vnT", "vid", "grad")):
        loads[n] = pltpu.make_async_copy(getattr(r, n + "_h"), getattr(r, n), r.lsem.at[i])
        loads[n].start()
    barrier(me, [{"grp": g, "fsdp": (f + j) % 32} for j in range(1, 32)] + [{"grp": (g + j) % 4, "fsdp": f} for j in range(1, 4)])
    position = lax.broadcasted_iota(jnp.int32, (256, 128), 0) + f * 256
    slot = (position >= r.edge[0]).astype(jnp.int32) + (position >= r.edge[1]).astype(jnp.int32)
    token_len = jnp.where(slot == 0, r.edge[2], jnp.where(slot == 1, r.edge[3], r.edge[4]))
    token_valid = lax.broadcasted_iota(jnp.int32, (256, 128), 1) < token_len
    scale = 1.0 / math.sqrt(HEAD_SIZE)

    def pick(a):
        return jnp.where(slot == 0, a[:, 0:128], jnp.where(slot == 1, a[:, 128:256], a[:, 256:384]))

    def placed(a):
        return jnp.concatenate([jnp.where(slot == s, a, 0.0).astype(BF) for s in range(3)], axis=1)

    for h in range(3):
        cols = pl.ds(h * 128, 128)
        scores = pick(dot(r.qb[:, cols], r.ks[0, :, cols], 1, 1)) * scale
        ex = jnp.where(token_valid, jnp.exp(scores), 0.0)
        w = ex / jnp.sum(ex, axis=-1, keepdims=True)
        r.w[h] = w
        mp = placed(w)
        r.mp[h] = mp
        r.att[:, cols] = dot(mp, r.ks[1, :, cols], 1, 0).astype(BF)

    def weight_grad(D, left, right):
        @pl.loop(0, 8)
        def _(i):
            rows = pl.ds(i * 384, 384)
            D[pl.ds(i * 4, 4)] = dot(left[rows], right[...], 1, 0).reshape(4, 96, 384).astype(BF)
    loads["gradT"].wait()
    weight_grad(r.Dw, r.gradT, r.att)
    S1 = Scatter(L, me, "d1", r.Dw, r.ra1, r.rb1, r.rx1)
    S2 = Scatter(L, me, "d2", r.Dq, r.ra2, r.rb2, r.rx2)
    s1, s2 = S1.stages(), S2.stages()
    s1[0]()
    loads["gq"].wait()
    O = TwoStep(L, me, "o", r.op, r.o0, r.o1, r.o2, r.o3)
    N = TwoStep(L, me, "n", r.dn, r.n0, r.n1, r.n2, r.n3)
    for j, s in enumerate(O.order()):
        r.op[s] = dot(r.att[...], r.gq[pl.ds(s * 8, 8), 96:192].reshape(768, 384), 1, 1).astype(BF)
        if j < 2:
            O.start(j)
    s1[1]()

    for h in range(3):
        cols = pl.ds(h * 128, 128)
        d_probs = pick(dot(r.da[:, cols], r.ks[1, :, cols], 1, 1))
        w = r.w[h]
        ds = w * (d_probs - jnp.sum(w * d_probs, axis=-1, keepdims=True)) * scale
        ms = placed(ds)
        r.ms[h] = ms
        r.dq[:, cols] = dot(ms, r.ks[0, :, cols], 1, 0).astype(BF)
    O.mid()
    loads["vnT"].wait()
    weight_grad(r.Dq, r.vnT, r.dq)
    s2[0]()
    s1[2]()
    s1[3]()
    for j, s in enumerate(N.order()):
        r.dn[s] = dot(r.dq[...], r.gq[pl.ds(s * 8, 8), 0:96].reshape(768, 384), 1, 1).astype(BF)
        if j < 2:
            N.start(j)
    for h in range(3):
        cols = pl.ds(h * 128, 128)
        kt = dot(r.ms[h], r.qb[:, cols], 0, 0)
        vt = dot(r.mp[h], r.da[:, cols], 0, 0)
        for s in range(3):
            rows = slice(s * 128, s * 128 + 128)
            both = jnp.stack([kt[rows].reshape(16, 8, 128), vt[rows].reshape(16, 8, 128)], axis=1)
            r.T[:, s, :, cols] = both.reshape(32, 8, 128).astype(BF)

    @pl.loop(1, 32)
    def _(j):
        to = (f + j) % 32
        pltpu.make_async_remote_copy(src_ref=r.T.at[to], dst_ref=r.RG.at[pl.ds(3 * f, 3)], send_sem=r.asem.at[4], recv_sem=r.asem.at[5], device_id={"grp": g, "fsdp": to}, device_id_type=MESH).start()
    N.mid()
    for i in range(4, 8):
        s1[i]()
    s2[1]()
    s2[2]()
    s1[8]()
    s2[3]()
    r.RG[pl.ds(96, 3)] = jnp.zeros((3, 8, 384), BF)
    r.RG[pl.ds(3 * f, 3)] = r.T[f]
    wait_bytes(r.RG.at[pl.ds(0, 93)], r.asem.at[4], r.asem.at[5], partner)

    @pl.loop(0, 32)
    def _(c):
        acc = r.RG[r.sidx[c * 5]].astype(F32)
        for m in range(1, 5):
            acc = acc + r.RG[r.sidx[c * 5 + m]].astype(F32)
        r.CG[c] = acc.astype(BF)

    @pl.loop(1, 32)
    def _(j):
        to = (f + j) % 32
        pltpu.make_async_remote_copy(src_ref=r.CG.at[to], dst_ref=r.KV.at[f], send_sem=r.asem.at[6], recv_sem=r.asem.at[7], device_id={"grp": g, "fsdp": to}, device_id_type=MESH).start()
    r.KV[f] = r.CG[f]
    for i in (9, 10):
        s1[i]()
    for i in (4, 5):
        s2[i]()
    O.end()
    loads["vid"].wait()
    loads["grad"].wait()
    cols = pl.ds(pl.multiple_of(g * 768, 768), 768)

    @pl.loop(0, 16)
    def _(i):
        rows = pl.ds(i * 16, 16)
        r.updated[rows] = (r.vid[rows, cols].astype(F32) + O.total(rows)).astype(BF)
    s2[6]()
    s2[7]()
    N.end()

    def video_hat(rows):
        return (r.vid[rows, cols].astype(F32) - r.mu[rows]) * r.inv[rows]

    @pl.loop(0, 16)
    def _(i):
        rows = pl.ds(i * 16, 16)
        t = N.total(rows)
        r.scol[0, rows] = jnp.sum(t, axis=1, keepdims=True)
        r.scol[1, rows] = jnp.sum(t * video_hat(rows), axis=1, keepdims=True)
    for k in range(2):
        r.stat[g, k] = jnp.broadcast_to(r.scol[k], (256, 128)).T[:8]
    grp = [{"grp": (g + j) % 4, "fsdp": f} for j in range(1, 4)]
    for j in range(1, 4):
        L.send(r.stat.at[g], r.stat.at[g], ("st", j), grp[j - 1])
    for i in (8, 9, 10):
        s2[i]()
    r.ograd[...] = S1.result()
    for j in range(1, 4):
        L.recv(r.stat.at[(g + 4 - j) % 4], ("st", j), grp[3 - j])
    for k in range(2):
        s = r.stat[0, k, :1] + r.stat[1, k, :1] + r.stat[2, k, :1] + r.stat[3, k, :1]
        r.scol[k] = jnp.broadcast_to(s / 3072, (128, 256)).T[:, :1]

    @pl.loop(0, 16)
    def _(i):
        rows = pl.ds(i * 16, 16)
        d = N.total(rows) - r.scol[0, rows] - video_hat(rows) * r.scol[1, rows]
        r.igrad[rows] = (r.grad[rows, cols].astype(F32) + r.inv[rows] * d).astype(BF)
    wait_bytes(r.KV.at[pl.ds(0, 31)], r.asem.at[6], r.asem.at[7], partner)
    r.kgrad[...] = r.KV[...].reshape(16, 2, 8, 384)[:, 0].astype(F32).reshape(128, 384).astype(BF)
    r.vgrad[...] = r.KV[...].reshape(16, 2, 8, 384)[:, 1].astype(F32).reshape(128, 384).astype(BF)
    r.qgrad[...] = S2.result()
    S1.sent()
    S2.sent()
    L.drain()


def hand_over(*refs):
    held, sem = refs[12:18], refs[18]
    into = [pltpu.make_async_copy(refs[i], held[i], sem.at[i]) for i in range(6)]
    out = [pltpu.make_async_copy(held[i], refs[6 + i], sem.at[6 + i]) for i in range(6)]
    for c in into:
        c.start()
    for i in range(6):
        into[i].wait()
        out[i].start()
    for c in out:
        c.wait()


def local(caption_states, caption_lens, text_gain, text_query, text_key, text_value, text_bias, text_out, final_gain, cross_key, cross_value, video_states, video_counts, sample_caption, cross_query, cross_out, out_grad):
    V, M, A = pltpu.VMEM, pltpu.SMEM, pl.ANY

    def call(kernel, name, cid, args, spaces, outs, far, tables, scratch, smem):
        return pl.pallas_call(
            kernel,
            out_shape=tuple(jax.ShapeDtypeStruct(s, d) for s, d in (outs | far).values()) + tuple(jax.ShapeDtypeStruct((n,), jnp.int32) for n in tables),
            in_specs=[pl.BlockSpec(memory_space=s) for s in spaces],
            out_specs=tuple(pl.BlockSpec(memory_space=V) for _ in outs) + tuple(pl.BlockSpec(memory_space=A) for _ in far) + tuple(pl.BlockSpec(memory_space=M) for _ in tables),
            scratch_shapes=[V(s, d) for s, d in (far | scratch).values()] + [M((n,), jnp.int32) for n in smem] + [DMA((128,)), DMA((32,)), DMA((8,))],
            compiler_params=pltpu.CompilerParams(collective_id=cid, has_side_effects=True, vmem_limit_bytes=58 << 20),
            name=name,
        )(*args)
    args = [caption_lens, video_counts, sample_caption, text_gain[None], final_gain[None], caption_states.reshape(128, 4096), text_query, text_key, text_value, text_bias, text_out, video_states, out_grad, cross_key, cross_value, cross_query, cross_out.T]
    qb, da, ks, mu, inv, gq, vnT, gradT, edge, sidx = call(encode, "encode", 0, args, [M] * 3 + [V] * 2 + [A] * 12, P_OUT, P_FAR, (8, 160), P_SCRATCH, P_TABLES.values())
    args = [edge, sidx, qb, da, ks, mu, inv, gq, vnT, gradT, video_states, out_grad]
    outs = call(attend, "attend", 1, args, [M] * 2 + [V] * 5 + [A] * 5, Q_OUT, {}, (), Q_SCRATCH, ())
    updated, igrad, qgrad, ograd, kgrad, vgrad = pl.pallas_call(
        hand_over,
        out_shape=tuple(jax.ShapeDtypeStruct(s, d) for s, d in Q_OUT.values()),
        in_specs=[pl.BlockSpec(memory_space=A)] * 6,
        out_specs=(pl.BlockSpec(memory_space=A),) * 6,
        scratch_shapes=[V(s, d) for s, d in Q_OUT.values()] + [DMA((12,))],
        name="hand_over",
    )(*outs)
    return updated, igrad, qgrad, ograd.T, kgrad[None], vgrad[None]


def solution(mesh):
    in_specs = (P("fsdp"), P(), P(), P(None, "grp"), P(None, "grp"), P(None, "grp"), P("grp"), P("grp"), P(), P("fsdp", "grp"), P("fsdp", "grp"), P("fsdp"), P(), P(), P("fsdp", "grp"), P("grp", "fsdp"), P("fsdp"))
    out_specs = (P("fsdp", "grp"), P("fsdp", "grp"), P("fsdp", "grp"), P("grp", "fsdp"), P("fsdp", None, "grp"), P("fsdp", None, "grp"))
    return jax.shard_map(local, mesh=mesh, in_specs=in_specs, out_specs=out_specs, check_vma=False)
```

```python
import math

import jax
import jax.numpy as jnp
from jax import lax
from jax.experimental import pallas as pl
from jax.experimental.pallas import tpu as pltpu
from jax.sharding import PartitionSpec as P
MESH = pl.DeviceIdType.MESH
BF, F32 = jnp.bfloat16, jnp.float32
DMA = pltpu.SemaphoreType.DMA
HEAD_SIZE = 128

class Links:
    def __init__(self, sems):
        self.sems, self.keys, self.pending = sems, {}, []
    def sem(self, key):
        return self.sems.at[self.keys.setdefault(key, len(self.keys))]
    def copy(self, src, dst, key, dev, group=None):
        send = self.sem(("s", group if group else key))
        return pltpu.make_async_remote_copy(src_ref=src, dst_ref=dst, send_sem=send, recv_sem=self.sem(("r", key)), device_id=dev, device_id_type=MESH)
    def send(self, src, dst, key, dev, group=None):
        c = self.copy(src, dst, key, dev, group)
        c.start()
        if group is None:
            self.pending.append(c)
    def recv(self, dst, key, dev, group=None):
        self.copy(dst, dst, key, dev, group).wait_recv()
    def sent(self, blocks, group, key, dev):
        self.copy(blocks, blocks, key, dev, group).wait_send()
    def drain(self):
        for c in self.pending:
            c.wait_send()
        self.pending = []

def place():
    g, f = lax.axis_index("grp"), lax.axis_index("fsdp")
    return dict(hi=g // 2, core=g % 2, y=f // 8, z=(f // 2) % 4, x=f % 2, g=g, f=f)

def dev(hi, core, y, z, x):
    return {"grp": hi * 2 + core, "fsdp": (y * 4 + z) * 2 + x}

class Gather:
    def __init__(self, L, me, name, G, rows):
        self.L, self.me, self.name, self.G, self.rows = L, me, name, G, rows
    def nb(self, part, first, d):
        m = self.me
        use_z = (m["x"] == 0) if (part == 0) == first else (m["x"] == 1)
        zi = jnp.where(use_z, (m["z"] + d) % 4, m["z"])
        yi = jnp.where(use_z, m["y"], (m["y"] + d) % 4)
        return {"fsdp": (yi * 4 + zi) * 2 + m["x"], "grp": m["g"]}
    def idx(self, part, d1, d2):
        m = self.me
        use_z = (m["x"] == 0) if part == 0 else (m["x"] == 1)
        dz = jnp.where(use_z, d1, d2)
        dy = jnp.where(use_z, d2, d1)
        px = m["x"] if part == 0 else 1 - m["x"]
        return (((m["y"] + dy) % 4) * 4 + (m["z"] + dz) % 4) * 2 + px
    def ref(self, part, d1, d2, half=None):
        b = self.G.at[self.idx(part, d1, d2)]
        if half is None:
            return b
        h = self.rows // 2
        return b.at[pl.ds(half * h, h)]
    def xsend(self, src):
        m = self.me
        self.L.send(src, self.G.at[m["f"]], (self.name, "x"), {"grp": m["g"], "fsdp": m["f"] + 1 - 2 * m["x"]}, self.name)
    def xrecv(self):
        m = self.me
        self.L.recv(self.ref(1, 0, 0), (self.name, "x"), {"grp": m["g"], "fsdp": m["f"] + 1 - 2 * m["x"]}, self.name)
    def s1(self, part, first, k, src=None):
        d = (0, 0) if first else (k, 0)
        r = self.ref(part, *d)
        src = r if src is None else src
        for s in (1, 3):
            self.L.send(src, r, (self.name, part, first, k, "s1", s), self.nb(part, first, s), self.name)
    def s2(self, part, first, k, s):
        o = 4 - s
        d = (o, 0) if first else (k, o)
        self.L.recv(self.ref(part, *d), (self.name, part, first, k, "s1", s), self.nb(part, first, o), self.name)
        half = 0 if s == 1 else 1
        r = self.ref(part, *d, half)
        self.L.send(r, r, (self.name, part, first, k, "s2", s), self.nb(part, first, s), self.name)
    def s3(self, part, first, k):
        d = (2, 0) if first else (k, 2)
        for s in (1, 3):
            half = 0 if s == 1 else 1
            self.L.recv(self.ref(part, *d, half), (self.name, part, first, k, "s2", s), self.nb(part, first, 4 - s), self.name)
    def stages(self, own):
        def a():
            self.s1(0, True, 0, own)
            self.s1(0, False, 0, own)
        def b():
            self.xrecv()
            self.s1(1, True, 0)
            self.s1(1, False, 0)
        def c():
            for part in (0, 1):
                self.s2(part, True, 0, 1)
                self.s2(part, True, 0, 3)
        def d():
            for k in (1, 3):
                self.s1(0, False, k); self.s1(1, False, k)
        def e():
            self.s3(0, True, 0); self.s1(0, False, 2)
            self.s3(1, True, 0); self.s1(1, False, 2)
        def fw(k):
            def f():
                for part in (0, 1):
                    self.s2(part, False, k, 1); self.s2(part, False, k, 3)
            return f
        def fin(k):
            def f():
                for part in (0, 1):
                    self.s3(part, False, k)
            return f
        return [a, b, c, d, e, fw(0), fw(1), fin(0), fw(3), fin(1), fw(2), fin(3), fin(2)]
    def sent(self):
        m = self.me
        self.L.sent(self.G.at[pl.ds(0, 31)], self.name, (self.name, "x"), {"grp": m["g"], "fsdp": m["f"] + 1 - 2 * m["x"]})

def barrier(me, devs):
    b = pltpu.get_barrier_semaphore()
    for d in devs:
        pl.semaphore_signal(b, inc=1, device_id=d, device_id_type=MESH)
    pl.semaphore_wait(b, len(devs))

def neighbours(me):
    m = me
    out = [{"grp": m["g"], "fsdp": m["f"] + 1 - 2 * m["x"]}]
    for d in (1, 3):
        out.append({"grp": m["g"], "fsdp": (m["y"] * 4 + (m["z"] + d) % 4) * 2 + m["x"]})
        out.append({"grp": m["g"], "fsdp": (((m["y"] + d) % 4) * 4 + m["z"]) * 2 + m["x"]})
    return out


class TwoStep:
    def __init__(self, L, me, name, parts, r0, r1, s1, r2):
        self.L, self.me, self.name = L, me, name
        self.parts, self.r, self.s1, self.r2 = parts, (r0, r1), s1, r2
        self.sib = {"grp": me["g"] + 1 - 2 * me["core"], "fsdp": me["f"]}
        self.opp = {"grp": (1 - me["hi"]) * 2 + me["core"], "fsdp": me["f"]}
    def order(self):
        hi, core = self.me["hi"], self.me["core"]
        return [2 * (1 - hi) + 1 - core, 2 * hi + 1 - core, 2 * (1 - hi) + core, 2 * hi + core]
    def start(self, j):
        self.L.send(self.parts.at[self.order()[j]], self.r[j], (self.name, "c", j), self.sib)
    def mid(self):
        m = self.me
        self.L.recv(self.r[0], (self.name, "c", 0), self.sib)
        for i in range(self.s1.shape[0] // 32):
            rows = pl.ds(i * 32, 32)
            self.s1[rows] = (self.parts[2 * (1 - m["hi"]) + m["core"], rows].astype(F32) + self.r[0][rows].astype(F32)).astype(BF)
        self.L.send(self.s1, self.r2, (self.name, "o"), self.opp)
    def end(self):
        self.L.recv(self.r[1], (self.name, "c", 1), self.sib)
        self.L.recv(self.r2, (self.name, "o"), self.opp)
    def total(self, rows):
        m = self.me
        return self.parts[2 * m["hi"] + m["core"], rows].astype(F32) + self.r[1][rows].astype(F32) + self.r2[rows].astype(F32)


def along_x(me, d):
    X = (me["hi"] * 2 + me["x"] + d) % 4
    return X // 2, X % 2


def same_core(me, d):
    hi, x = along_x(me, d)
    return dev(hi, me["core"], me["y"], me["z"], x)


class Eight:
    def __init__(self, L, me, name, E, rows):
        self.L, self.me, self.name, self.E, self.rows = L, me, name, E, rows
        self.sib = {"grp": me["g"] + 1 - 2 * me["core"], "fsdp": me["f"]}
    def ref(self, d, core, half=None):
        hi, x = along_x(self.me, d)
        r = self.E.at[x, hi * 2 + core]
        if half is None:
            return r
        h = self.rows // 2
        return r.at[pl.ds(half * h, h)]
    def start(self):
        r = self.ref(0, self.me["core"])
        for s in (1, 3):
            self.L.send(r, r, (self.name, "s1", s), same_core(self.me, s))
        self.L.send(r, r, (self.name, "sib", 0), self.sib)
    def mid(self):
        c = self.me["core"]
        for s in (1, 3):
            r = self.ref(4 - s, c)
            self.L.recv(r, (self.name, "s1", s), same_core(self.me, s))
            half = 0 if s == 1 else 1
            rh = self.ref(4 - s, c, half)
            self.L.send(rh, rh, (self.name, "s2", s), same_core(self.me, s))
            self.L.send(r, r, (self.name, "sib", 4 - s), self.sib)
    def mid2(self):
        c = self.me["core"]
        for s in (1, 3):
            half = 0 if s == 1 else 1
            rh = self.ref(2, c, half)
            self.L.recv(rh, (self.name, "s2", s), same_core(self.me, s))
            self.L.send(rh, rh, (self.name, "sib2", s), self.sib)
    def end(self):
        oc = 1 - self.me["core"]
        for d in (0, 1, 3):
            self.L.recv(self.ref(d, oc), (self.name, "sib", d), self.sib)
        for s in (1, 3):
            self.L.recv(self.ref(2, oc, 0 if s == 1 else 1), (self.name, "sib2", s), self.sib)


def eight_others(me):
    out = []
    for d in range(4):
        hi, x = along_x(me, d)
        for c in (0, 1):
            if d == 0 and c == 0:
                continue
            core = 1 - me["core"] if c == 1 else me["core"]
            out.append(((d, c), dev(hi, core, me["y"], me["z"], x), (x, hi * 2 + core)))
    return out


class Scatter:
    def __init__(self, L, me, name, D, ra, rb, rx):
        self.L, self.me, self.name, self.D, self.ra, self.rb, self.rx = L, me, name, D, ra, rb, rx
        self.rows = D.shape[1]
    def axis(self, part, stage):
        m = self.me
        own = m["x"] == 0 if part == 0 else m["x"] == 1
        return own if stage == 1 else jnp.logical_not(own)
    def nb(self, part, stage, d):
        m = self.me
        use_z = self.axis(part, stage)
        zi = jnp.where(use_z, (m["z"] + d) % 4, m["z"])
        yi = jnp.where(use_z, m["y"], (m["y"] + d) % 4)
        return {"fsdp": (yi * 4 + zi) * 2 + m["x"], "grp": m["g"]}
    def ref(self, part, stage, k, d, half=None):
        m = self.me
        use_z = self.axis(part, stage)
        dz = jnp.where(use_z, d, k)
        dy = jnp.where(use_z, k, d)
        px = m["x"] if part == 0 else 1 - m["x"]
        b = self.D.at[(((m["y"] + dy) % 4) * 4 + (m["z"] + dz) % 4) * 2 + px]
        if half is None:
            return b
        h = self.rows // 2
        return b.at[pl.ds(half * h, h)]
    def slot(self, stage, k):
        return k if stage == 0 else 4
    def far(self, part, stage, k):
        h = self.rows // 2
        for s in (1, 3):
            half = 0 if s == 1 else 1
            self.L.send(self.ref(part, stage, k, 2, half), self.ra.at[part, self.slot(stage, k), half], (self.name, part, stage, k, "far", s), self.nb(part, stage, s), self.name)
    def near(self, part, stage, k):
        h = self.rows // 2
        for s in (1, 3):
            half = 0 if s == 1 else 1
            buf = self.ra.at[part, self.slot(stage, k), half]
            self.L.recv(buf, (self.name, part, stage, k, "far", s), self.nb(part, stage, 4 - s), self.name)
            r = self.ref(part, stage, k, s, half)
            r[...] = (r[...].astype(F32) + buf[...].astype(F32)).astype(BF)
            self.L.send(self.ref(part, stage, k, s), self.rb.at[part, self.slot(stage, k), half], (self.name, part, stage, k, "near", s), self.nb(part, stage, s), self.name)
    def total(self, part, stage, k):
        for s in (1, 3):
            half = 0 if s == 1 else 1
            self.L.recv(self.rb.at[part, self.slot(stage, k), half], (self.name, part, stage, k, "near", s), self.nb(part, stage, 4 - s), self.name)
        b = self.rb.at[part, self.slot(stage, k)]
        return self.ref(part, stage, k, 0)[...].astype(F32) + b[0].astype(F32) + b[1].astype(F32)
    def fold(self, part, stage, k):
        t = self.total(part, stage, k)
        self.ref(part, stage, k, 0)[...] = t.astype(BF)
    def partner(self):
        m = self.me
        return {"grp": m["g"], "fsdp": m["f"] + 1 - 2 * m["x"]}
    def xsend(self):
        self.fold(1, 1, 0)
        self.L.send(self.ref(1, 1, 0, 0), self.rx, (self.name, "x"), self.partner(), self.name)
    def result(self):
        t = self.total(0, 1, 0)
        self.L.recv(self.rx, (self.name, "x"), self.partner(), self.name)
        return t + self.rx[...].astype(F32)
    def stages(self):
        def a():
            for k in (2, 1, 3, 0):
                for part in (1, 0):
                    self.far(part, 0, k)
        def b(k):
            def f():
                for part in (1, 0):
                    self.near(part, 0, k)
            return f
        def c(k):
            def f():
                for part in (1, 0):
                    self.fold(part, 0, k)
                    if k == 2:
                        self.far(part, 1, 0)
            return f
        def d():
            for part in (1, 0):
                self.near(part, 1, 0)
        return [a, b(2), b(1), c(2), b(3), c(1), b(0), c(3), d, c(0), self.xsend]
    def sent(self):
        self.L.sent(self.D.at[pl.ds(0, 31)], self.name, (self.name, "x"), self.partner())


def wait_bytes(like, send_sem, recv_sem, devid, recv=True, send=True):
    c = pltpu.make_async_remote_copy(src_ref=like, dst_ref=like, send_sem=send_sem, recv_sem=recv_sem, device_id=devid, device_id_type=MESH)
    if recv:
        c.wait_recv()
    if send:
        c.wait_send()


def dot(a, b, ca, cb):
    return lax.dot_general(a, b, (((ca,), (cb,)), ((), ())), preferred_element_type=F32)


class Refs:
    pass


P_IN = ["lens", "counts", "scap", "tgain", "fgain", "cs_h", "tq_h", "tk_h", "tv_h", "bias_h", "tout_h", "vid_h", "grad_h", "ck_h", "cv_h", "cq_h", "co_h"]
P_OUT = {
    "qb": ((256, 384), BF),
    "da": ((256, 384), BF),
    "ks": ((2, 384, 384), BF),
    "mu": ((256, 1), F32),
    "inv": ((256, 1), F32),
}
P_FAR = {
    "gq": ((32, 192, 384), BF),
    "vnT": ((3072, 256), BF),
    "gradT": ((3072, 256), BF),
}
P_SCRATCH = {
    "kv": ((2, 128, 384), BF),
    "qo": ((192, 384), BF),
    "cs": ((128, 4096), BF),
    "normed": ((128, 4096), BF),
    "wt": ((2, 4096, 512), BF),
    "bias": ((8, 128, 128), F32),
    "tqkv": ((3, 128, 512), BF),
    "tm": ((128, 512), BF),
    "vid": ((256, 3072), BF),
    "grad": ((256, 3072), BF),
    "vn": ((256, 3072), BF),
    "gw": ((32, 128, 384), BF),
    "parts": ((4, 128, 1024), BF),
    "t0": ((128, 1024), BF),
    "t1": ((128, 1024), BF),
    "t2": ((128, 1024), BF),
    "t3": ((128, 1024), BF),
    "E": ((2, 4, 128, 1024), BF),
    "sscol": ((128, 1), F32),
    "SS": ((2, 4, 8, 128), F32),
    "kvp": ((16, 2, 8, 384), BF),
    "C": ((32, 8, 384), BF),
    "sb": ((32, 3, 8, 384), BF),
    "R": ((32, 3, 8, 384), BF),
}
P_TABLES = {"end": 32, "first": 32, "cap": 96, "samp": 32}
Q_IN = ["edge", "sidx", "qb", "da", "ks", "mu", "inv", "gq_h", "vnT_h", "gradT_h", "vid_h", "grad_h"]
Q_OUT = {
    "updated": ((256, 768), BF),
    "igrad": ((256, 768), BF),
    "qgrad": ((96, 384), F32),
    "ograd": ((96, 384), F32),
    "kgrad": ((128, 384), BF),
    "vgrad": ((128, 384), BF),
}
Q_SCRATCH = {
    "gq": ((32, 192, 384), BF),
    "vnT": ((3072, 256), BF),
    "gradT": ((3072, 256), BF),
    "vid": ((256, 3072), BF),
    "grad": ((256, 3072), BF),
    "att": ((256, 384), BF),
    "dq": ((256, 384), BF),
    "w": ((3, 256, 128), F32),
    "mp": ((3, 256, 384), BF),
    "ms": ((3, 256, 384), BF),
    "T": ((32, 3, 8, 384), BF),
    "Dw": ((32, 96, 384), BF),
    "Dq": ((32, 96, 384), BF),
    "ra1": ((2, 5, 2, 48, 384), BF),
    "rb1": ((2, 5, 2, 96, 384), BF),
    "rx1": ((96, 384), BF),
    "ra2": ((2, 5, 2, 48, 384), BF),
    "rb2": ((2, 5, 2, 96, 384), BF),
    "rx2": ((96, 384), BF),
    "op": ((4, 256, 768), BF),
    "o0": ((256, 768), BF),
    "o1": ((256, 768), BF),
    "o2": ((256, 768), BF),
    "o3": ((256, 768), BF),
    "dn": ((4, 256, 768), BF),
    "n0": ((256, 768), BF),
    "n1": ((256, 768), BF),
    "n2": ((256, 768), BF),
    "n3": ((256, 768), BF),
    "scol": ((2, 256, 1), F32),
    "stat": ((4, 2, 8, 256), F32),
    "RG": ((99, 8, 384), BF),
    "CG": ((32, 8, 384), BF),
    "KV": ((32, 8, 384), BF),
}


def fill_tables(r):
    def total(s, acc):
        acc = acc + r.counts[s]
        r.end[s] = acc
        return acc
    lax.fori_loop(0, 32, total, jnp.int32(0))

    @pl.loop(0, 32)
    def _(d):
        count = jnp.int32(0)
        for s in range(32):
            count = count + (r.end[s] <= 256 * d).astype(jnp.int32)
        r.first[d] = count
        for t in range(3):
            r.cap[d * 3 + t] = r.scap[jnp.minimum(count + t, 31)]

    @pl.loop(0, 32)
    def _(c):
        s = jnp.int32(0)
        for t in range(32):
            s = s + jnp.where(r.scap[t] == c, t, 0)
        s = jnp.minimum(s, 31)
        stop = r.end[s]
        d0 = (stop - r.counts[s]) // 256
        for m in range(5):
            d = d0 + m
            valid = (d < 32) & (d * 256 < stop)
            r.sidx[c * 5 + m] = jnp.clip(jnp.where(valid, 3 * d + s - r.first[jnp.minimum(d, 31)], 96), 0, 96)


def named(refs, names):
    r = Refs()
    for n, ref in zip(names, refs):
        setattr(r, n, ref)
    return r


def encode(*refs):
    r = named(refs, P_IN + list(P_OUT) + [n + "_o" for n in P_FAR] + ["edge", "sidx"] + list(P_FAR) + list(P_SCRATCH) + list(P_TABLES) + ["sems", "lsem", "asem"])
    me = place()
    f, g, core, hi = me["f"], me["g"], me["core"], me["hi"]
    L = Links(r.sems)
    loads = {}

    def load(name, src, dst):
        c = pltpu.make_async_copy(src, dst, r.lsem.at[len(loads)])
        c.start()
        loads[name] = c
    load("ck", r.ck_h, r.kv.at[0])
    load("cv", r.cv_h, r.kv.at[1])
    load("cq", r.cq_h, r.qo.at[pl.ds(0, 96)])
    load("co", r.co_h, r.qo.at[pl.ds(96, 96)])
    load("cs", r.cs_h, r.cs)

    def load_text(a, wh):
        for k in range(2):
            rows = pl.ds(k * 2048, 2048)
            load(("wt", a, k), wh.at[rows], r.wt.at[a % 2, rows])
    load_text(0, r.tq_h)
    load_text(1, r.tk_h)
    load("bias", r.bias_h, r.bias)
    load("vid", r.vid_h, r.vid)
    load("grad", r.grad_h, r.grad)

    others = eight_others(me)
    fs = [{"grp": g, "fsdp": (f + j) % 32} for j in range(1, 32)]
    barrier(me, fs + [{"grp": (g + j) % 4, "fsdp": f // 2 * 2 + x} for j in range(1, 4) for x in range(2)])

    A, B = Gather(L, me, "w", r.gw, 128), Gather(L, me, "q", r.gq, 192)
    sa, sb = A.stages(r.kv.at[me["x"]]), B.stages(r.qo)
    for n in ("ck", "cv", "cq", "co"):
        loads[n].wait()
    A.xsend(r.kv.at[1 - me["x"]])
    sa[0]()
    B.xsend(r.qo)
    sb[0]()
    r.gw[f] = r.kv[me["x"]]
    r.gq[f] = r.qo[...]

    loads["cs"].wait()

    @pl.loop(0, 8)
    def _(i):
        rows = pl.ds(i * 16, 16)
        x = r.cs[rows].astype(F32)
        mean_square = jnp.mean(x * x, axis=-1, keepdims=True)
        r.normed[rows] = (x * lax.rsqrt(mean_square + 1e-06) * r.tgain[...]).astype(BF)

    def project(a):
        acc = jnp.zeros((128, 512), F32)
        for k in range(2):
            loads["wt", a, k].wait()
            acc = acc + jnp.dot(r.normed[:, pl.ds(k * 2048, 2048)], r.wt[a % 2, pl.ds(k * 2048, 2048)], preferred_element_type=F32)
        r.tqkv[a] = acc.astype(BF)
    project(0)
    load_text(2, r.tv_h)
    sa[1]()
    project(1)
    for k in range(8):
        load(("wo", k), r.tout_h.at[:, pl.ds(k * 512, 512)], r.wt.at[1, pl.ds(k * 512, 512)])
    sb[1]()
    project(2)
    sa[2]()
    sa[3]()
    loads["bias"].wait()
    lane = lax.broadcasted_iota(jnp.int32, (128, 128), 1)
    valid = lane < r.lens[f]

    def text_pair(p):
        cols = pl.ds(p * 128, 128)
        q, k, v = r.tqkv[0, :, cols], r.tqkv[1, :, cols], r.tqkv[2, :, cols]
        out = []
        for i in range(2):
            qh = jnp.where((lane < 64) == (i == 0), q.astype(F32), 0.0).astype(BF)
            ex = jnp.where(valid, jnp.exp(dot(qh, k, 1, 1) + r.bias[2 * p + i]), 0.0)
            wts = (ex / jnp.sum(ex, axis=-1, keepdims=True)).astype(BF)
            out.append(dot(wts, v, 1, 0))
        r.tm[:, cols] = jnp.where(lane < 64, out[0], out[1]).astype(BF)
    text_pair(0)
    text_pair(1)
    sb[2]()
    sb[3]()
    text_pair(2)
    text_pair(3)
    sa[4]()
    sa[5]()
    for k in range(8):
        loads["wo", k].wait()
    T = TwoStep(L, me, "t", r.parts, r.t0, r.t1, r.t2, r.t3)
    for j, s in enumerate(T.order()):
        for n in range(2):
            cols = pl.ds(n * 512, 512)
            r.parts[s, :, cols] = jnp.dot(r.tm[...], r.wt[1, pl.ds((2 * s + n) * 512, 512)], preferred_element_type=F32).astype(BF)
        if j < 2:
            T.start(j)
    sb[4]()
    sb[5]()
    T.mid()
    sa[6]()
    sb[6]()
    fill_tables(r)
    T.end()

    @pl.loop(0, 8)
    def _(i):
        rows, cols = pl.ds(i * 16, 16), pl.ds(pl.multiple_of(g * 1024, 1024), 1024)
        ts = T.total(rows) + r.cs[rows, cols].astype(F32)
        r.E[me["x"], g, rows] = (ts * r.fgain[:, cols]).astype(BF)
        r.sscol[rows] = jnp.sum(ts * ts, axis=1, keepdims=True)
    X = Eight(L, me, "e", r.E, 128)
    X.start()
    r.SS[me["x"], g] = jnp.broadcast_to(r.sscol[...], (128, 128)).T[:8]
    mine = r.SS.at[me["x"], g]
    for key, d, _ in others:
        L.send(mine, mine, ("ss", (4 - key[0]) % 4, key[1]), d)
    sa[7]()
    sa[8]()

    loads["vid"].wait()

    @pl.loop(0, 16)
    def _(i):
        rows = pl.ds(i * 16, 16)
        v = r.vid[rows].astype(F32)
        mean = jnp.mean(v, axis=-1, keepdims=True)
        center = v - mean
        inverse = lax.rsqrt(jnp.mean(center * center, axis=-1, keepdims=True) + 1e-06)
        r.mu[rows], r.inv[rows] = mean, inverse
        r.vn[rows] = (center * inverse).astype(BF)
    X.mid()
    sb[7]()
    sb[8]()
    loads["grad"].wait()

    @pl.loop(0, 24)
    def _(i):
        lanes = pl.ds(pl.multiple_of(i * 128, 128), 128)
        r.vnT[lanes] = r.vn[:, lanes].T
        r.gradT[lanes] = r.grad[:, lanes].T
    load("vnT_o", r.vnT, r.vnT_o)
    load("gradT_o", r.gradT, r.gradT_o)
    X.mid2()
    for i in range(9, 13):
        sa[i]()
    sb[9]()
    sb[10]()
    X.end()
    for key, d, slot in others:
        L.recv(r.SS.at[slot[0], slot[1]], ("ss", key[0], key[1]), d)

    acc = jnp.zeros((256, 384), F32)
    for k in range(4):
        acc = acc + jnp.dot(r.E[:, k].reshape(256, 1024), r.gw[k * 8 : k * 8 + 8].reshape(1024, 384), preferred_element_type=F32)
    for c in range(2):
        ss = r.SS[c, 0, :1] + r.SS[c, 1, :1] + r.SS[c, 2, :1] + r.SS[c, 3, :1]
        col = jnp.broadcast_to(ss, (128, 128)).T[:, :1]
        r.kvp[:, c] = (acc[c * 128 : c * 128 + 128] * lax.rsqrt(col / 4096 + 1e-06)).reshape(16, 8, 384).astype(BF)

    partner = {"grp": g, "fsdp": (f + 1) % 32}
    yz = f // 2

    @pl.loop(1, 16)
    def _(j):
        to = (yz + j) % 16
        pltpu.make_async_remote_copy(src_ref=r.kvp.at[to], dst_ref=r.C.at[pl.ds(2 * yz, 2)], send_sem=r.asem.at[0], recv_sem=r.asem.at[1], device_id={"grp": g, "fsdp": to * 2 + me["x"]}, device_id_type=MESH).start()
    r.C[pl.ds(2 * yz, 2)] = r.kvp[yz]
    wait_bytes(r.C.at[pl.ds(0, 30)], r.asem.at[0], r.asem.at[1], partner)

    @pl.loop(1, 32)
    def _(j):
        to = (f + j) % 32
        for s in range(3):
            r.sb[to, s] = r.C[r.cap[to * 3 + s]]
        pltpu.make_async_remote_copy(src_ref=r.sb.at[to], dst_ref=r.R.at[f], send_sem=r.asem.at[2], recv_sem=r.asem.at[3], device_id={"grp": g, "fsdp": to}, device_id_type=MESH).start()
    for s in range(3):
        r.R[f, s] = r.C[r.cap[f * 3 + s]]
    for s in sb[11:]:
        s()
    load("gq_o", r.gq, r.gq_o)

    acc = jnp.zeros((256, 384), F32)
    acc2 = jnp.zeros((256, 384), F32)
    for k in range(4):
        cols = pl.ds(k * 768, 768)
        acc = acc + jnp.dot(r.vn[:, cols], r.gq[k * 8 : k * 8 + 8, 0:96].reshape(768, 384), preferred_element_type=F32)
    r.qb[...] = acc.astype(BF)
    for k in range(4):
        cols = pl.ds(k * 768, 768)
        acc2 = acc2 + jnp.dot(r.grad[:, cols], r.gq[k * 8 : k * 8 + 8, 96:192].reshape(768, 384), preferred_element_type=F32)
    r.da[...] = acc2.astype(BF)

    first = r.first[f]
    r.edge[0], r.edge[1] = r.end[jnp.minimum(first, 31)], r.end[jnp.minimum(first + 1, 31)]
    for s in range(3):
        r.edge[2 + s] = r.lens[r.cap[f * 3 + s]]
    wait_bytes(r.R.at[pl.ds(0, 31)], r.asem.at[2], r.asem.at[3], partner)
    for kv in range(2):
        for s in range(3):
            r.ks[kv, pl.ds(s * 128, 128)] = r.R[:, s].reshape(16, 2, 8, 384)[:, kv].astype(F32).reshape(128, 384).astype(BF)
    A.sent()
    B.sent()
    L.drain()
    for n in P_FAR:
        loads[n + "_o"].wait()


def attend(*refs):
    r = named(refs, Q_IN + list(Q_OUT) + list(Q_SCRATCH) + ["sems", "lsem", "asem"])
    me = place()
    f, g, core, hi = me["f"], me["g"], me["core"], me["hi"]
    L = Links(r.sems)
    partner = {"grp": g, "fsdp": (f + 1) % 32}
    loads = {}
    for i, n in enumerate(("gradT", "gq", "vnT", "vid", "grad")):
        loads[n] = pltpu.make_async_copy(getattr(r, n + "_h"), getattr(r, n), r.lsem.at[i])
        loads[n].start()
    barrier(me, [{"grp": g, "fsdp": (f + j) % 32} for j in range(1, 32)] + [{"grp": (g + j) % 4, "fsdp": f} for j in range(1, 4)])
    position = lax.broadcasted_iota(jnp.int32, (256, 128), 0) + f * 256
    slot = (position >= r.edge[0]).astype(jnp.int32) + (position >= r.edge[1]).astype(jnp.int32)
    token_len = jnp.where(slot == 0, r.edge[2], jnp.where(slot == 1, r.edge[3], r.edge[4]))
    token_valid = lax.broadcasted_iota(jnp.int32, (256, 128), 1) < token_len
    scale = 1.0 / math.sqrt(HEAD_SIZE)

    def pick(a):
        return jnp.where(slot == 0, a[:, 0:128], jnp.where(slot == 1, a[:, 128:256], a[:, 256:384]))

    def placed(a):
        return jnp.concatenate([jnp.where(slot == s, a, 0.0).astype(BF) for s in range(3)], axis=1)

    for h in range(3):
        cols = pl.ds(h * 128, 128)
        scores = pick(dot(r.qb[:, cols], r.ks[0, :, cols], 1, 1)) * scale
        ex = jnp.where(token_valid, jnp.exp(scores), 0.0)
        w = ex / jnp.sum(ex, axis=-1, keepdims=True)
        r.w[h] = w
        mp = placed(w)
        r.mp[h] = mp
        r.att[:, cols] = dot(mp, r.ks[1, :, cols], 1, 0).astype(BF)

    def weight_grad(D, left, right):
        @pl.loop(0, 8)
        def _(i):
            rows = pl.ds(i * 384, 384)
            D[pl.ds(i * 4, 4)] = dot(left[rows], right[...], 1, 0).reshape(4, 96, 384).astype(BF)
    loads["gradT"].wait()
    weight_grad(r.Dw, r.gradT, r.att)
    S1 = Scatter(L, me, "d1", r.Dw, r.ra1, r.rb1, r.rx1)
    S2 = Scatter(L, me, "d2", r.Dq, r.ra2, r.rb2, r.rx2)
    s1, s2 = S1.stages(), S2.stages()
    s1[0]()
    loads["gq"].wait()
    O = TwoStep(L, me, "o", r.op, r.o0, r.o1, r.o2, r.o3)
    N = TwoStep(L, me, "n", r.dn, r.n0, r.n1, r.n2, r.n3)
    for j, s in enumerate(O.order()):
        r.op[s] = dot(r.att[...], r.gq[pl.ds(s * 8, 8), 96:192].reshape(768, 384), 1, 1).astype(BF)
        if j < 2:
            O.start(j)
    s1[1]()

    for h in range(3):
        cols = pl.ds(h * 128, 128)
        d_probs = pick(dot(r.da[:, cols], r.ks[1, :, cols], 1, 1))
        w = r.w[h]
        ds = w * (d_probs - jnp.sum(w * d_probs, axis=-1, keepdims=True)) * scale
        ms = placed(ds)
        r.ms[h] = ms
        r.dq[:, cols] = dot(ms, r.ks[0, :, cols], 1, 0).astype(BF)
    O.mid()
    loads["vnT"].wait()
    weight_grad(r.Dq, r.vnT, r.dq)
    s2[0]()
    s1[2]()
    s1[3]()
    for j, s in enumerate(N.order()):
        r.dn[s] = dot(r.dq[...], r.gq[pl.ds(s * 8, 8), 0:96].reshape(768, 384), 1, 1).astype(BF)
        if j < 2:
            N.start(j)
    for h in range(3):
        cols = pl.ds(h * 128, 128)
        kt = dot(r.ms[h], r.qb[:, cols], 0, 0)
        vt = dot(r.mp[h], r.da[:, cols], 0, 0)
        for s in range(3):
            rows = slice(s * 128, s * 128 + 128)
            both = jnp.stack([kt[rows].reshape(16, 8, 128), vt[rows].reshape(16, 8, 128)], axis=1)
            r.T[:, s, :, cols] = both.reshape(32, 8, 128).astype(BF)

    @pl.loop(1, 32)
    def _(j):
        to = (f + j) % 32
        pltpu.make_async_remote_copy(src_ref=r.T.at[to], dst_ref=r.RG.at[pl.ds(3 * f, 3)], send_sem=r.asem.at[4], recv_sem=r.asem.at[5], device_id={"grp": g, "fsdp": to}, device_id_type=MESH).start()
    N.mid()
    for i in range(4, 8):
        s1[i]()
    s2[1]()
    s2[2]()
    s1[8]()
    for i in (3, 4):
        s2[i]()
    for i in (9, 10):
        s1[i]()
    for i in (5, 6, 7):
        s2[i]()
    r.RG[pl.ds(96, 3)] = jnp.zeros((3, 8, 384), BF)
    r.RG[pl.ds(3 * f, 3)] = r.T[f]
    wait_bytes(r.RG.at[pl.ds(0, 93)], r.asem.at[4], r.asem.at[5], partner)

    @pl.loop(0, 32)
    def _(c):
        acc = r.RG[r.sidx[c * 5]].astype(F32)
        for m in range(1, 5):
            acc = acc + r.RG[r.sidx[c * 5 + m]].astype(F32)
        r.CG[c] = acc.astype(BF)

    @pl.loop(1, 32)
    def _(j):
        to = (f + j) % 32
        pltpu.make_async_remote_copy(src_ref=r.CG.at[to], dst_ref=r.KV.at[f], send_sem=r.asem.at[6], recv_sem=r.asem.at[7], device_id={"grp": g, "fsdp": to}, device_id_type=MESH).start()
    r.KV[f] = r.CG[f]
    s2[8]()
    O.end()
    loads["vid"].wait()
    loads["grad"].wait()
    cols = pl.ds(pl.multiple_of(g * 768, 768), 768)

    @pl.loop(0, 16)
    def _(i):
        rows = pl.ds(i * 16, 16)
        r.updated[rows] = (r.vid[rows, cols].astype(F32) + O.total(rows)).astype(BF)
    N.end()

    def video_hat(rows):
        return (r.vid[rows, cols].astype(F32) - r.mu[rows]) * r.inv[rows]

    @pl.loop(0, 16)
    def _(i):
        rows = pl.ds(i * 16, 16)
        t = N.total(rows)
        r.scol[0, rows] = jnp.sum(t, axis=1, keepdims=True)
        r.scol[1, rows] = jnp.sum(t * video_hat(rows), axis=1, keepdims=True)
    for k in range(2):
        r.stat[g, k] = jnp.broadcast_to(r.scol[k], (256, 128)).T[:8]
    grp = [{"grp": (g + j) % 4, "fsdp": f} for j in range(1, 4)]
    for j in range(1, 4):
        L.send(r.stat.at[g], r.stat.at[g], ("st", j), grp[j - 1])
    for i in (9, 10):
        s2[i]()
    r.ograd[...] = S1.result()
    for j in range(1, 4):
        L.recv(r.stat.at[(g + 4 - j) % 4], ("st", j), grp[3 - j])
    for k in range(2):
        s = r.stat[0, k, :1] + r.stat[1, k, :1] + r.stat[2, k, :1] + r.stat[3, k, :1]
        r.scol[k] = jnp.broadcast_to(s / 3072, (128, 256)).T[:, :1]

    @pl.loop(0, 16)
    def _(i):
        rows = pl.ds(i * 16, 16)
        d = N.total(rows) - r.scol[0, rows] - video_hat(rows) * r.scol[1, rows]
        r.igrad[rows] = (r.grad[rows, cols].astype(F32) + r.inv[rows] * d).astype(BF)
    wait_bytes(r.KV.at[pl.ds(0, 31)], r.asem.at[6], r.asem.at[7], partner)
    r.kgrad[...] = r.KV[...].reshape(16, 2, 8, 384)[:, 0].astype(F32).reshape(128, 384).astype(BF)
    r.vgrad[...] = r.KV[...].reshape(16, 2, 8, 384)[:, 1].astype(F32).reshape(128, 384).astype(BF)
    r.qgrad[...] = S2.result()
    S1.sent()
    S2.sent()
    L.drain()


def hand_over(*refs):
    held, sem = refs[12:18], refs[18]
    into = [pltpu.make_async_copy(refs[i], held[i], sem.at[i]) for i in range(6)]
    out = [pltpu.make_async_copy(held[i], refs[6 + i], sem.at[6 + i]) for i in range(6)]
    for c in into:
        c.start()
    for i in range(6):
        into[i].wait()
        out[i].start()
    for c in out:
        c.wait()


def local(caption_states, caption_lens, text_gain, text_query, text_key, text_value, text_bias, text_out, final_gain, cross_key, cross_value, video_states, video_counts, sample_caption, cross_query, cross_out, out_grad):
    V, M, A = pltpu.VMEM, pltpu.SMEM, pl.ANY

    def call(kernel, name, cid, args, spaces, outs, far, tables, scratch, smem):
        return pl.pallas_call(
            kernel,
            out_shape=tuple(jax.ShapeDtypeStruct(s, d) for s, d in (outs | far).values()) + tuple(jax.ShapeDtypeStruct((n,), jnp.int32) for n in tables),
            in_specs=[pl.BlockSpec(memory_space=s) for s in spaces],
            out_specs=tuple(pl.BlockSpec(memory_space=V) for _ in outs) + tuple(pl.BlockSpec(memory_space=A) for _ in far) + tuple(pl.BlockSpec(memory_space=M) for _ in tables),
            scratch_shapes=[V(s, d) for s, d in (far | scratch).values()] + [M((n,), jnp.int32) for n in smem] + [DMA((128,)), DMA((32,)), DMA((8,))],
            compiler_params=pltpu.CompilerParams(collective_id=cid, has_side_effects=True, vmem_limit_bytes=58 << 20),
            name=name,
        )(*args)
    args = [caption_lens, video_counts, sample_caption, text_gain[None], final_gain[None], caption_states.reshape(128, 4096), text_query, text_key, text_value, text_bias, text_out, video_states, out_grad, cross_key, cross_value, cross_query, cross_out.T]
    qb, da, ks, mu, inv, gq, vnT, gradT, edge, sidx = call(encode, "encode", 0, args, [M] * 3 + [V] * 2 + [A] * 12, P_OUT, P_FAR, (8, 160), P_SCRATCH, P_TABLES.values())
    args = [edge, sidx, qb, da, ks, mu, inv, gq, vnT, gradT, video_states, out_grad]
    outs = call(attend, "attend", 1, args, [M] * 2 + [V] * 5 + [A] * 5, Q_OUT, {}, (), Q_SCRATCH, ())
    updated, igrad, qgrad, ograd, kgrad, vgrad = pl.pallas_call(
        hand_over,
        out_shape=tuple(jax.ShapeDtypeStruct(s, d) for s, d in Q_OUT.values()),
        in_specs=[pl.BlockSpec(memory_space=A)] * 6,
        out_specs=(pl.BlockSpec(memory_space=A),) * 6,
        scratch_shapes=[V(s, d) for s, d in Q_OUT.values()] + [DMA((12,))],
        name="hand_over",
    )(*outs)
    return updated, igrad, qgrad, ograd.T, kgrad[None], vgrad[None]


def solution(mesh):
    in_specs = (P("fsdp"), P(), P(), P(None, "grp"), P(None, "grp"), P(None, "grp"), P("grp"), P("grp"), P(), P("fsdp", "grp"), P("fsdp", "grp"), P("fsdp"), P(), P(), P("fsdp", "grp"), P("grp", "fsdp"), P("fsdp"))
    out_specs = (P("fsdp", "grp"), P("fsdp", "grp"), P("fsdp", "grp"), P("grp", "fsdp"), P("fsdp", None, "grp"), P("fsdp", None, "grp"))
    return jax.shard_map(local, mesh=mesh, in_specs=in_specs, out_specs=out_specs, check_vma=False)
```

```python
import math

import jax
import jax.numpy as jnp
from jax import lax
from jax.experimental import pallas as pl
from jax.experimental.pallas import tpu as pltpu
from jax.sharding import PartitionSpec as P
MESH = pl.DeviceIdType.MESH
BF, F32 = jnp.bfloat16, jnp.float32
DMA = pltpu.SemaphoreType.DMA
HEAD_SIZE = 128

class Links:
    def __init__(self, sems):
        self.sems, self.keys, self.pending = sems, {}, []
    def sem(self, key):
        return self.sems.at[self.keys.setdefault(key, len(self.keys))]
    def copy(self, src, dst, key, dev, group=None):
        send = self.sem(("s", group if group else key))
        return pltpu.make_async_remote_copy(src_ref=src, dst_ref=dst, send_sem=send, recv_sem=self.sem(("r", key)), device_id=dev, device_id_type=MESH)
    def send(self, src, dst, key, dev, group=None):
        c = self.copy(src, dst, key, dev, group)
        c.start()
        if group is None:
            self.pending.append(c)
    def recv(self, dst, key, dev, group=None):
        self.copy(dst, dst, key, dev, group).wait_recv()
    def sent(self, blocks, group, key, dev):
        self.copy(blocks, blocks, key, dev, group).wait_send()
    def drain(self):
        for c in self.pending:
            c.wait_send()
        self.pending = []

def place():
    g, f = lax.axis_index("grp"), lax.axis_index("fsdp")
    return dict(hi=g // 2, core=g % 2, y=f // 8, z=(f // 2) % 4, x=f % 2, g=g, f=f)

def dev(hi, core, y, z, x):
    return {"grp": hi * 2 + core, "fsdp": (y * 4 + z) * 2 + x}

class Gather:
    def __init__(self, L, me, name, G, rows):
        self.L, self.me, self.name, self.G, self.rows = L, me, name, G, rows
    def nb(self, part, first, d):
        m = self.me
        use_z = (m["x"] == 0) if (part == 0) == first else (m["x"] == 1)
        zi = jnp.where(use_z, (m["z"] + d) % 4, m["z"])
        yi = jnp.where(use_z, m["y"], (m["y"] + d) % 4)
        return {"fsdp": (yi * 4 + zi) * 2 + m["x"], "grp": m["g"]}
    def idx(self, part, d1, d2):
        m = self.me
        use_z = (m["x"] == 0) if part == 0 else (m["x"] == 1)
        dz = jnp.where(use_z, d1, d2)
        dy = jnp.where(use_z, d2, d1)
        px = m["x"] if part == 0 else 1 - m["x"]
        return (((m["y"] + dy) % 4) * 4 + (m["z"] + dz) % 4) * 2 + px
    def ref(self, part, d1, d2, half=None):
        b = self.G.at[self.idx(part, d1, d2)]
        if half is None:
            return b
        h = self.rows // 2
        return b.at[pl.ds(half * h, h)]
    def xsend(self, src):
        m = self.me
        self.L.send(src, self.G.at[m["f"]], (self.name, "x"), {"grp": m["g"], "fsdp": m["f"] + 1 - 2 * m["x"]}, self.name)
    def xrecv(self):
        m = self.me
        self.L.recv(self.ref(1, 0, 0), (self.name, "x"), {"grp": m["g"], "fsdp": m["f"] + 1 - 2 * m["x"]}, self.name)
    def s1(self, part, first, k, src=None):
        d = (0, 0) if first else (k, 0)
        r = self.ref(part, *d)
        src = r if src is None else src
        for s in (1, 3):
            self.L.send(src, r, (self.name, part, first, k, "s1", s), self.nb(part, first, s), self.name)
    def s2(self, part, first, k, s):
        o = 4 - s
        d = (o, 0) if first else (k, o)
        self.L.recv(self.ref(part, *d), (self.name, part, first, k, "s1", s), self.nb(part, first, o), self.name)
        half = 0 if s == 1 else 1
        r = self.ref(part, *d, half)
        self.L.send(r, r, (self.name, part, first, k, "s2", s), self.nb(part, first, s), self.name)
    def s3(self, part, first, k):
        d = (2, 0) if first else (k, 2)
        for s in (1, 3):
            half = 0 if s == 1 else 1
            self.L.recv(self.ref(part, *d, half), (self.name, part, first, k, "s2", s), self.nb(part, first, 4 - s), self.name)
    def stages(self, own):
        def a():
            self.s1(0, True, 0, own)
            self.s1(0, False, 0, own)
        def b():
            self.xrecv()
            self.s1(1, True, 0)
            self.s1(1, False, 0)
        def c():
            for part in (0, 1):
                self.s2(part, True, 0, 1)
                self.s2(part, True, 0, 3)
        def d():
            for k in (1, 3):
                self.s1(0, False, k); self.s1(1, False, k)
        def e():
            self.s3(0, True, 0); self.s1(0, False, 2)
            self.s3(1, True, 0); self.s1(1, False, 2)
        def fw(k):
            def f():
                for part in (0, 1):
                    self.s2(part, False, k, 1); self.s2(part, False, k, 3)
            return f
        def fin(k):
            def f():
                for part in (0, 1):
                    self.s3(part, False, k)
            return f
        return [a, b, c, d, e, fw(0), fw(1), fin(0), fw(3), fin(1), fw(2), fin(3), fin(2)]
    def sent(self):
        m = self.me
        self.L.sent(self.G.at[pl.ds(0, 31)], self.name, (self.name, "x"), {"grp": m["g"], "fsdp": m["f"] + 1 - 2 * m["x"]})

def greet(devs):
    b = pltpu.get_barrier_semaphore()
    for d in devs:
        pl.semaphore_signal(b, inc=1, device_id=d, device_id_type=MESH)
    return len(devs)


def meet(count):
    pl.semaphore_wait(pltpu.get_barrier_semaphore(), count)


def neighbours(me):
    m = me
    out = [{"grp": m["g"], "fsdp": m["f"] + 1 - 2 * m["x"]}]
    for d in (1, 3):
        out.append({"grp": m["g"], "fsdp": (m["y"] * 4 + (m["z"] + d) % 4) * 2 + m["x"]})
        out.append({"grp": m["g"], "fsdp": (((m["y"] + d) % 4) * 4 + m["z"]) * 2 + m["x"]})
    return out


class TwoStep:
    def __init__(self, L, me, name, parts, r0, r1, s1, r2):
        self.L, self.me, self.name = L, me, name
        self.parts, self.r, self.s1, self.r2 = parts, (r0, r1), s1, r2
        self.sib = {"grp": me["g"] + 1 - 2 * me["core"], "fsdp": me["f"]}
        self.opp = {"grp": (1 - me["hi"]) * 2 + me["core"], "fsdp": me["f"]}
    def order(self):
        hi, core = self.me["hi"], self.me["core"]
        return [2 * (1 - hi) + 1 - core, 2 * hi + 1 - core, 2 * (1 - hi) + core, 2 * hi + core]
    def start(self, j):
        self.L.send(self.parts.at[self.order()[j]], self.r[j], (self.name, "c", j), self.sib)
    def mid(self):
        m = self.me
        self.L.recv(self.r[0], (self.name, "c", 0), self.sib)
        for i in range(self.s1.shape[0] // 32):
            rows = pl.ds(i * 32, 32)
            self.s1[rows] = (self.parts[2 * (1 - m["hi"]) + m["core"], rows].astype(F32) + self.r[0][rows].astype(F32)).astype(BF)
        self.L.send(self.s1, self.r2, (self.name, "o"), self.opp)
    def end(self):
        self.L.recv(self.r[1], (self.name, "c", 1), self.sib)
        self.L.recv(self.r2, (self.name, "o"), self.opp)
    def total(self, rows):
        m = self.me
        return self.parts[2 * m["hi"] + m["core"], rows].astype(F32) + self.r[1][rows].astype(F32) + self.r2[rows].astype(F32)


def along_x(me, d):
    X = (me["hi"] * 2 + me["x"] + d) % 4
    return X // 2, X % 2


def same_core(me, d):
    hi, x = along_x(me, d)
    return dev(hi, me["core"], me["y"], me["z"], x)


class Eight:
    def __init__(self, L, me, name, E, rows):
        self.L, self.me, self.name, self.E, self.rows = L, me, name, E, rows
        self.sib = {"grp": me["g"] + 1 - 2 * me["core"], "fsdp": me["f"]}
    def ref(self, d, core, half=None):
        hi, x = along_x(self.me, d)
        r = self.E.at[x, hi * 2 + core]
        if half is None:
            return r
        h = self.rows // 2
        return r.at[pl.ds(half * h, h)]
    def start(self):
        r = self.ref(0, self.me["core"])
        for s in (1, 3):
            self.L.send(r, r, (self.name, "s1", s), same_core(self.me, s))
        self.L.send(r, r, (self.name, "sib", 0), self.sib)
    def mid(self):
        c = self.me["core"]
        for s in (1, 3):
            r = self.ref(4 - s, c)
            self.L.recv(r, (self.name, "s1", s), same_core(self.me, s))
            half = 0 if s == 1 else 1
            rh = self.ref(4 - s, c, half)
            self.L.send(rh, rh, (self.name, "s2", s), same_core(self.me, s))
            self.L.send(r, r, (self.name, "sib", 4 - s), self.sib)
    def mid2(self):
        c = self.me["core"]
        for s in (1, 3):
            half = 0 if s == 1 else 1
            rh = self.ref(2, c, half)
            self.L.recv(rh, (self.name, "s2", s), same_core(self.me, s))
            self.L.send(rh, rh, (self.name, "sib2", s), self.sib)
    def end(self):
        oc = 1 - self.me["core"]
        for d in (0, 1, 3):
            self.L.recv(self.ref(d, oc), (self.name, "sib", d), self.sib)
        for s in (1, 3):
            self.L.recv(self.ref(2, oc, 0 if s == 1 else 1), (self.name, "sib2", s), self.sib)


def eight_others(me):
    out = []
    for d in range(4):
        hi, x = along_x(me, d)
        for c in (0, 1):
            if d == 0 and c == 0:
                continue
            core = 1 - me["core"] if c == 1 else me["core"]
            out.append(((d, c), dev(hi, core, me["y"], me["z"], x), (x, hi * 2 + core)))
    return out


class Scatter:
    def __init__(self, L, me, name, D, ra, rb, rx):
        self.L, self.me, self.name, self.D, self.ra, self.rb, self.rx = L, me, name, D, ra, rb, rx
        self.rows = D.shape[1]
    def axis(self, part, stage):
        m = self.me
        own = m["x"] == 0 if part == 0 else m["x"] == 1
        return own if stage == 1 else jnp.logical_not(own)
    def nb(self, part, stage, d):
        m = self.me
        use_z = self.axis(part, stage)
        zi = jnp.where(use_z, (m["z"] + d) % 4, m["z"])
        yi = jnp.where(use_z, m["y"], (m["y"] + d) % 4)
        return {"fsdp": (yi * 4 + zi) * 2 + m["x"], "grp": m["g"]}
    def ref(self, part, stage, k, d, half=None):
        m = self.me
        use_z = self.axis(part, stage)
        dz = jnp.where(use_z, d, k)
        dy = jnp.where(use_z, k, d)
        px = m["x"] if part == 0 else 1 - m["x"]
        b = self.D.at[(((m["y"] + dy) % 4) * 4 + (m["z"] + dz) % 4) * 2 + px]
        if half is None:
            return b
        h = self.rows // 2
        return b.at[pl.ds(half * h, h)]
    def slot(self, stage, k):
        return k if stage == 0 else 4
    def far(self, part, stage, k):
        h = self.rows // 2
        for s in (1, 3):
            half = 0 if s == 1 else 1
            self.L.send(self.ref(part, stage, k, 2, half), self.ra.at[part, self.slot(stage, k), half], (self.name, part, stage, k, "far", s), self.nb(part, stage, s), self.name)
    def near(self, part, stage, k):
        h = self.rows // 2
        for s in (1, 3):
            half = 0 if s == 1 else 1
            buf = self.ra.at[part, self.slot(stage, k), half]
            self.L.recv(buf, (self.name, part, stage, k, "far", s), self.nb(part, stage, 4 - s), self.name)
            r = self.ref(part, stage, k, s, half)
            r[...] = (r[...].astype(F32) + buf[...].astype(F32)).astype(BF)
            self.L.send(self.ref(part, stage, k, s), self.rb.at[part, self.slot(stage, k), half], (self.name, part, stage, k, "near", s), self.nb(part, stage, s), self.name)
    def total(self, part, stage, k):
        for s in (1, 3):
            half = 0 if s == 1 else 1
            self.L.recv(self.rb.at[part, self.slot(stage, k), half], (self.name, part, stage, k, "near", s), self.nb(part, stage, 4 - s), self.name)
        b = self.rb.at[part, self.slot(stage, k)]
        return self.ref(part, stage, k, 0)[...].astype(F32) + b[0].astype(F32) + b[1].astype(F32)
    def fold(self, part, stage, k):
        t = self.total(part, stage, k)
        self.ref(part, stage, k, 0)[...] = t.astype(BF)
    def partner(self):
        m = self.me
        return {"grp": m["g"], "fsdp": m["f"] + 1 - 2 * m["x"]}
    def xsend(self):
        self.fold(1, 1, 0)
        self.L.send(self.ref(1, 1, 0, 0), self.rx, (self.name, "x"), self.partner(), self.name)
    def result(self):
        t = self.total(0, 1, 0)
        self.L.recv(self.rx, (self.name, "x"), self.partner(), self.name)
        return t + self.rx[...].astype(F32)
    def stages(self):
        def a():
            for k in (2, 1, 3, 0):
                for part in (1, 0):
                    self.far(part, 0, k)
        def b(k):
            def f():
                for part in (1, 0):
                    self.near(part, 0, k)
            return f
        def c(k):
            def f():
                for part in (1, 0):
                    self.fold(part, 0, k)
                    if k == 2:
                        self.far(part, 1, 0)
            return f
        def d():
            for part in (1, 0):
                self.near(part, 1, 0)
        return [a, b(2), b(1), c(2), b(3), c(1), b(0), c(3), d, c(0), self.xsend]
    def sent(self):
        self.L.sent(self.D.at[pl.ds(0, 31)], self.name, (self.name, "x"), self.partner())


def wait_bytes(like, send_sem, recv_sem, devid, recv=True, send=True):
    c = pltpu.make_async_remote_copy(src_ref=like, dst_ref=like, send_sem=send_sem, recv_sem=recv_sem, device_id=devid, device_id_type=MESH)
    if recv:
        c.wait_recv()
    if send:
        c.wait_send()


def dot(a, b, ca, cb):
    return lax.dot_general(a, b, (((ca,), (cb,)), ((), ())), preferred_element_type=F32)


class Refs:
    pass


P_IN = ["lens", "counts", "scap", "tgain", "fgain", "cs_h", "tq_h", "tk_h", "tv_h", "bias_h", "tout_h", "vid_h", "grad_h", "ck_h", "cv_h", "cq_h", "co_h"]
P_OUT = {
    "qb": ((256, 384), BF),
    "da": ((256, 384), BF),
    "ks": ((2, 384, 384), BF),
    "mu": ((256, 1), F32),
    "inv": ((256, 1), F32),
}
P_FAR = {
    "gq": ((32, 192, 384), BF),
    "vnT": ((3072, 256), BF),
    "gradT": ((3072, 256), BF),
}
P_SCRATCH = {
    "kv": ((2, 128, 384), BF),
    "qo": ((192, 384), BF),
    "cs": ((128, 4096), BF),
    "normed": ((128, 4096), BF),
    "wt": ((2, 4096, 512), BF),
    "bias": ((8, 128, 128), F32),
    "tqkv": ((3, 128, 512), BF),
    "tm": ((128, 512), BF),
    "vid": ((256, 3072), BF),
    "grad": ((256, 3072), BF),
    "vn": ((256, 3072), BF),
    "gw": ((32, 128, 384), BF),
    "parts": ((4, 128, 1024), BF),
    "t0": ((128, 1024), BF),
    "t1": ((128, 1024), BF),
    "t2": ((128, 1024), BF),
    "t3": ((128, 1024), BF),
    "E": ((2, 4, 128, 1024), BF),
    "sscol": ((128, 1), F32),
    "SS": ((2, 4, 8, 128), F32),
    "kvp": ((16, 2, 8, 384), BF),
    "C": ((32, 8, 384), BF),
    "sb": ((32, 3, 8, 384), BF),
    "R": ((32, 3, 8, 384), BF),
}
P_TABLES = {"end": 32, "first": 32, "cap": 96, "samp": 32}
Q_IN = ["edge", "sidx", "qb", "da", "ks", "mu", "inv", "gq_h", "vnT_h", "gradT_h", "vid_h", "grad_h"]
Q_OUT = {
    "updated": ((256, 768), BF),
    "igrad": ((256, 768), BF),
    "qgrad": ((96, 384), F32),
    "ograd": ((96, 384), F32),
    "kgrad": ((128, 384), BF),
    "vgrad": ((128, 384), BF),
}
Q_SCRATCH = {
    "gq": ((32, 192, 384), BF),
    "vnT": ((3072, 256), BF),
    "gradT": ((3072, 256), BF),
    "vid": ((256, 3072), BF),
    "grad": ((256, 3072), BF),
    "att": ((256, 384), BF),
    "dq": ((256, 384), BF),
    "w": ((3, 256, 128), F32),
    "mp": ((3, 256, 384), BF),
    "ms": ((3, 256, 384), BF),
    "T": ((32, 3, 8, 384), BF),
    "Dw": ((32, 96, 384), BF),
    "Dq": ((32, 96, 384), BF),
    "ra1": ((2, 5, 2, 48, 384), BF),
    "rb1": ((2, 5, 2, 96, 384), BF),
    "rx1": ((96, 384), BF),
    "ra2": ((2, 5, 2, 48, 384), BF),
    "rb2": ((2, 5, 2, 96, 384), BF),
    "rx2": ((96, 384), BF),
    "op": ((4, 256, 768), BF),
    "o0": ((256, 768), BF),
    "o1": ((256, 768), BF),
    "o2": ((256, 768), BF),
    "o3": ((256, 768), BF),
    "dn": ((4, 256, 768), BF),
    "n0": ((256, 768), BF),
    "n1": ((256, 768), BF),
    "n2": ((256, 768), BF),
    "n3": ((256, 768), BF),
    "scol": ((2, 256, 1), F32),
    "stat": ((4, 2, 8, 256), F32),
    "RG": ((99, 8, 384), BF),
    "CG": ((32, 8, 384), BF),
    "KV": ((32, 8, 384), BF),
}


def fill_tables(r):
    def total(s, acc):
        acc = acc + r.counts[s]
        r.end[s] = acc
        return acc
    lax.fori_loop(0, 32, total, jnp.int32(0))

    @pl.loop(0, 32)
    def _(d):
        count = jnp.int32(0)
        for s in range(32):
            count = count + (r.end[s] <= 256 * d).astype(jnp.int32)
        r.first[d] = count
        for t in range(3):
            r.cap[d * 3 + t] = r.scap[jnp.minimum(count + t, 31)]

    @pl.loop(0, 32)
    def _(c):
        s = jnp.int32(0)
        for t in range(32):
            s = s + jnp.where(r.scap[t] == c, t, 0)
        s = jnp.minimum(s, 31)
        stop = r.end[s]
        d0 = (stop - r.counts[s]) // 256
        for m in range(5):
            d = d0 + m
            valid = (d < 32) & (d * 256 < stop)
            r.sidx[c * 5 + m] = jnp.clip(jnp.where(valid, 3 * d + s - r.first[jnp.minimum(d, 31)], 96), 0, 96)


def named(refs, names):
    r = Refs()
    for n, ref in zip(names, refs):
        setattr(r, n, ref)
    return r


def encode(*refs):
    r = named(refs, P_IN + list(P_OUT) + [n + "_o" for n in P_FAR] + ["edge", "sidx"] + list(P_FAR) + list(P_SCRATCH) + list(P_TABLES) + ["sems", "lsem", "asem"])
    me = place()
    f, g, core, hi = me["f"], me["g"], me["core"], me["hi"]
    fs = [{"grp": g, "fsdp": (f + j) % 32} for j in range(1, 32)]
    count = greet(fs + [{"grp": (g + j) % 4, "fsdp": f // 2 * 2 + x} for j in range(1, 4) for x in range(2)])
    L = Links(r.sems)
    loads = {}

    def load(name, src, dst):
        c = pltpu.make_async_copy(src, dst, r.lsem.at[len(loads)])
        c.start()
        loads[name] = c
    load("ck", r.ck_h, r.kv.at[0])
    load("cv", r.cv_h, r.kv.at[1])
    load("cq", r.cq_h, r.qo.at[pl.ds(0, 96)])
    load("co", r.co_h, r.qo.at[pl.ds(96, 96)])
    load("cs", r.cs_h, r.cs)

    def load_text(a, wh):
        for k in range(2):
            rows = pl.ds(k * 2048, 2048)
            load(("wt", a, k), wh.at[rows], r.wt.at[a % 2, rows])
    load_text(0, r.tq_h)
    load_text(1, r.tk_h)
    load("bias", r.bias_h, r.bias)
    load("vid", r.vid_h, r.vid)
    load("grad", r.grad_h, r.grad)

    others = eight_others(me)
    meet(count)

    A, B = Gather(L, me, "w", r.gw, 128), Gather(L, me, "q", r.gq, 192)
    sa, sb = A.stages(r.kv.at[me["x"]]), B.stages(r.qo)
    for n in ("ck", "cv", "cq", "co"):
        loads[n].wait()
    A.xsend(r.kv.at[1 - me["x"]])
    sa[0]()
    B.xsend(r.qo)
    sb[0]()
    r.gw[f] = r.kv[me["x"]]
    r.gq[f] = r.qo[...]

    loads["cs"].wait()

    @pl.loop(0, 8)
    def _(i):
        rows = pl.ds(i * 16, 16)
        x = r.cs[rows].astype(F32)
        mean_square = jnp.mean(x * x, axis=-1, keepdims=True)
        r.normed[rows] = (x * lax.rsqrt(mean_square + 1e-06) * r.tgain[...]).astype(BF)

    def project(a):
        acc = jnp.zeros((128, 512), F32)
        for k in range(2):
            loads["wt", a, k].wait()
            acc = acc + jnp.dot(r.normed[:, pl.ds(k * 2048, 2048)], r.wt[a % 2, pl.ds(k * 2048, 2048)], preferred_element_type=F32)
        r.tqkv[a] = acc.astype(BF)
    project(0)
    load_text(2, r.tv_h)
    sa[1]()
    project(1)
    for k in range(8):
        load(("wo", k), r.tout_h.at[:, pl.ds(k * 512, 512)], r.wt.at[1, pl.ds(k * 512, 512)])
    sb[1]()
    project(2)
    sa[2]()
    sa[3]()
    loads["bias"].wait()
    lane = lax.broadcasted_iota(jnp.int32, (128, 128), 1)
    valid = lane < r.lens[f]

    def text_pair(p):
        cols = pl.ds(p * 128, 128)
        q, k, v = r.tqkv[0, :, cols], r.tqkv[1, :, cols], r.tqkv[2, :, cols]
        out = []
        for i in range(2):
            qh = jnp.where((lane < 64) == (i == 0), q.astype(F32), 0.0).astype(BF)
            ex = jnp.where(valid, jnp.exp(dot(qh, k, 1, 1) + r.bias[2 * p + i]), 0.0)
            wts = (ex / jnp.sum(ex, axis=-1, keepdims=True)).astype(BF)
            out.append(dot(wts, v, 1, 0))
        r.tm[:, cols] = jnp.where(lane < 64, out[0], out[1]).astype(BF)
    text_pair(0)
    text_pair(1)
    sb[2]()
    sb[3]()
    text_pair(2)
    text_pair(3)
    sa[4]()
    sa[5]()
    for k in range(8):
        loads["wo", k].wait()
    T = TwoStep(L, me, "t", r.parts, r.t0, r.t1, r.t2, r.t3)
    for j, s in enumerate(T.order()):
        for n in range(2):
            cols = pl.ds(n * 512, 512)
            r.parts[s, :, cols] = jnp.dot(r.tm[...], r.wt[1, pl.ds((2 * s + n) * 512, 512)], preferred_element_type=F32).astype(BF)
        if j < 2:
            T.start(j)
    sb[4]()
    sb[5]()
    T.mid()
    sa[6]()
    sb[6]()
    fill_tables(r)
    T.end()

    @pl.loop(0, 8)
    def _(i):
        rows, cols = pl.ds(i * 16, 16), pl.ds(pl.multiple_of(g * 1024, 1024), 1024)
        ts = T.total(rows) + r.cs[rows, cols].astype(F32)
        r.E[me["x"], g, rows] = (ts * r.fgain[:, cols]).astype(BF)
        r.sscol[rows] = jnp.sum(ts * ts, axis=1, keepdims=True)
    X = Eight(L, me, "e", r.E, 128)
    X.start()
    r.SS[me["x"], g] = jnp.broadcast_to(r.sscol[...], (128, 128)).T[:8]
    mine = r.SS.at[me["x"], g]
    for key, d, _ in others:
        L.send(mine, mine, ("ss", (4 - key[0]) % 4, key[1]), d)
    sa[7]()
    sa[8]()

    loads["vid"].wait()

    @pl.loop(0, 16)
    def _(i):
        rows = pl.ds(i * 16, 16)
        v = r.vid[rows].astype(F32)
        mean = jnp.mean(v, axis=-1, keepdims=True)
        center = v - mean
        inverse = lax.rsqrt(jnp.mean(center * center, axis=-1, keepdims=True) + 1e-06)
        r.mu[rows], r.inv[rows] = mean, inverse
        r.vn[rows] = (center * inverse).astype(BF)
    X.mid()
    sb[7]()
    sb[8]()
    loads["grad"].wait()

    @pl.loop(0, 24)
    def _(i):
        lanes = pl.ds(pl.multiple_of(i * 128, 128), 128)
        r.vnT[lanes] = r.vn[:, lanes].T
        r.gradT[lanes] = r.grad[:, lanes].T
    load("vnT_o", r.vnT, r.vnT_o)
    load("gradT_o", r.gradT, r.gradT_o)
    X.mid2()
    for i in range(9, 13):
        sa[i]()
    sb[9]()
    sb[10]()
    X.end()
    for key, d, slot in others:
        L.recv(r.SS.at[slot[0], slot[1]], ("ss", key[0], key[1]), d)

    acc = jnp.zeros((256, 384), F32)
    for k in range(4):
        acc = acc + jnp.dot(r.E[:, k].reshape(256, 1024), r.gw[k * 8 : k * 8 + 8].reshape(1024, 384), preferred_element_type=F32)
    for c in range(2):
        ss = r.SS[c, 0, :1] + r.SS[c, 1, :1] + r.SS[c, 2, :1] + r.SS[c, 3, :1]
        col = jnp.broadcast_to(ss, (128, 128)).T[:, :1]
        r.kvp[:, c] = (acc[c * 128 : c * 128 + 128] * lax.rsqrt(col / 4096 + 1e-06)).reshape(16, 8, 384).astype(BF)

    partner = {"grp": g, "fsdp": (f + 1) % 32}
    yz = f // 2

    @pl.loop(1, 16)
    def _(j):
        to = (yz + j) % 16
        pltpu.make_async_remote_copy(src_ref=r.kvp.at[to], dst_ref=r.C.at[pl.ds(2 * yz, 2)], send_sem=r.asem.at[0], recv_sem=r.asem.at[1], device_id={"grp": g, "fsdp": to * 2 + me["x"]}, device_id_type=MESH).start()
    r.C[pl.ds(2 * yz, 2)] = r.kvp[yz]
    wait_bytes(r.C.at[pl.ds(0, 30)], r.asem.at[0], r.asem.at[1], partner)

    @pl.loop(1, 32)
    def _(j):
        to = (f + j) % 32
        for s in range(3):
            r.sb[to, s] = r.C[r.cap[to * 3 + s]]
        pltpu.make_async_remote_copy(src_ref=r.sb.at[to], dst_ref=r.R.at[f], send_sem=r.asem.at[2], recv_sem=r.asem.at[3], device_id={"grp": g, "fsdp": to}, device_id_type=MESH).start()
    for s in range(3):
        r.R[f, s] = r.C[r.cap[f * 3 + s]]
    for s in sb[11:]:
        s()
    load("gq_o", r.gq, r.gq_o)

    acc = jnp.zeros((256, 384), F32)
    acc2 = jnp.zeros((256, 384), F32)
    for k in range(4):
        cols = pl.ds(k * 768, 768)
        acc = acc + jnp.dot(r.vn[:, cols], r.gq[k * 8 : k * 8 + 8, 0:96].reshape(768, 384), preferred_element_type=F32)
    r.qb[...] = acc.astype(BF)
    for k in range(4):
        cols = pl.ds(k * 768, 768)
        acc2 = acc2 + jnp.dot(r.grad[:, cols], r.gq[k * 8 : k * 8 + 8, 96:192].reshape(768, 384), preferred_element_type=F32)
    r.da[...] = acc2.astype(BF)

    first = r.first[f]
    r.edge[0], r.edge[1] = r.end[jnp.minimum(first, 31)], r.end[jnp.minimum(first + 1, 31)]
    for s in range(3):
        r.edge[2 + s] = r.lens[r.cap[f * 3 + s]]
    wait_bytes(r.R.at[pl.ds(0, 31)], r.asem.at[2], r.asem.at[3], partner)
    for kv in range(2):
        for s in range(3):
            r.ks[kv, pl.ds(s * 128, 128)] = r.R[:, s].reshape(16, 2, 8, 384)[:, kv].astype(F32).reshape(128, 384).astype(BF)
    A.sent()
    B.sent()
    L.drain()
    for n in P_FAR:
        loads[n + "_o"].wait()


def attend(*refs):
    r = named(refs, Q_IN + list(Q_OUT) + list(Q_SCRATCH) + ["sems", "lsem", "asem"])
    me = place()
    f, g, core, hi = me["f"], me["g"], me["core"], me["hi"]
    count = greet([{"grp": g, "fsdp": (f + j) % 32} for j in range(1, 32)] + [{"grp": (g + j) % 4, "fsdp": f} for j in range(1, 4)])
    L = Links(r.sems)
    partner = {"grp": g, "fsdp": (f + 1) % 32}
    loads = {}
    for i, n in enumerate(("gradT", "gq", "vnT", "vid", "grad")):
        loads[n] = pltpu.make_async_copy(getattr(r, n + "_h"), getattr(r, n), r.lsem.at[i])
        loads[n].start()
    position = lax.broadcasted_iota(jnp.int32, (256, 128), 0) + f * 256
    slot = (position >= r.edge[0]).astype(jnp.int32) + (position >= r.edge[1]).astype(jnp.int32)
    token_len = jnp.where(slot == 0, r.edge[2], jnp.where(slot == 1, r.edge[3], r.edge[4]))
    token_valid = lax.broadcasted_iota(jnp.int32, (256, 128), 1) < token_len
    scale = 1.0 / math.sqrt(HEAD_SIZE)

    def pick(a):
        return jnp.where(slot == 0, a[:, 0:128], jnp.where(slot == 1, a[:, 128:256], a[:, 256:384]))

    def placed(a):
        return jnp.concatenate([jnp.where(slot == s, a, 0.0).astype(BF) for s in range(3)], axis=1)

    for h in range(3):
        cols = pl.ds(h * 128, 128)
        scores = pick(dot(r.qb[:, cols], r.ks[0, :, cols], 1, 1)) * scale
        ex = jnp.where(token_valid, jnp.exp(scores), 0.0)
        w = ex / jnp.sum(ex, axis=-1, keepdims=True)
        r.w[h] = w
        mp = placed(w)
        r.mp[h] = mp
        r.att[:, cols] = dot(mp, r.ks[1, :, cols], 1, 0).astype(BF)

    def weight_grad(D, left, right):
        @pl.loop(0, 8)
        def _(i):
            rows = pl.ds(i * 384, 384)
            D[pl.ds(i * 4, 4)] = dot(left[rows], right[...], 1, 0).reshape(4, 96, 384).astype(BF)
    loads["gradT"].wait()
    weight_grad(r.Dw, r.gradT, r.att)
    S1 = Scatter(L, me, "d1", r.Dw, r.ra1, r.rb1, r.rx1)
    S2 = Scatter(L, me, "d2", r.Dq, r.ra2, r.rb2, r.rx2)
    s1, s2 = S1.stages(), S2.stages()
    meet(count)
    s1[0]()
    loads["gq"].wait()
    O = TwoStep(L, me, "o", r.op, r.o0, r.o1, r.o2, r.o3)
    N = TwoStep(L, me, "n", r.dn, r.n0, r.n1, r.n2, r.n3)
    for j, s in enumerate(O.order()):
        r.op[s] = dot(r.att[...], r.gq[pl.ds(s * 8, 8), 96:192].reshape(768, 384), 1, 1).astype(BF)
        if j < 2:
            O.start(j)
    s1[1]()

    for h in range(3):
        cols = pl.ds(h * 128, 128)
        d_probs = pick(dot(r.da[:, cols], r.ks[1, :, cols], 1, 1))
        w = r.w[h]
        ds = w * (d_probs - jnp.sum(w * d_probs, axis=-1, keepdims=True)) * scale
        ms = placed(ds)
        r.ms[h] = ms
        r.dq[:, cols] = dot(ms, r.ks[0, :, cols], 1, 0).astype(BF)
    O.mid()
    loads["vnT"].wait()
    weight_grad(r.Dq, r.vnT, r.dq)
    s2[0]()
    s1[2]()
    s1[3]()
    for j, s in enumerate(N.order()):
        r.dn[s] = dot(r.dq[...], r.gq[pl.ds(s * 8, 8), 0:96].reshape(768, 384), 1, 1).astype(BF)
        if j < 2:
            N.start(j)
    for h in range(3):
        cols = pl.ds(h * 128, 128)
        kt = dot(r.ms[h], r.qb[:, cols], 0, 0)
        vt = dot(r.mp[h], r.da[:, cols], 0, 0)
        for s in range(3):
            rows = slice(s * 128, s * 128 + 128)
            both = jnp.stack([kt[rows].reshape(16, 8, 128), vt[rows].reshape(16, 8, 128)], axis=1)
            r.T[:, s, :, cols] = both.reshape(32, 8, 128).astype(BF)

    @pl.loop(1, 32)
    def _(j):
        to = (f + j) % 32
        pltpu.make_async_remote_copy(src_ref=r.T.at[to], dst_ref=r.RG.at[pl.ds(3 * f, 3)], send_sem=r.asem.at[4], recv_sem=r.asem.at[5], device_id={"grp": g, "fsdp": to}, device_id_type=MESH).start()
    N.mid()
    for i in range(4, 8):
        s1[i]()
    s2[1]()
    s2[2]()
    s1[8]()
    for i in (3, 4):
        s2[i]()
    for i in (9, 10):
        s1[i]()
    for i in (5, 6, 7):
        s2[i]()
    r.RG[pl.ds(96, 3)] = jnp.zeros((3, 8, 384), BF)
    r.RG[pl.ds(3 * f, 3)] = r.T[f]
    wait_bytes(r.RG.at[pl.ds(0, 93)], r.asem.at[4], r.asem.at[5], partner)

    @pl.loop(0, 32)
    def _(c):
        acc = r.RG[r.sidx[c * 5]].astype(F32)
        for m in range(1, 5):
            acc = acc + r.RG[r.sidx[c * 5 + m]].astype(F32)
        r.CG[c] = acc.astype(BF)

    @pl.loop(1, 32)
    def _(j):
        to = (f + j) % 32
        pltpu.make_async_remote_copy(src_ref=r.CG.at[to], dst_ref=r.KV.at[f], send_sem=r.asem.at[6], recv_sem=r.asem.at[7], device_id={"grp": g, "fsdp": to}, device_id_type=MESH).start()
    r.KV[f] = r.CG[f]
    s2[8]()
    O.end()
    loads["vid"].wait()
    loads["grad"].wait()
    cols = pl.ds(pl.multiple_of(g * 768, 768), 768)

    @pl.loop(0, 16)
    def _(i):
        rows = pl.ds(i * 16, 16)
        r.updated[rows] = (r.vid[rows, cols].astype(F32) + O.total(rows)).astype(BF)
    N.end()

    def video_hat(rows):
        return (r.vid[rows, cols].astype(F32) - r.mu[rows]) * r.inv[rows]

    @pl.loop(0, 16)
    def _(i):
        rows = pl.ds(i * 16, 16)
        t = N.total(rows)
        r.scol[0, rows] = jnp.sum(t, axis=1, keepdims=True)
        r.scol[1, rows] = jnp.sum(t * video_hat(rows), axis=1, keepdims=True)
    for k in range(2):
        r.stat[g, k] = jnp.broadcast_to(r.scol[k], (256, 128)).T[:8]
    grp = [{"grp": (g + j) % 4, "fsdp": f} for j in range(1, 4)]
    for j in range(1, 4):
        L.send(r.stat.at[g], r.stat.at[g], ("st", j), grp[j - 1])
    for i in (9, 10):
        s2[i]()
    r.ograd[...] = S1.result()
    for j in range(1, 4):
        L.recv(r.stat.at[(g + 4 - j) % 4], ("st", j), grp[3 - j])
    for k in range(2):
        s = r.stat[0, k, :1] + r.stat[1, k, :1] + r.stat[2, k, :1] + r.stat[3, k, :1]
        r.scol[k] = jnp.broadcast_to(s / 3072, (128, 256)).T[:, :1]

    @pl.loop(0, 16)
    def _(i):
        rows = pl.ds(i * 16, 16)
        d = N.total(rows) - r.scol[0, rows] - video_hat(rows) * r.scol[1, rows]
        r.igrad[rows] = (r.grad[rows, cols].astype(F32) + r.inv[rows] * d).astype(BF)
    wait_bytes(r.KV.at[pl.ds(0, 31)], r.asem.at[6], r.asem.at[7], partner)
    r.kgrad[...] = r.KV[...].reshape(16, 2, 8, 384)[:, 0].astype(F32).reshape(128, 384).astype(BF)
    r.vgrad[...] = r.KV[...].reshape(16, 2, 8, 384)[:, 1].astype(F32).reshape(128, 384).astype(BF)
    r.qgrad[...] = S2.result()
    S1.sent()
    S2.sent()
    L.drain()


def hand_over(*refs):
    held, sem = refs[12:18], refs[18]
    into = [pltpu.make_async_copy(refs[i], held[i], sem.at[i]) for i in range(6)]
    out = [pltpu.make_async_copy(held[i], refs[6 + i], sem.at[6 + i]) for i in range(6)]
    for c in into:
        c.start()
    for i in range(6):
        into[i].wait()
        out[i].start()
    for c in out:
        c.wait()


def local(caption_states, caption_lens, text_gain, text_query, text_key, text_value, text_bias, text_out, final_gain, cross_key, cross_value, video_states, video_counts, sample_caption, cross_query, cross_out, out_grad):
    V, M, A = pltpu.VMEM, pltpu.SMEM, pl.ANY

    def call(kernel, name, cid, args, spaces, outs, far, tables, scratch, smem):
        return pl.pallas_call(
            kernel,
            out_shape=tuple(jax.ShapeDtypeStruct(s, d) for s, d in (outs | far).values()) + tuple(jax.ShapeDtypeStruct((n,), jnp.int32) for n in tables),
            in_specs=[pl.BlockSpec(memory_space=s) for s in spaces],
            out_specs=tuple(pl.BlockSpec(memory_space=V) for _ in outs) + tuple(pl.BlockSpec(memory_space=A) for _ in far) + tuple(pl.BlockSpec(memory_space=M) for _ in tables),
            scratch_shapes=[V(s, d) for s, d in (far | scratch).values()] + [M((n,), jnp.int32) for n in smem] + [DMA((128,)), DMA((32,)), DMA((8,))],
            compiler_params=pltpu.CompilerParams(collective_id=cid, has_side_effects=True, vmem_limit_bytes=58 << 20),
            name=name,
        )(*args)
    args = [caption_lens, video_counts, sample_caption, text_gain[None], final_gain[None], caption_states.reshape(128, 4096), text_query, text_key, text_value, text_bias, text_out, video_states, out_grad, cross_key, cross_value, cross_query, cross_out.T]
    qb, da, ks, mu, inv, gq, vnT, gradT, edge, sidx = call(encode, "encode", 0, args, [M] * 3 + [V] * 2 + [A] * 12, P_OUT, P_FAR, (8, 160), P_SCRATCH, P_TABLES.values())
    args = [edge, sidx, qb, da, ks, mu, inv, gq, vnT, gradT, video_states, out_grad]
    outs = call(attend, "attend", 1, args, [M] * 2 + [V] * 5 + [A] * 5, Q_OUT, {}, (), Q_SCRATCH, ())
    updated, igrad, qgrad, ograd, kgrad, vgrad = pl.pallas_call(
        hand_over,
        out_shape=tuple(jax.ShapeDtypeStruct(s, d) for s, d in Q_OUT.values()),
        in_specs=[pl.BlockSpec(memory_space=A)] * 6,
        out_specs=(pl.BlockSpec(memory_space=A),) * 6,
        scratch_shapes=[V(s, d) for s, d in Q_OUT.values()] + [DMA((12,))],
        name="hand_over",
    )(*outs)
    return updated, igrad, qgrad, ograd.T, kgrad[None], vgrad[None]


def solution(mesh):
    in_specs = (P("fsdp"), P(), P(), P(None, "grp"), P(None, "grp"), P(None, "grp"), P("grp"), P("grp"), P(), P("fsdp", "grp"), P("fsdp", "grp"), P("fsdp"), P(), P(), P("fsdp", "grp"), P("grp", "fsdp"), P("fsdp"))
    out_specs = (P("fsdp", "grp"), P("fsdp", "grp"), P("fsdp", "grp"), P("grp", "fsdp"), P("fsdp", None, "grp"), P("fsdp", None, "grp"))
    return jax.shard_map(local, mesh=mesh, in_specs=in_specs, out_specs=out_specs, check_vma=False)
```

```python
import math

import jax
import jax.numpy as jnp
from jax import lax
from jax.experimental import pallas as pl
from jax.experimental.pallas import tpu as pltpu
from jax.sharding import PartitionSpec as P
MESH = pl.DeviceIdType.MESH
BF, F32 = jnp.bfloat16, jnp.float32
DMA = pltpu.SemaphoreType.DMA
HEAD_SIZE = 128

class Links:
    def __init__(self, sems):
        self.sems, self.keys, self.pending = sems, {}, []
    def sem(self, key):
        return self.sems.at[self.keys.setdefault(key, len(self.keys))]
    def copy(self, src, dst, key, dev, group=None):
        send = self.sem(("s", group if group else key))
        return pltpu.make_async_remote_copy(src_ref=src, dst_ref=dst, send_sem=send, recv_sem=self.sem(("r", key)), device_id=dev, device_id_type=MESH)
    def send(self, src, dst, key, dev, group=None):
        c = self.copy(src, dst, key, dev, group)
        c.start()
        if group is None:
            self.pending.append(c)
    def recv(self, dst, key, dev, group=None):
        self.copy(dst, dst, key, dev, group).wait_recv()
    def sent(self, blocks, group, key, dev):
        self.copy(blocks, blocks, key, dev, group).wait_send()
    def drain(self):
        for c in self.pending:
            c.wait_send()
        self.pending = []

def place():
    g, f = lax.axis_index("grp"), lax.axis_index("fsdp")
    return dict(hi=g // 2, core=g % 2, y=f // 8, z=(f // 2) % 4, x=f % 2, g=g, f=f)

def dev(hi, core, y, z, x):
    return {"grp": hi * 2 + core, "fsdp": (y * 4 + z) * 2 + x}

class Gather:
    def __init__(self, L, me, name, G, rows):
        self.L, self.me, self.name, self.G, self.rows = L, me, name, G, rows
    def nb(self, part, first, d):
        m = self.me
        use_z = (m["x"] == 0) if (part == 0) == first else (m["x"] == 1)
        zi = jnp.where(use_z, (m["z"] + d) % 4, m["z"])
        yi = jnp.where(use_z, m["y"], (m["y"] + d) % 4)
        return {"fsdp": (yi * 4 + zi) * 2 + m["x"], "grp": m["g"]}
    def idx(self, part, d1, d2):
        m = self.me
        use_z = (m["x"] == 0) if part == 0 else (m["x"] == 1)
        dz = jnp.where(use_z, d1, d2)
        dy = jnp.where(use_z, d2, d1)
        px = m["x"] if part == 0 else 1 - m["x"]
        return (((m["y"] + dy) % 4) * 4 + (m["z"] + dz) % 4) * 2 + px
    def ref(self, part, d1, d2, half=None):
        b = self.G.at[self.idx(part, d1, d2)]
        if half is None:
            return b
        h = self.rows // 2
        return b.at[pl.ds(half * h, h)]
    def xsend(self, src):
        m = self.me
        self.L.send(src, self.G.at[m["f"]], (self.name, "x"), {"grp": m["g"], "fsdp": m["f"] + 1 - 2 * m["x"]}, self.name)
    def xrecv(self):
        m = self.me
        self.L.recv(self.ref(1, 0, 0), (self.name, "x"), {"grp": m["g"], "fsdp": m["f"] + 1 - 2 * m["x"]}, self.name)
    def s1(self, part, first, k, src=None):
        d = (0, 0) if first else (k, 0)
        r = self.ref(part, *d)
        src = r if src is None else src
        for s in (1, 3):
            self.L.send(src, r, (self.name, part, first, k, "s1", s), self.nb(part, first, s), self.name)
    def s2(self, part, first, k, s):
        o = 4 - s
        d = (o, 0) if first else (k, o)
        self.L.recv(self.ref(part, *d), (self.name, part, first, k, "s1", s), self.nb(part, first, o), self.name)
        half = 0 if s == 1 else 1
        r = self.ref(part, *d, half)
        self.L.send(r, r, (self.name, part, first, k, "s2", s), self.nb(part, first, s), self.name)
    def s3(self, part, first, k):
        d = (2, 0) if first else (k, 2)
        for s in (1, 3):
            half = 0 if s == 1 else 1
            self.L.recv(self.ref(part, *d, half), (self.name, part, first, k, "s2", s), self.nb(part, first, 4 - s), self.name)
    def stages(self, own):
        def a():
            self.s1(0, True, 0, own)
            self.s1(0, False, 0, own)
        def b():
            self.xrecv()
            self.s1(1, True, 0)
            self.s1(1, False, 0)
        def c():
            for part in (0, 1):
                self.s2(part, True, 0, 1)
                self.s2(part, True, 0, 3)
        def d():
            for k in (1, 3):
                self.s1(0, False, k); self.s1(1, False, k)
        def e():
            self.s3(0, True, 0); self.s1(0, False, 2)
            self.s3(1, True, 0); self.s1(1, False, 2)
        def fw(k):
            def f():
                for part in (0, 1):
                    self.s2(part, False, k, 1); self.s2(part, False, k, 3)
            return f
        def fin(k):
            def f():
                for part in (0, 1):
                    self.s3(part, False, k)
            return f
        return [a, b, c, d, e, fw(0), fw(1), fin(0), fw(3), fin(1), fw(2), fin(3), fin(2)]
    def sent(self):
        m = self.me
        self.L.sent(self.G.at[pl.ds(0, 31)], self.name, (self.name, "x"), {"grp": m["g"], "fsdp": m["f"] + 1 - 2 * m["x"]})

def greet(devs):
    b = pltpu.get_barrier_semaphore()
    for d in devs:
        pl.semaphore_signal(b, inc=1, device_id=d, device_id_type=MESH)
    return len(devs)


def meet(count):
    pl.semaphore_wait(pltpu.get_barrier_semaphore(), count)


def neighbours(me):
    m = me
    out = [{"grp": m["g"], "fsdp": m["f"] + 1 - 2 * m["x"]}]
    for d in (1, 3):
        out.append({"grp": m["g"], "fsdp": (m["y"] * 4 + (m["z"] + d) % 4) * 2 + m["x"]})
        out.append({"grp": m["g"], "fsdp": (((m["y"] + d) % 4) * 4 + m["z"]) * 2 + m["x"]})
    return out


class TwoStep:
    def __init__(self, L, me, name, parts, r0, r1, s1, r2):
        self.L, self.me, self.name = L, me, name
        self.parts, self.r, self.s1, self.r2 = parts, (r0, r1), s1, r2
        self.sib = {"grp": me["g"] + 1 - 2 * me["core"], "fsdp": me["f"]}
        self.opp = {"grp": (1 - me["hi"]) * 2 + me["core"], "fsdp": me["f"]}
    def order(self):
        hi, core = self.me["hi"], self.me["core"]
        return [2 * (1 - hi) + 1 - core, 2 * hi + 1 - core, 2 * (1 - hi) + core, 2 * hi + core]
    def start(self, j):
        self.L.send(self.parts.at[self.order()[j]], self.r[j], (self.name, "c", j), self.sib)
    def mid(self):
        m = self.me
        self.L.recv(self.r[0], (self.name, "c", 0), self.sib)
        for i in range(self.s1.shape[0] // 32):
            rows = pl.ds(i * 32, 32)
            self.s1[rows] = (self.parts[2 * (1 - m["hi"]) + m["core"], rows].astype(F32) + self.r[0][rows].astype(F32)).astype(BF)
        self.L.send(self.s1, self.r2, (self.name, "o"), self.opp)
    def end(self):
        self.L.recv(self.r[1], (self.name, "c", 1), self.sib)
        self.L.recv(self.r2, (self.name, "o"), self.opp)
    def total(self, rows):
        m = self.me
        return self.parts[2 * m["hi"] + m["core"], rows].astype(F32) + self.r[1][rows].astype(F32) + self.r2[rows].astype(F32)


def along_x(me, d):
    X = (me["hi"] * 2 + me["x"] + d) % 4
    return X // 2, X % 2


def same_core(me, d):
    hi, x = along_x(me, d)
    return dev(hi, me["core"], me["y"], me["z"], x)


class Eight:
    def __init__(self, L, me, name, E, rows):
        self.L, self.me, self.name, self.E, self.rows = L, me, name, E, rows
        self.sib = {"grp": me["g"] + 1 - 2 * me["core"], "fsdp": me["f"]}
    def ref(self, d, core, half=None):
        hi, x = along_x(self.me, d)
        r = self.E.at[x, hi * 2 + core]
        if half is None:
            return r
        h = self.rows // 2
        return r.at[pl.ds(half * h, h)]
    def start(self):
        r = self.ref(0, self.me["core"])
        for s in (1, 3):
            self.L.send(r, r, (self.name, "s1", s), same_core(self.me, s))
        self.L.send(r, r, (self.name, "sib", 0), self.sib)
    def mid(self):
        c = self.me["core"]
        for s in (1, 3):
            r = self.ref(4 - s, c)
            self.L.recv(r, (self.name, "s1", s), same_core(self.me, s))
            half = 0 if s == 1 else 1
            rh = self.ref(4 - s, c, half)
            self.L.send(rh, rh, (self.name, "s2", s), same_core(self.me, s))
            self.L.send(r, r, (self.name, "sib", 4 - s), self.sib)
    def mid2(self):
        c = self.me["core"]
        for s in (1, 3):
            half = 0 if s == 1 else 1
            rh = self.ref(2, c, half)
            self.L.recv(rh, (self.name, "s2", s), same_core(self.me, s))
            self.L.send(rh, rh, (self.name, "sib2", s), self.sib)
    def end(self):
        oc = 1 - self.me["core"]
        for d in (0, 1, 3):
            self.L.recv(self.ref(d, oc), (self.name, "sib", d), self.sib)
        for s in (1, 3):
            self.L.recv(self.ref(2, oc, 0 if s == 1 else 1), (self.name, "sib2", s), self.sib)


def eight_others(me):
    out = []
    for d in range(4):
        hi, x = along_x(me, d)
        for c in (0, 1):
            if d == 0 and c == 0:
                continue
            core = 1 - me["core"] if c == 1 else me["core"]
            out.append(((d, c), dev(hi, core, me["y"], me["z"], x), (x, hi * 2 + core)))
    return out


class Scatter:
    def __init__(self, L, me, name, D, ra, rb, rx):
        self.L, self.me, self.name, self.D, self.ra, self.rb, self.rx = L, me, name, D, ra, rb, rx
        self.rows = D.shape[1]
    def axis(self, part, stage):
        m = self.me
        own = m["x"] == 0 if part == 0 else m["x"] == 1
        return own if stage == 1 else jnp.logical_not(own)
    def nb(self, part, stage, d):
        m = self.me
        use_z = self.axis(part, stage)
        zi = jnp.where(use_z, (m["z"] + d) % 4, m["z"])
        yi = jnp.where(use_z, m["y"], (m["y"] + d) % 4)
        return {"fsdp": (yi * 4 + zi) * 2 + m["x"], "grp": m["g"]}
    def ref(self, part, stage, k, d, half=None):
        m = self.me
        use_z = self.axis(part, stage)
        dz = jnp.where(use_z, d, k)
        dy = jnp.where(use_z, k, d)
        px = m["x"] if part == 0 else 1 - m["x"]
        b = self.D.at[(((m["y"] + dy) % 4) * 4 + (m["z"] + dz) % 4) * 2 + px]
        if half is None:
            return b
        h = self.rows // 2
        return b.at[pl.ds(half * h, h)]
    def slot(self, stage, k):
        return k if stage == 0 else 4
    def far(self, part, stage, k):
        h = self.rows // 2
        for s in (1, 3):
            half = 0 if s == 1 else 1
            self.L.send(self.ref(part, stage, k, 2, half), self.ra.at[part, self.slot(stage, k), half], (self.name, part, stage, k, "far", s), self.nb(part, stage, s), self.name)
    def near(self, part, stage, k):
        h = self.rows // 2
        for s in (1, 3):
            half = 0 if s == 1 else 1
            buf = self.ra.at[part, self.slot(stage, k), half]
            self.L.recv(buf, (self.name, part, stage, k, "far", s), self.nb(part, stage, 4 - s), self.name)
            r = self.ref(part, stage, k, s, half)
            r[...] = (r[...].astype(F32) + buf[...].astype(F32)).astype(BF)
            self.L.send(self.ref(part, stage, k, s), self.rb.at[part, self.slot(stage, k), half], (self.name, part, stage, k, "near", s), self.nb(part, stage, s), self.name)
    def total(self, part, stage, k):
        for s in (1, 3):
            half = 0 if s == 1 else 1
            self.L.recv(self.rb.at[part, self.slot(stage, k), half], (self.name, part, stage, k, "near", s), self.nb(part, stage, 4 - s), self.name)
        b = self.rb.at[part, self.slot(stage, k)]
        return self.ref(part, stage, k, 0)[...].astype(F32) + b[0].astype(F32) + b[1].astype(F32)
    def fold(self, part, stage, k):
        t = self.total(part, stage, k)
        self.ref(part, stage, k, 0)[...] = t.astype(BF)
    def partner(self):
        m = self.me
        return {"grp": m["g"], "fsdp": m["f"] + 1 - 2 * m["x"]}
    def xsend(self):
        self.fold(1, 1, 0)
        self.L.send(self.ref(1, 1, 0, 0), self.rx, (self.name, "x"), self.partner(), self.name)
    def result(self):
        t = self.total(0, 1, 0)
        self.L.recv(self.rx, (self.name, "x"), self.partner(), self.name)
        return t + self.rx[...].astype(F32)
    def stages(self):
        def a():
            for k in (2, 1, 3, 0):
                for part in (1, 0):
                    self.far(part, 0, k)
        def b(k):
            def f():
                for part in (1, 0):
                    self.near(part, 0, k)
            return f
        def c(k):
            def f():
                for part in (1, 0):
                    self.fold(part, 0, k)
                    if k == 2:
                        self.far(part, 1, 0)
            return f
        def d():
            for part in (1, 0):
                self.near(part, 1, 0)
        return [a, b(2), b(1), c(2), b(3), c(1), b(0), c(3), d, c(0), self.xsend]
    def sent(self):
        self.L.sent(self.D.at[pl.ds(0, 31)], self.name, (self.name, "x"), self.partner())


def wait_bytes(like, send_sem, recv_sem, devid, recv=True, send=True):
    c = pltpu.make_async_remote_copy(src_ref=like, dst_ref=like, send_sem=send_sem, recv_sem=recv_sem, device_id=devid, device_id_type=MESH)
    if recv:
        c.wait_recv()
    if send:
        c.wait_send()


def dot(a, b, ca, cb):
    return lax.dot_general(a, b, (((ca,), (cb,)), ((), ())), preferred_element_type=F32)


class Refs:
    pass


P_IN = ["lens", "counts", "scap", "tgain", "fgain", "cs_h", "tq_h", "tk_h", "tv_h", "bias_h", "tout_h", "vid_h", "grad_h", "ck_h", "cv_h", "cq_h", "co_h"]
P_OUT = {
    "qb": ((256, 384), BF),
    "da": ((256, 384), BF),
    "ks": ((2, 384, 384), BF),
    "mu": ((256, 1), F32),
    "inv": ((256, 1), F32),
}
P_FAR = {
    "gq": ((32, 192, 384), BF),
    "vnT": ((3072, 256), BF),
    "gradT": ((3072, 256), BF),
}
P_SCRATCH = {
    "kv": ((2, 128, 384), BF),
    "qo": ((192, 384), BF),
    "cs": ((128, 4096), BF),
    "normed": ((128, 4096), BF),
    "wt": ((2, 4096, 512), BF),
    "bias": ((8, 128, 128), F32),
    "tqkv": ((3, 128, 512), BF),
    "tm": ((128, 512), BF),
    "vid": ((256, 3072), BF),
    "grad": ((256, 3072), BF),
    "vn": ((256, 3072), BF),
    "gw": ((32, 128, 384), BF),
    "parts": ((4, 128, 1024), BF),
    "t0": ((128, 1024), BF),
    "t1": ((128, 1024), BF),
    "t2": ((128, 1024), BF),
    "t3": ((128, 1024), BF),
    "E": ((2, 4, 128, 1024), BF),
    "sscol": ((128, 1), F32),
    "SS": ((2, 4, 8, 128), F32),
    "kvp": ((16, 2, 8, 384), BF),
    "C": ((32, 8, 384), BF),
    "sb": ((32, 3, 8, 384), BF),
    "R": ((32, 3, 8, 384), BF),
}
P_TABLES = {"end": 32, "first": 32, "cap": 96, "samp": 32}
Q_IN = ["edge", "sidx", "qb", "da", "ks", "mu", "inv", "gq_h", "vnT_h", "gradT_h", "vid_h", "grad_h"]
Q_OUT = {
    "updated": ((256, 768), BF),
    "igrad": ((256, 768), BF),
    "qgrad": ((96, 384), F32),
    "ograd": ((96, 384), F32),
    "kgrad": ((128, 384), BF),
    "vgrad": ((128, 384), BF),
}
Q_SCRATCH = {
    "gq": ((32, 192, 384), BF),
    "vnT": ((3072, 256), BF),
    "gradT": ((3072, 256), BF),
    "vid": ((256, 3072), BF),
    "grad": ((256, 3072), BF),
    "att": ((256, 384), BF),
    "dq": ((256, 384), BF),
    "w": ((3, 256, 128), F32),
    "mp": ((3, 256, 384), BF),
    "ms": ((3, 256, 384), BF),
    "T": ((32, 3, 8, 384), BF),
    "Dw": ((32, 96, 384), BF),
    "Dq": ((32, 96, 384), BF),
    "ra1": ((2, 5, 2, 48, 384), BF),
    "rb1": ((2, 5, 2, 96, 384), BF),
    "rx1": ((96, 384), BF),
    "ra2": ((2, 5, 2, 48, 384), BF),
    "rb2": ((2, 5, 2, 96, 384), BF),
    "rx2": ((96, 384), BF),
    "op": ((4, 256, 768), BF),
    "o0": ((256, 768), BF),
    "o1": ((256, 768), BF),
    "o2": ((256, 768), BF),
    "o3": ((256, 768), BF),
    "dn": ((4, 256, 768), BF),
    "n0": ((256, 768), BF),
    "n1": ((256, 768), BF),
    "n2": ((256, 768), BF),
    "n3": ((256, 768), BF),
    "scol": ((2, 256, 1), F32),
    "stat": ((4, 2, 8, 256), F32),
    "RG": ((99, 8, 384), BF),
    "CG": ((32, 8, 384), BF),
    "KV": ((32, 8, 384), BF),
}


def fill_tables(r):
    def total(s, acc):
        acc = acc + r.counts[s]
        r.end[s] = acc
        return acc
    lax.fori_loop(0, 32, total, jnp.int32(0))

    @pl.loop(0, 32)
    def _(d):
        count = jnp.int32(0)
        for s in range(32):
            count = count + (r.end[s] <= 256 * d).astype(jnp.int32)
        r.first[d] = count
        for t in range(3):
            r.cap[d * 3 + t] = r.scap[jnp.minimum(count + t, 31)]

    @pl.loop(0, 32)
    def _(c):
        s = jnp.int32(0)
        for t in range(32):
            s = s + jnp.where(r.scap[t] == c, t, 0)
        s = jnp.minimum(s, 31)
        stop = r.end[s]
        d0 = (stop - r.counts[s]) // 256
        for m in range(5):
            d = d0 + m
            valid = (d < 32) & (d * 256 < stop)
            r.sidx[c * 5 + m] = jnp.clip(jnp.where(valid, 3 * d + s - r.first[jnp.minimum(d, 31)], 96), 0, 96)


def named(refs, names):
    r = Refs()
    for n, ref in zip(names, refs):
        setattr(r, n, ref)
    return r


def encode(*refs):
    r = named(refs, P_IN + list(P_OUT) + [n + "_o" for n in P_FAR] + ["edge", "sidx"] + list(P_FAR) + list(P_SCRATCH) + list(P_TABLES) + ["sems", "lsem", "asem"])
    me = place()
    f, g, core, hi = me["f"], me["g"], me["core"], me["hi"]
    fs = [{"grp": g, "fsdp": (f + j) % 32} for j in range(1, 32)]
    count = greet(fs + [{"grp": (g + j) % 4, "fsdp": f // 2 * 2 + x} for j in range(1, 4) for x in range(2)])
    L = Links(r.sems)
    loads = {}

    def load(name, src, dst):
        c = pltpu.make_async_copy(src, dst, r.lsem.at[len(loads)])
        c.start()
        loads[name] = c
    load("ck", r.ck_h, r.kv.at[0])
    load("cv", r.cv_h, r.kv.at[1])
    load("cq", r.cq_h, r.qo.at[pl.ds(0, 96)])
    load("co", r.co_h, r.qo.at[pl.ds(96, 96)])
    load("cs", r.cs_h, r.cs)

    def load_text(a, wh):
        for k in range(2):
            rows = pl.ds(k * 2048, 2048)
            load(("wt", a, k), wh.at[rows], r.wt.at[a % 2, rows])
    load_text(0, r.tq_h)
    load_text(1, r.tk_h)
    load("bias", r.bias_h, r.bias)
    load("vid", r.vid_h, r.vid)
    load("grad", r.grad_h, r.grad)

    others = eight_others(me)
    meet(count)

    A, B = Gather(L, me, "w", r.gw, 128), Gather(L, me, "q", r.gq, 192)
    sa, sb = A.stages(r.kv.at[me["x"]]), B.stages(r.qo)
    for n in ("ck", "cv", "cq", "co"):
        loads[n].wait()
    A.xsend(r.kv.at[1 - me["x"]])
    sa[0]()
    B.xsend(r.qo)
    sb[0]()
    r.gw[f] = r.kv[me["x"]]
    r.gq[f] = r.qo[...]

    loads["cs"].wait()

    @pl.loop(0, 8)
    def _(i):
        rows = pl.ds(i * 16, 16)
        x = r.cs[rows].astype(F32)
        mean_square = jnp.mean(x * x, axis=-1, keepdims=True)
        r.normed[rows] = (x * lax.rsqrt(mean_square + 1e-06) * r.tgain[...]).astype(BF)

    def project(a):
        acc = jnp.zeros((128, 512), F32)
        for k in range(2):
            loads["wt", a, k].wait()
            acc = acc + jnp.dot(r.normed[:, pl.ds(k * 2048, 2048)], r.wt[a % 2, pl.ds(k * 2048, 2048)], preferred_element_type=F32)
        r.tqkv[a] = acc.astype(BF)
    project(0)
    load_text(2, r.tv_h)
    sa[1]()
    project(1)
    for k in range(8):
        load(("wo", k), r.tout_h.at[:, pl.ds(k * 512, 512)], r.wt.at[1, pl.ds(k * 512, 512)])
    sb[1]()
    project(2)
    sa[2]()
    sa[3]()
    loads["bias"].wait()
    lane = lax.broadcasted_iota(jnp.int32, (128, 128), 1)
    valid = lane < r.lens[f]

    def text_pair(p):
        cols = pl.ds(p * 128, 128)
        q, k, v = r.tqkv[0, :, cols], r.tqkv[1, :, cols], r.tqkv[2, :, cols]
        out = []
        for i in range(2):
            qh = jnp.where((lane < 64) == (i == 0), q.astype(F32), 0.0).astype(BF)
            ex = jnp.where(valid, jnp.exp(dot(qh, k, 1, 1) + r.bias[2 * p + i]), 0.0)
            wts = (ex / jnp.sum(ex, axis=-1, keepdims=True)).astype(BF)
            out.append(dot(wts, v, 1, 0))
        r.tm[:, cols] = jnp.where(lane < 64, out[0], out[1]).astype(BF)
    text_pair(0)
    text_pair(1)
    sb[2]()
    sb[3]()
    text_pair(2)
    text_pair(3)
    sa[4]()
    sa[5]()
    for k in range(8):
        loads["wo", k].wait()
    T = TwoStep(L, me, "t", r.parts, r.t0, r.t1, r.t2, r.t3)
    for j, s in enumerate(T.order()):
        for n in range(2):
            cols = pl.ds(n * 512, 512)
            r.parts[s, :, cols] = jnp.dot(r.tm[...], r.wt[1, pl.ds((2 * s + n) * 512, 512)], preferred_element_type=F32).astype(BF)
        if j < 2:
            T.start(j)
    sb[4]()
    sb[5]()
    T.mid()
    sa[6]()
    sb[6]()
    fill_tables(r)
    T.end()

    @pl.loop(0, 8)
    def _(i):
        rows, cols = pl.ds(i * 16, 16), pl.ds(pl.multiple_of(g * 1024, 1024), 1024)
        ts = T.total(rows) + r.cs[rows, cols].astype(F32)
        r.E[me["x"], g, rows] = (ts * r.fgain[:, cols]).astype(BF)
        r.sscol[rows] = jnp.sum(ts * ts, axis=1, keepdims=True)
    X = Eight(L, me, "e", r.E, 128)
    X.start()
    r.SS[me["x"], g] = jnp.broadcast_to(r.sscol[...], (128, 128)).T[:8]
    mine = r.SS.at[me["x"], g]
    for key, d, _ in others:
        L.send(mine, mine, ("ss", (4 - key[0]) % 4, key[1]), d)
    sa[7]()
    sa[8]()

    loads["vid"].wait()

    @pl.loop(0, 16)
    def _(i):
        rows = pl.ds(i * 16, 16)
        v = r.vid[rows].astype(F32)
        mean = jnp.mean(v, axis=-1, keepdims=True)
        center = v - mean
        inverse = lax.rsqrt(jnp.mean(center * center, axis=-1, keepdims=True) + 1e-06)
        r.mu[rows], r.inv[rows] = mean, inverse
        r.vn[rows] = (center * inverse).astype(BF)
    X.mid()
    sb[7]()
    sb[8]()
    loads["grad"].wait()

    @pl.loop(0, 24)
    def _(i):
        lanes = pl.ds(pl.multiple_of(i * 128, 128), 128)
        r.vnT[lanes] = r.vn[:, lanes].T
        r.gradT[lanes] = r.grad[:, lanes].T
    load("vnT_o", r.vnT, r.vnT_o)
    load("gradT_o", r.gradT, r.gradT_o)
    X.mid2()
    for i in range(9, 13):
        sa[i]()
    sb[9]()
    sb[10]()
    X.end()
    for key, d, slot in others:
        L.recv(r.SS.at[slot[0], slot[1]], ("ss", key[0], key[1]), d)

    acc = jnp.zeros((256, 384), F32)
    for k in range(4):
        acc = acc + jnp.dot(r.E[:, k].reshape(256, 1024), r.gw[k * 8 : k * 8 + 8].reshape(1024, 384), preferred_element_type=F32)
    for c in range(2):
        ss = r.SS[c, 0, :1] + r.SS[c, 1, :1] + r.SS[c, 2, :1] + r.SS[c, 3, :1]
        col = jnp.broadcast_to(ss, (128, 128)).T[:, :1]
        r.kvp[:, c] = (acc[c * 128 : c * 128 + 128] * lax.rsqrt(col / 4096 + 1e-06)).reshape(16, 8, 384).astype(BF)

    partner = {"grp": g, "fsdp": (f + 1) % 32}
    yz = f // 2

    @pl.loop(1, 16)
    def _(j):
        to = (yz + j) % 16
        pltpu.make_async_remote_copy(src_ref=r.kvp.at[to], dst_ref=r.C.at[pl.ds(2 * yz, 2)], send_sem=r.asem.at[0], recv_sem=r.asem.at[1], device_id={"grp": g, "fsdp": to * 2 + me["x"]}, device_id_type=MESH).start()
    r.C[pl.ds(2 * yz, 2)] = r.kvp[yz]
    wait_bytes(r.C.at[pl.ds(0, 30)], r.asem.at[0], r.asem.at[1], partner)

    @pl.loop(1, 32)
    def _(j):
        to = (f + j) % 32
        for s in range(3):
            r.sb[to, s] = r.C[r.cap[to * 3 + s]]
        pltpu.make_async_remote_copy(src_ref=r.sb.at[to], dst_ref=r.R.at[f], send_sem=r.asem.at[2], recv_sem=r.asem.at[3], device_id={"grp": g, "fsdp": to}, device_id_type=MESH).start()
    for s in range(3):
        r.R[f, s] = r.C[r.cap[f * 3 + s]]
    for s in sb[11:]:
        s()
    load("gq_o", r.gq, r.gq_o)

    acc = jnp.zeros((256, 384), F32)
    acc2 = jnp.zeros((256, 384), F32)
    for k in range(4):
        cols = pl.ds(k * 768, 768)
        acc = acc + jnp.dot(r.vn[:, cols], r.gq[k * 8 : k * 8 + 8, 0:96].reshape(768, 384), preferred_element_type=F32)
    r.qb[...] = acc.astype(BF)
    for k in range(4):
        cols = pl.ds(k * 768, 768)
        acc2 = acc2 + jnp.dot(r.grad[:, cols], r.gq[k * 8 : k * 8 + 8, 96:192].reshape(768, 384), preferred_element_type=F32)
    r.da[...] = acc2.astype(BF)

    first = r.first[f]
    r.edge[0], r.edge[1] = r.end[jnp.minimum(first, 31)], r.end[jnp.minimum(first + 1, 31)]
    for s in range(3):
        r.edge[2 + s] = r.lens[r.cap[f * 3 + s]]
    wait_bytes(r.R.at[pl.ds(0, 31)], r.asem.at[2], r.asem.at[3], partner)
    for kv in range(2):
        for s in range(3):
            r.ks[kv, pl.ds(s * 128, 128)] = r.R[:, s].reshape(16, 2, 8, 384)[:, kv].astype(F32).reshape(128, 384).astype(BF)
    A.sent()
    B.sent()
    L.drain()
    for n in P_FAR:
        loads[n + "_o"].wait()


def attend(*refs):
    r = named(refs, Q_IN + list(Q_OUT) + list(Q_SCRATCH) + ["sems", "lsem", "asem"])
    me = place()
    f, g, core, hi = me["f"], me["g"], me["core"], me["hi"]
    count = greet([{"grp": g, "fsdp": (f + j) % 32} for j in range(1, 32)] + [{"grp": (g + j) % 4, "fsdp": f} for j in range(1, 4)])
    L = Links(r.sems)
    partner = {"grp": g, "fsdp": (f + 1) % 32}
    loads = {}
    for i, n in enumerate(("gradT", "gq", "vnT", "vid", "grad")):
        loads[n] = pltpu.make_async_copy(getattr(r, n + "_h"), getattr(r, n), r.lsem.at[i])
        loads[n].start()
    position = lax.broadcasted_iota(jnp.int32, (256, 128), 0) + f * 256
    slot = (position >= r.edge[0]).astype(jnp.int32) + (position >= r.edge[1]).astype(jnp.int32)
    token_len = jnp.where(slot == 0, r.edge[2], jnp.where(slot == 1, r.edge[3], r.edge[4]))
    token_valid = lax.broadcasted_iota(jnp.int32, (256, 128), 1) < token_len
    scale = 1.0 / math.sqrt(HEAD_SIZE)

    def pick(a):
        return jnp.where(slot == 0, a[:, 0:128], jnp.where(slot == 1, a[:, 128:256], a[:, 256:384]))

    def placed(a):
        return jnp.concatenate([jnp.where(slot == s, a, 0.0).astype(BF) for s in range(3)], axis=1)

    for h in range(3):
        cols = pl.ds(h * 128, 128)
        scores = pick(dot(r.qb[:, cols], r.ks[0, :, cols], 1, 1)) * scale
        ex = jnp.where(token_valid, jnp.exp(scores), 0.0)
        w = ex / jnp.sum(ex, axis=-1, keepdims=True)
        r.w[h] = w
        mp = placed(w)
        r.mp[h] = mp
        r.att[:, cols] = dot(mp, r.ks[1, :, cols], 1, 0).astype(BF)

    def weight_grad(D, left, right):
        @pl.loop(0, 8)
        def _(i):
            rows = pl.ds(i * 384, 384)
            D[pl.ds(i * 4, 4)] = dot(left[rows], right[...], 1, 0).reshape(4, 96, 384).astype(BF)
    loads["gradT"].wait()
    weight_grad(r.Dw, r.gradT, r.att)
    S1 = Scatter(L, me, "d1", r.Dw, r.ra1, r.rb1, r.rx1)
    S2 = Scatter(L, me, "d2", r.Dq, r.ra2, r.rb2, r.rx2)
    s1, s2 = S1.stages(), S2.stages()
    meet(count)
    s1[0]()
    loads["gq"].wait()
    O = TwoStep(L, me, "o", r.op, r.o0, r.o1, r.o2, r.o3)
    N = TwoStep(L, me, "n", r.dn, r.n0, r.n1, r.n2, r.n3)
    s1[1]()

    for h in range(3):
        cols = pl.ds(h * 128, 128)
        d_probs = pick(dot(r.da[:, cols], r.ks[1, :, cols], 1, 1))
        w = r.w[h]
        ds = w * (d_probs - jnp.sum(w * d_probs, axis=-1, keepdims=True)) * scale
        ms = placed(ds)
        r.ms[h] = ms
        r.dq[:, cols] = dot(ms, r.ks[0, :, cols], 1, 0).astype(BF)
    loads["vnT"].wait()
    weight_grad(r.Dq, r.vnT, r.dq)
    s2[0]()
    for j, s in enumerate(O.order()):
        r.op[s] = dot(r.att[...], r.gq[pl.ds(s * 8, 8), 96:192].reshape(768, 384), 1, 1).astype(BF)
        if j < 2:
            O.start(j)
    s1[2]()
    s1[3]()
    for j, s in enumerate(N.order()):
        r.dn[s] = dot(r.dq[...], r.gq[pl.ds(s * 8, 8), 0:96].reshape(768, 384), 1, 1).astype(BF)
        if j < 2:
            N.start(j)
    for h in range(3):
        cols = pl.ds(h * 128, 128)
        kt = dot(r.ms[h], r.qb[:, cols], 0, 0)
        vt = dot(r.mp[h], r.da[:, cols], 0, 0)
        for s in range(3):
            rows = slice(s * 128, s * 128 + 128)
            both = jnp.stack([kt[rows].reshape(16, 8, 128), vt[rows].reshape(16, 8, 128)], axis=1)
            r.T[:, s, :, cols] = both.reshape(32, 8, 128).astype(BF)

    @pl.loop(1, 32)
    def _(j):
        to = (f + j) % 32
        pltpu.make_async_remote_copy(src_ref=r.T.at[to], dst_ref=r.RG.at[pl.ds(3 * f, 3)], send_sem=r.asem.at[4], recv_sem=r.asem.at[5], device_id={"grp": g, "fsdp": to}, device_id_type=MESH).start()
    O.mid()
    N.mid()
    for i in range(4, 8):
        s1[i]()
    s2[1]()
    s2[2]()
    s1[8]()
    for i in (3, 4):
        s2[i]()
    for i in (9, 10):
        s1[i]()
    for i in (5, 6, 7):
        s2[i]()
    r.RG[pl.ds(96, 3)] = jnp.zeros((3, 8, 384), BF)
    r.RG[pl.ds(3 * f, 3)] = r.T[f]
    wait_bytes(r.RG.at[pl.ds(0, 93)], r.asem.at[4], r.asem.at[5], partner)

    @pl.loop(0, 32)
    def _(c):
        acc = r.RG[r.sidx[c * 5]].astype(F32)
        for m in range(1, 5):
            acc = acc + r.RG[r.sidx[c * 5 + m]].astype(F32)
        r.CG[c] = acc.astype(BF)

    @pl.loop(1, 32)
    def _(j):
        to = (f + j) % 32
        pltpu.make_async_remote_copy(src_ref=r.CG.at[to], dst_ref=r.KV.at[f], send_sem=r.asem.at[6], recv_sem=r.asem.at[7], device_id={"grp": g, "fsdp": to}, device_id_type=MESH).start()
    r.KV[f] = r.CG[f]
    s2[8]()
    O.end()
    loads["vid"].wait()
    loads["grad"].wait()
    cols = pl.ds(pl.multiple_of(g * 768, 768), 768)

    @pl.loop(0, 16)
    def _(i):
        rows = pl.ds(i * 16, 16)
        r.updated[rows] = (r.vid[rows, cols].astype(F32) + O.total(rows)).astype(BF)
    N.end()

    def video_hat(rows):
        return (r.vid[rows, cols].astype(F32) - r.mu[rows]) * r.inv[rows]

    @pl.loop(0, 16)
    def _(i):
        rows = pl.ds(i * 16, 16)
        t = N.total(rows)
        r.scol[0, rows] = jnp.sum(t, axis=1, keepdims=True)
        r.scol[1, rows] = jnp.sum(t * video_hat(rows), axis=1, keepdims=True)
    for k in range(2):
        r.stat[g, k] = jnp.broadcast_to(r.scol[k], (256, 128)).T[:8]
    grp = [{"grp": (g + j) % 4, "fsdp": f} for j in range(1, 4)]
    for j in range(1, 4):
        L.send(r.stat.at[g], r.stat.at[g], ("st", j), grp[j - 1])
    for i in (9, 10):
        s2[i]()
    r.ograd[...] = S1.result()
    for j in range(1, 4):
        L.recv(r.stat.at[(g + 4 - j) % 4], ("st", j), grp[3 - j])
    for k in range(2):
        s = r.stat[0, k, :1] + r.stat[1, k, :1] + r.stat[2, k, :1] + r.stat[3, k, :1]
        r.scol[k] = jnp.broadcast_to(s / 3072, (128, 256)).T[:, :1]

    @pl.loop(0, 16)
    def _(i):
        rows = pl.ds(i * 16, 16)
        d = N.total(rows) - r.scol[0, rows] - video_hat(rows) * r.scol[1, rows]
        r.igrad[rows] = (r.grad[rows, cols].astype(F32) + r.inv[rows] * d).astype(BF)
    wait_bytes(r.KV.at[pl.ds(0, 31)], r.asem.at[6], r.asem.at[7], partner)
    r.kgrad[...] = r.KV[...].reshape(16, 2, 8, 384)[:, 0].astype(F32).reshape(128, 384).astype(BF)
    r.vgrad[...] = r.KV[...].reshape(16, 2, 8, 384)[:, 1].astype(F32).reshape(128, 384).astype(BF)
    r.qgrad[...] = S2.result()
    S1.sent()
    S2.sent()
    L.drain()


def hand_over(*refs):
    held, sem = refs[12:18], refs[18]
    into = [pltpu.make_async_copy(refs[i], held[i], sem.at[i]) for i in range(6)]
    out = [pltpu.make_async_copy(held[i], refs[6 + i], sem.at[6 + i]) for i in range(6)]
    for c in into:
        c.start()
    for i in range(6):
        into[i].wait()
        out[i].start()
    for c in out:
        c.wait()


def local(caption_states, caption_lens, text_gain, text_query, text_key, text_value, text_bias, text_out, final_gain, cross_key, cross_value, video_states, video_counts, sample_caption, cross_query, cross_out, out_grad):
    V, M, A = pltpu.VMEM, pltpu.SMEM, pl.ANY

    def call(kernel, name, cid, args, spaces, outs, far, tables, scratch, smem):
        return pl.pallas_call(
            kernel,
            out_shape=tuple(jax.ShapeDtypeStruct(s, d) for s, d in (outs | far).values()) + tuple(jax.ShapeDtypeStruct((n,), jnp.int32) for n in tables),
            in_specs=[pl.BlockSpec(memory_space=s) for s in spaces],
            out_specs=tuple(pl.BlockSpec(memory_space=V) for _ in outs) + tuple(pl.BlockSpec(memory_space=A) for _ in far) + tuple(pl.BlockSpec(memory_space=M) for _ in tables),
            scratch_shapes=[V(s, d) for s, d in (far | scratch).values()] + [M((n,), jnp.int32) for n in smem] + [DMA((128,)), DMA((32,)), DMA((8,))],
            compiler_params=pltpu.CompilerParams(collective_id=cid, has_side_effects=True, vmem_limit_bytes=58 << 20),
            name=name,
        )(*args)
    args = [caption_lens, video_counts, sample_caption, text_gain[None], final_gain[None], caption_states.reshape(128, 4096), text_query, text_key, text_value, text_bias, text_out, video_states, out_grad, cross_key, cross_value, cross_query, cross_out.T]
    qb, da, ks, mu, inv, gq, vnT, gradT, edge, sidx = call(encode, "encode", 0, args, [M] * 3 + [V] * 2 + [A] * 12, P_OUT, P_FAR, (8, 160), P_SCRATCH, P_TABLES.values())
    args = [edge, sidx, qb, da, ks, mu, inv, gq, vnT, gradT, video_states, out_grad]
    outs = call(attend, "attend", 1, args, [M] * 2 + [V] * 5 + [A] * 5, Q_OUT, {}, (), Q_SCRATCH, ())
    updated, igrad, qgrad, ograd, kgrad, vgrad = pl.pallas_call(
        hand_over,
        out_shape=tuple(jax.ShapeDtypeStruct(s, d) for s, d in Q_OUT.values()),
        in_specs=[pl.BlockSpec(memory_space=A)] * 6,
        out_specs=(pl.BlockSpec(memory_space=A),) * 6,
        scratch_shapes=[V(s, d) for s, d in Q_OUT.values()] + [DMA((12,))],
        name="hand_over",
    )(*outs)
    return updated, igrad, qgrad, ograd.T, kgrad[None], vgrad[None]


def solution(mesh):
    in_specs = (P("fsdp"), P(), P(), P(None, "grp"), P(None, "grp"), P(None, "grp"), P("grp"), P("grp"), P(), P("fsdp", "grp"), P("fsdp", "grp"), P("fsdp"), P(), P(), P("fsdp", "grp"), P("grp", "fsdp"), P("fsdp"))
    out_specs = (P("fsdp", "grp"), P("fsdp", "grp"), P("fsdp", "grp"), P("grp", "fsdp"), P("fsdp", None, "grp"), P("fsdp", None, "grp"))
    return jax.shard_map(local, mesh=mesh, in_specs=in_specs, out_specs=out_specs, check_vma=False)
```
